32 devices in a mesh: dp: 8 (over z, y), head: 4 (over x, core).
Axes of the slice: x: 2, y: 2, z: 4, core: 2. Of those that a mesh axis runs over, the one named last changes fastest.
Arguments:
- hidden_input: bfloat16 [40, 512, 768], P('dp'), may hold values from -6 to 6
- grad_out: bfloat16 [40, 512, 768], P('dp', 'head'), may hold values from -6 to 6
- pair_lengths: int32 [40], P('dp'), may hold values from 64 to 512, as said below
- query_key_value_weight: bfloat16 [3, 768, 768], P(None, None, 'head'), may hold values from -0.21875 to 0.21875
- qkv_bias: float32 [3, 768], replicated, may hold values from -4 to 4
- output_projection_weight: bfloat16 [768, 768], P('head'), may hold values from -0.875 to 0.875
- shifts: float32 [4, 768], replicated, may hold values from -4 to 4
- gains: float32 [2, 768], replicated, may hold values from 0.5 to 1.5
- up_projection_weight: bfloat16 [768, 3072], P(None, 'head'), may hold values from -0.21875 to 0.21875
- up_bias: float32 [3072], replicated, may hold values from -4 to 4
- down_projection_weight: bfloat16 [3072, 768], P('head'), may hold values from -0.109375 to 0.109375
- adapters_model: float32 [10, 768, 16], P(None, ('dp', 'head'))
- adapters_inner: float32 [2, 3072, 16], P(None, ('dp', 'head'))
- stats_model: float32 [10, 768, 768], P(None, ('dp', 'head')), as said below
- stats_inner: float32 [2, 3072, 3072], P(None, ('dp', 'head')), as said below
- stats_rank: float32 [12, 16, 16], replicated, as said below
- roots_model: float32 [10, 768, 768], P(None, ('dp', 'head'))
- roots_inner: float32 [2, 3072, 3072], P(None, ('dp', 'head'))
- roots_rank: float32 [12, 16, 16], replicated
Outputs:
- hidden_out: bfloat16 [40, 512, 768], P('dp', 'head')
- grad_in: bfloat16 [40, 512, 768], P('dp', 'head')
- grads_model: float32 [10, 768, 16], P(None, ('dp', 'head'))
- grads_inner: float32 [2, 3072, 16], P(None, ('dp', 'head'))
- adapters_model_new: float32 [10, 768, 16], P(None, ('dp', 'head'))
- adapters_inner_new: float32 [2, 3072, 16], P(None, ('dp', 'head'))
- stats_model_new: float32 [10, 768, 768], P(None, ('dp', 'head'))
- stats_inner_new: float32 [2, 3072, 3072], P(None, ('dp', 'head'))
- stats_rank_new: float32 [12, 16, 16], replicated
The draws below stay inside these ranges and needn't reach their ends.
Inputs may be any that keep to these rules, and one draw needn't show every extreme that they name: `pair_lengths`: a pair's tokens come first in its slot and padding follows; some pair fills its whole slot. `stats_model`: each matrix is symmetric. `stats_inner`: each matrix is symmetric. `stats_rank`: each matrix is symmetric.
All inputs are finite; a program needn't handle non-finite values.
Results may differ from the reference program's by a relative error of at most 0.024.
Values may be sent and summed in bfloat16 or wider, within the bound.
A program may use at most 128 MiB of HBM per device.

```python
import math
import jax
import jax.numpy as jnp
from jax import lax

D = 768
H = 12
DH = 64
FF = 3072
R = 16
LEN = 512
SEQ_DEV = 5
SEQS = 40
TOKENS = 20480
N_DP = 8


def draw_noise(key, shape_of):
    return jax.random.normal(key, shape_of, jnp.float32)


def draw_pair_lengths(key, part):
    key = jax.random.fold_in(key, 1)
    drawn_lengths = jax.random.randint(key, (SEQS,), LEN // 8, LEN + 1)
    return drawn_lengths.at[0].set(LEN).astype(jnp.int32)


def draw_adapters_model(key, part):
    key = jax.random.fold_in(key, 2)
    scales = jnp.where(jnp.arange(10) < 5, D ** (-0.5), 0.0625).astype(jnp.float32)
    return draw_noise(key, (10, D, R)) * scales[:, None, None]


def draw_adapters_inner(key, part):
    key = jax.random.fold_in(key, 3)
    scales = jnp.where(jnp.arange(2) < 1, FF ** (-0.5), 0.0625).astype(jnp.float32)
    return draw_noise(key, (2, FF, R)) * scales[:, None, None]


def draw_symmetric(key, matrices, order, level, inner_count):
    key_first, key_second = jax.random.split(key)
    diagonal = level * jax.random.uniform(key_first, (matrices, order), jnp.float32, 1.0, 4.0)
    noise_draw = draw_noise(key_second, (matrices, order, order))
    root_diagonal = jnp.sqrt(diagonal)
    off_part = (noise_draw + jnp.swapaxes(noise_draw, 1, 2)) * (0.7071067811865476 / math.sqrt(inner_count))
    off_part = off_part * root_diagonal[:, :, None] * root_diagonal[:, None, :]
    off_part = off_part * (1.0 - jnp.eye(order, dtype=jnp.float32))
    return off_part + diagonal[:, :, None] * jnp.eye(order, dtype=jnp.float32)


def draw_stats_model(key, part):
    key = jax.random.fold_in(key, 4)
    return draw_symmetric(key, 10, D, float(TOKENS * R), R)


def draw_stats_inner(key, part):
    key = jax.random.fold_in(key, 5)
    return draw_symmetric(key, 2, FF, float(TOKENS * R), R)


def draw_stats_rank(key, part):
    key = jax.random.fold_in(key, 6)
    key_model, key_inner = jax.random.split(key)
    model_part = draw_symmetric(key_model, 10, R, float(TOKENS * D), D)
    inner_part = draw_symmetric(key_inner, 2, R, float(TOKENS * FF), FF)
    return jnp.concatenate([model_part, inner_part], axis=0)


def draw_root_rows(key, matrices, order):
    key_first, key_second = jax.random.split(key)
    row_ramp = jnp.arange(order, dtype=jnp.float32) / max(order - 1, 1)
    row_scale = (10.0 ** row_ramp)[None, :] * jax.random.uniform(key_first, (matrices, order), jnp.float32, 0.7, 1.4)
    base_matrix = jnp.eye(order, dtype=jnp.float32) + draw_noise(key_second, (matrices, order, order)) * (0.35 / math.sqrt(order))
    return base_matrix * row_scale[:, :, None]


def draw_roots_model(key, part):
    key = jax.random.fold_in(key, 7)
    return draw_root_rows(key, 10, D)


def draw_roots_inner(key, part):
    key = jax.random.fold_in(key, 8)
    return draw_root_rows(key, 2, FF)


def draw_roots_rank(key, part):
    key = jax.random.fold_in(key, 9)
    key_first, key_second = jax.random.split(key)
    column_scale = jnp.exp(jax.random.uniform(key_first, (12, R), jnp.float32, 0.0, math.log(10.0)))
    base_matrix = jnp.eye(R, dtype=jnp.float32) + draw_noise(key_second, (12, R, R)) * (0.35 / math.sqrt(R))
    return base_matrix * column_scale[:, None, :]


def steps_of(rng, extent, shards, least, high):
    loudness = 1.0
    for position, blocks in shards:
        heights = jax.random.uniform(jax.random.fold_in(jax.random.fold_in(rng, 6), position), (blocks,), jnp.float32, least / len(shards), high / len(shards))
        loudness = loudness * jnp.repeat(jnp.exp(heights), extent[position] // blocks).reshape((-1,) + (1,) * (len(extent) - 1 - position))
    return loudness


def gaussian(key, dims, width, limit, shards=(), kind=jnp.bfloat16):
    drawn = width * jax.random.normal(key, dims, jnp.float32)
    if shards:
        drawn = drawn * steps_of(key, dims, shards, -0.22, 0.18)
    return jnp.clip(drawn, -limit, limit).astype(kind)


def setup_inputs(seed: int = 0) -> dict:
    splits = jax.random.split(jax.random.key(seed), 20)
    hidden_input = gaussian(splits[0], (SEQS, LEN, D), 1.0, 6.0, ((0, 8),))
    grad_out = gaussian(splits[1], (SEQS, LEN, D), 1.0, 6.0, ((0, 8), (1, 4)))
    pair_lengths = draw_pair_lengths(jax.random.fold_in(splits[19], 71), 0)
    query_key_value_weight = gaussian(splits[3], (3, D, D), D ** -0.5, 0.21875, ((2, 4),))
    qkv_bias = gaussian(splits[4], (3, D), 0.3, 4.0, (), jnp.float32)
    output_projection_weight = gaussian(splits[5], (D, D), (D // 16) ** -0.5, 0.875, ((0, 4),))
    shifts = gaussian(splits[6], (4, D), 0.3, 4.0, (), jnp.float32)
    gains = jnp.clip(1.0 + 0.1 * jax.random.normal(splits[7], (2, D), jnp.float32), 0.5, 1.5)
    up_projection_weight = gaussian(splits[8], (D, FF), D ** -0.5, 0.21875, ((1, 4),))
    up_bias = gaussian(splits[9], (FF,), 0.3, 4.0, (), jnp.float32)
    down_projection_weight = gaussian(splits[10], (FF, D), FF ** -0.5, 0.109375, ((0, 4),))
    adapters_model = draw_adapters_model(jax.random.fold_in(splits[19], 71), 0)
    adapters_inner = draw_adapters_inner(jax.random.fold_in(splits[19], 71), 0)
    stats_model = draw_stats_model(jax.random.fold_in(splits[19], 71), 0)
    stats_inner = draw_stats_inner(jax.random.fold_in(splits[19], 71), 0)
    stats_rank = draw_stats_rank(jax.random.fold_in(splits[19], 71), 0)
    roots_model = draw_roots_model(jax.random.fold_in(splits[19], 71), 0)
    roots_inner = draw_roots_inner(jax.random.fold_in(splits[19], 71), 0)
    roots_rank = draw_roots_rank(jax.random.fold_in(splits[19], 71), 0)
    return dict(hidden_input=hidden_input, grad_out=grad_out, pair_lengths=pair_lengths, query_key_value_weight=query_key_value_weight, qkv_bias=qkv_bias, output_projection_weight=output_projection_weight, shifts=shifts, gains=gains, up_projection_weight=up_projection_weight, up_bias=up_bias, down_projection_weight=down_projection_weight, adapters_model=adapters_model, adapters_inner=adapters_inner, stats_model=stats_model, stats_inner=stats_inner, stats_rank=stats_rank, roots_model=roots_model, roots_inner=roots_inner, roots_rank=roots_rank)


@jax.custom_vjp
def reduced_float(v):
    return lax.optimization_barrier(v.astype(jnp.bfloat16)).astype(jnp.float32)

@jax.custom_vjp
def reduced_float_backward(v):
    return v

def low_keep(v):
    return (reduced_float(v), None)

def low_pass(kept, grad):
    return (grad,)

def back_keep(v):
    return (v, None)

def back_low(kept, grad):
    return (reduced_float(grad),)
reduced_float.defvjp(low_keep, low_pass)
reduced_float_backward.defvjp(back_keep, back_low)
highest_precision = lax.Precision.HIGHEST
lowrank_scale = 2.0
rate_first = 0.01
rate_second = 0.16
stat_decay = 0.5

def layer_norm(values, gain, offset):
    centre = values - lax.optimization_barrier(jnp.mean(values, axis=-1, keepdims=True))
    spread = lax.optimization_barrier(jnp.mean(centre * centre, axis=-1, keepdims=True))
    return centre * lax.rsqrt(spread + 1e-05) * gain + offset

def gelu_exact(values):
    return 0.5 * values * (1.0 + jax.scipy.special.erf(values * 0.7071067811865476))

def attend_one(packed):
    projected_rows, key_valid = packed
    queries = projected_rows[:, 0]
    key_rows = projected_rows[:, 1]
    value_rows = projected_rows[:, 2]
    scores = reduced_float_backward(jnp.einsum('qhd,khd->hqk', queries, key_rows, precision=highest_precision) * DH ** (-0.5))
    scores = jnp.where(key_valid[None, None, :], scores, -1e+30)
    weights = jax.nn.softmax(scores, axis=-1)
    return jnp.einsum('hqk,khd->qhd', reduced_float(weights), value_rows, precision=highest_precision)

def forward(token_rows, model_reduced_float, inner_reduced_float, pair_valid, frozen):
    query_key_value_weight, qkv_bias, output_projection_weight, shifts, gains, up_projection_weight, up_bias, down_projection_weight = frozen
    seq_count = token_rows.shape[0]
    flattened_rows = token_rows.reshape(-1, D)
    lowrank_input = reduced_float(reduced_float_backward(jnp.einsum('bu,vua->bva', flattened_rows, model_reduced_float[0:3], precision=highest_precision)))
    projected_rows = jnp.einsum('td,jdc->tjc', flattened_rows, query_key_value_weight, precision=highest_precision) + qkv_bias[None]
    projected_rows = projected_rows + lowrank_scale * jnp.einsum('wzd,znd->wzn', lowrank_input, model_reduced_float[5:8], precision=highest_precision)
    projected_rows = reduced_float(reduced_float_backward(projected_rows)).reshape(seq_count, LEN, 3, H, DH)
    attention_result = lax.map(jax.checkpoint(attend_one), (projected_rows, pair_valid))
    attention_result = reduced_float(reduced_float_backward(attention_result.reshape(-1, D)))
    attention_inner_rank = reduced_float(reduced_float_backward(jnp.dot(attention_result, model_reduced_float[3], precision=highest_precision)))
    attention_full_width = jnp.dot(attention_result, output_projection_weight, precision=highest_precision) + shifts[0]
    attention_full_width = reduced_float_backward(attention_full_width + lowrank_scale * jnp.dot(attention_inner_rank, model_reduced_float[8].T, precision=highest_precision))
    mid_norm = layer_norm(flattened_rows + attention_full_width, gains[0], shifts[1])
    middle_reduced_float = reduced_float(mid_norm)
    up_inner_rank = reduced_float(reduced_float_backward(jnp.dot(middle_reduced_float, model_reduced_float[4], precision=highest_precision)))
    up_preactivation = jnp.dot(middle_reduced_float, up_projection_weight, precision=highest_precision) + up_bias
    up_preactivation = reduced_float_backward(up_preactivation + lowrank_scale * jnp.dot(up_inner_rank, inner_reduced_float[1].T, precision=highest_precision))
    up_activated = reduced_float(gelu_exact(up_preactivation))
    down_inner_rank = reduced_float(reduced_float_backward(jnp.dot(up_activated, inner_reduced_float[0], precision=highest_precision)))
    feedforward_full_width = jnp.dot(up_activated, down_projection_weight, precision=highest_precision) + shifts[2]
    feedforward_full_width = reduced_float_backward(feedforward_full_width + lowrank_scale * jnp.dot(down_inner_rank, model_reduced_float[9].T, precision=highest_precision))
    result = layer_norm(mid_norm + feedforward_full_width, gains[1], shifts[3])
    return result.reshape(seq_count, LEN, D)

def reference(hidden_input, grad_out, pair_lengths, query_key_value_weight, qkv_bias, output_projection_weight, shifts, gains, up_projection_weight, up_bias, down_projection_weight, adapters_model, adapters_inner, stats_model, stats_inner, stats_rank, roots_model, roots_inner, roots_rank):
    frozen = (query_key_value_weight.astype(jnp.float32), qkv_bias, output_projection_weight.astype(jnp.float32), shifts, gains, up_projection_weight.astype(jnp.float32), up_bias, down_projection_weight.astype(jnp.float32))
    model_reduced_float = adapters_model.astype(jnp.bfloat16).astype(jnp.float32)
    inner_reduced_float = adapters_inner.astype(jnp.bfloat16).astype(jnp.float32)
    pair_valid = jnp.arange(LEN, dtype=jnp.int32)[None, :] < pair_lengths[:, None]
    groups_in = hidden_input.reshape(N_DP, SEQ_DEV, LEN, D)
    groups_grad = grad_out.reshape(N_DP, SEQ_DEV, LEN, D)
    groups_valid = pair_valid.reshape(N_DP, SEQ_DEV, LEN)

    def one_group(carry, packed):
        token_rows, grad_rows, valid_rows = packed

        def local_forward(tokens_float, model_float, inner_float):
            return forward(tokens_float, model_float, inner_float, valid_rows, frozen)
        result, pull_back = jax.vjp(local_forward, token_rows.astype(jnp.float32), model_reduced_float, inner_reduced_float)
        grad_tokens, grad_model, grad_inner = pull_back(grad_rows.astype(jnp.float32))
        return ((carry[0] + grad_model, carry[1] + grad_inner), (result.astype(jnp.bfloat16), grad_tokens.astype(jnp.bfloat16)))
    start = (jnp.zeros_like(adapters_model), jnp.zeros_like(adapters_inner))
    totals, produced = lax.scan(one_group, start, (groups_in, groups_grad, groups_valid))
    grads_model, grads_inner = totals
    hidden_out = produced[0].reshape(SEQS, LEN, D)
    grad_in = produced[1].reshape(SEQS, LEN, D)
    stats_model_new = stat_decay * stats_model + (1.0 - stat_decay) * jnp.einsum('jar,jbr->jab', grads_model, grads_model, precision=highest_precision)
    stats_inner_new = stat_decay * stats_inner + (1.0 - stat_decay) * jnp.einsum('jar,jbr->jab', grads_inner, grads_inner, precision=highest_precision)
    gram_rank = jnp.concatenate([jnp.einsum('jar,jas->jrs', grads_model, grads_model, precision=highest_precision), jnp.einsum('jar,jas->jrs', grads_inner, grads_inner, precision=highest_precision)], axis=0)
    stats_rank_new = stat_decay * stats_rank + (1.0 - stat_decay) * gram_rank
    step_model = jnp.einsum('jab,jbr->jar', roots_model, grads_model, precision=highest_precision)
    step_model = jnp.einsum('jar,jrs->jas', step_model, roots_rank[0:10], precision=highest_precision)
    step_inner = jnp.einsum('jab,jbr->jar', roots_inner, grads_inner, precision=highest_precision)
    step_inner = jnp.einsum('jar,jrs->jas', step_inner, roots_rank[10:12], precision=highest_precision)
    rates_model = jnp.where(jnp.arange(10) < 5, rate_first, rate_second)
    rates_inner = jnp.where(jnp.arange(2) < 1, rate_first, rate_second)
    scale_model = rates_model * lax.rsqrt(lax.optimization_barrier(jnp.mean(step_model * step_model, axis=(1, 2))) + 1e-06)
    scale_inner = rates_inner * lax.rsqrt(lax.optimization_barrier(jnp.mean(step_inner * step_inner, axis=(1, 2))) + 1e-06)
    adapters_model_new = adapters_model - scale_model[:, None, None] * step_model
    adapters_inner_new = adapters_inner - scale_inner[:, None, None] * step_inner
    return (hidden_out, grad_in, grads_model, grads_inner, adapters_model_new, adapters_inner_new, stats_model_new, stats_inner_new, stats_rank_new)
```

```python
import functools

import jax
import jax.numpy as jnp
from jax import lax
from jax.experimental import pallas as pl
from jax.experimental.pallas import tpu as pltpu
from jax.sharding import PartitionSpec as P

DH = 64
RANK = 16
LANES = 128
LOWRANK = 2.0
RATE_FIRST = 0.01
RATE_SECOND = 0.16
DECAY = 0.5
EPS_NORM = 1e-5
MESH = pl.DeviceIdType.MESH
F32 = jnp.float32
BF16 = jnp.bfloat16
HIGH = lax.Precision.HIGHEST

EARLY_SLOTS = (0, 1, 2, 5, 6, 7)
LATE_SLOTS = (3, 4, 8, 9)


def slot_of(j):
    if j in EARLY_SLOTS:
        return 0, EARLY_SLOTS.index(j)
    return 1, LATE_SLOTS.index(j)


def nn(a, b, precision=None):
    return lax.dot_general(
        a, b, (((1,), (0,)), ((), ())), precision=precision, preferred_element_type=F32
    )


def nt(a, b, precision=None):
    return lax.dot_general(
        a, b, (((1,), (1,)), ((), ())), precision=precision, preferred_element_type=F32
    )


def tn(a, b, precision=None):
    return lax.dot_general(
        a, b, (((0,), (0,)), ((), ())), precision=precision, preferred_element_type=F32
    )


def vmem():
    return pl.BlockSpec(memory_space=pltpu.VMEM)


def anywhere():
    return pl.BlockSpec(memory_space=pl.ANY)


def greet(nd, nh):
    d, h = lax.axis_index("dp"), lax.axis_index("head")
    barrier = pltpu.get_barrier_semaphore()
    for k in range(1, nd):
        pl.semaphore_signal(
            barrier, inc=1, device_id=(lax.rem(d + k, nd), h), device_id_type=MESH
        )
    for k in range(1, nh):
        pl.semaphore_signal(
            barrier, inc=1, device_id=(d, lax.rem(h + k, nh)), device_id_type=MESH
        )
    pl.semaphore_wait(barrier, nd + nh - 2)


def spread(nd, nh, out_ref, own_copy, sems):
    send_d, recv_d, send_h, recv_h = sems
    d, h = lax.axis_index("dp"), lax.axis_index("head")
    own_copy()
    mine = out_ref.at[:, d, h]
    copies = []
    for k in range(1, nd):
        c = pltpu.make_async_remote_copy(
            mine, mine, send_d.at[k], recv_d.at[k],
            device_id=(lax.rem(d + k, nd), h), device_id_type=MESH,
        )
        c.start()
        copies.append(c)
    for c in copies:
        c.wait()
    column = out_ref.at[:, :, h]
    copies = []
    for k in range(1, nh):
        c = pltpu.make_async_remote_copy(
            column, column, send_h.at[k], recv_h.at[k],
            device_id=(d, lax.rem(h + k, nh)), device_id_type=MESH,
        )
        c.start()
        copies.append(c)
    for c in copies:
        c.wait()


def gather_kernel(nd, nh, x_ref, out_ref, *sems):
    greet(nd, nh)
    d, h = lax.axis_index("dp"), lax.axis_index("head")

    def own_copy():
        out_ref[:, d, h] = x_ref[...]

    spread(nd, nh, out_ref, own_copy, sems)


def gather_all(x, nd, nh, collective_id, name):
    tiles, rows, _ = x.shape
    return pl.pallas_call(
        functools.partial(gather_kernel, nd, nh),
        out_shape=jax.ShapeDtypeStruct((tiles, nd, nh, rows, LANES), F32),
        in_specs=[vmem()],
        out_specs=vmem(),
        scratch_shapes=[pltpu.SemaphoreType.DMA((nd,))] * 2
        + [pltpu.SemaphoreType.DMA((nh,))] * 2,
        compiler_params=pltpu.CompilerParams(
            collective_id=collective_id, has_side_effects=True, vmem_limit_bytes=40 << 20
        ),
        name=name,
    )(x)


def reduce_kernel(nd, nh, g_ref, out_ref, total, from_head, from_dp, send_a, recv_a, send_b, recv_b, *sems):
    greet(nd, nh)
    d, h = lax.axis_index("dp"), lax.axis_index("head")
    copies = []
    for k in range(1, nh):
        peer = lax.rem(h + k, nh)
        c = pltpu.make_async_remote_copy(
            g_ref.at[:, :, peer], from_head.at[k], send_a.at[k], recv_a.at[k],
            device_id=(d, peer), device_id_type=MESH,
        )
        c.start()
        copies.append(c)
    for c in copies:
        c.wait()
    held = g_ref[:, :, h]
    for k in range(1, nh):
        held = held + from_head[k]
    total[...] = held
    copies = []
    for k in range(1, nd):
        peer = lax.rem(d + k, nd)
        c = pltpu.make_async_remote_copy(
            total.at[:, peer], from_dp.at[k], send_b.at[k], recv_b.at[k],
            device_id=(peer, h), device_id_type=MESH,
        )
        c.start()
        copies.append(c)
    for c in copies:
        c.wait()

    def own_copy():
        mine = total[:, d]
        for k in range(1, nd):
            mine = mine + from_dp[k]
        out_ref[:, d, h] = mine

    spread(nd, nh, out_ref, own_copy, sems)


def reduce_all(g, collective_id, name):
    tiles, nd, nh, rows, _ = g.shape
    return pl.pallas_call(
        functools.partial(reduce_kernel, nd, nh),
        out_shape=jax.ShapeDtypeStruct(g.shape, F32),
        in_specs=[vmem()],
        out_specs=vmem(),
        scratch_shapes=[
            pltpu.VMEM((tiles, nd, rows, LANES), F32),
            pltpu.VMEM((nh, tiles, nd, rows, LANES), F32),
            pltpu.VMEM((nd, tiles, rows, LANES), F32),
        ]
        + [pltpu.SemaphoreType.DMA((nh,))] * 2
        + [pltpu.SemaphoreType.DMA((nd,))] * 4
        + [pltpu.SemaphoreType.DMA((nh,))] * 2,
        compiler_params=pltpu.CompilerParams(
            collective_id=collective_id, has_side_effects=True, vmem_limit_bytes=56 << 20
        ),
        name=name,
    )(g)


def attend_kernel(
    lengths, x_ref, w_ref, pn_ref, bias_ref, proj_ref, p_ref, inv_ref, o_ref, wt_out, wt, bias_col
):
    step = pl.program_id(0)
    h = lax.axis_index("head")
    width = w_ref.shape[2]
    keys = x_ref.shape[1]

    @pl.when(step == 0)
    def _():
        pt = pn_ref[...].T.astype(BF16)
        own = pn_ref[pl.ds(pl.multiple_of(h * width, width), width), :].astype(BF16)
        for j in range(3):
            up = own[:, (3 + j) * RANK : (4 + j) * RANK]
            delta = nn(up, pt[j * RANK : (j + 1) * RANK])
            wt[j * width : (j + 1) * width] = (
                w_ref[j].astype(F32).T + LOWRANK * delta
            ).astype(BF16)
        wt[3 * width : 3 * width + 3 * RANK] = pt[0 : 3 * RANK]
        wt_out[...] = wt[...]
        bias_col[...] = bias_ref[...].T

    proj = nt(wt[...], x_ref[0])
    rows = pl.ds(pl.multiple_of(h * width, width), width)
    for j in range(3):
        proj_ref[0, j * width : (j + 1) * width] = (
            proj[j * width : (j + 1) * width] + bias_col[rows, j : j + 1]
        ).astype(BF16)
    proj_ref[0, 3 * width :] = proj[3 * width :].astype(BF16)
    valid = lax.broadcasted_iota(jnp.int32, (keys, 1), 0) < lengths[step]
    results = []
    for head in range(width // DH):
        part = slice(head * DH, (head + 1) * DH)
        qt = proj_ref[0, part] * jnp.asarray(DH ** (-0.5), BF16)
        kt = proj_ref[0, width + head * DH : width + (head + 1) * DH]
        vt = proj_ref[0, 2 * width + head * DH : 2 * width + (head + 1) * DH]
        st = jnp.where(valid, tn(kt, qt), -1e30)
        top = jnp.max(st, axis=0, keepdims=True)
        et = jnp.exp(st - top)
        inverse = 1.0 / jnp.sum(et, axis=0, keepdims=True)
        low = et.astype(BF16)
        p_ref[0, head] = low
        inv_ref[0, head : head + 1] = inverse
        results.append(nn(vt, low) * inverse)
    o_ref[0] = jnp.concatenate(results, axis=0).T.astype(BF16)


def attend(hidden, lengths, weight, packed, bias):
    count, keys, model = hidden.shape
    width = weight.shape[2]
    heads = width // DH
    tall = 3 * width + 3 * RANK
    bias = jnp.pad(bias, ((0, 5), (0, 0)))
    return pl.pallas_call(
        attend_kernel,
        grid_spec=pltpu.PrefetchScalarGridSpec(
            num_scalar_prefetch=1,
            grid=(count,),
            in_specs=[
                pl.BlockSpec((1, keys, model), lambda s, n: (s, 0, 0)),
                vmem(), vmem(), vmem(),
            ],
            out_specs=[
                pl.BlockSpec((1, tall, keys), lambda s, n: (s, 0, 0)),
                pl.BlockSpec((1, heads, keys, keys), lambda s, n: (s, 0, 0, 0)),
                pl.BlockSpec((1, heads, keys), lambda s, n: (s, 0, 0)),
                pl.BlockSpec((1, keys, width), lambda s, n: (s, 0, 0)),
                vmem(),
            ],
            scratch_shapes=[pltpu.VMEM((tall, model), BF16), pltpu.VMEM((model, 8), F32)],
        ),
        out_shape=[
            jax.ShapeDtypeStruct((count, tall, keys), BF16),
            jax.ShapeDtypeStruct((count, heads, keys, keys), BF16),
            jax.ShapeDtypeStruct((count, heads, keys), F32),
            jax.ShapeDtypeStruct((count, keys, width), BF16),
            jax.ShapeDtypeStruct((tall, model), BF16),
        ],
        compiler_params=pltpu.CompilerParams(vmem_limit_bytes=48 << 20),
        name="attend",
    )(lengths, hidden, weight, packed, bias)


def tail_density(a):
    e = jnp.exp(-0.5 * a * a)
    t = 1.0 / (1.0 + (0.3275911 * 0.7071067811865476) * jnp.abs(a))
    poly = 1.061405429 * t - 1.453152027
    poly = poly * t + 1.421413741
    poly = poly * t - 0.284496736
    poly = poly * t + 0.254829592
    q = (0.5 * poly * t) * e
    return jnp.where(a >= 0, 1.0 - q, q), e * 0.3989422804014327


def centred(v):
    c = v - jnp.mean(v, axis=-1, keepdims=True)
    inverse = lax.rsqrt(jnp.mean(c * c, axis=-1, keepdims=True) + EPS_NORM)
    return c * inverse, inverse


def norm_back(e, n, inverse):
    return inverse * (
        e - jnp.mean(e, axis=-1, keepdims=True) - n * jnp.mean(e * n, axis=-1, keepdims=True)
    )


def token_kernel(
    nh, o0, o1, o2, o3, x_hbm, gout, wo0, wo1, wo2, wo3, wu0, wu1, wu2, wu3, wd0, wd1, wd2, wd3,
    tile_a, tile_b, shifts, gains, up_bias,
    result, first, go0, go1, go2, go3, grad_a, grad_b,
    x, wo, ocat, wu, wd, f, slope, h1, n1, i1, h1b, r2, gf, acc, gat, bt, gbt, sem_x, sem_w,
):
    h = lax.axis_index("head")
    pairs, part, model = x.shape
    tokens = pairs * part
    width = wo0.shape[0]
    relative = [jnp.bitwise_xor(h, r) for r in range(nh)]
    own = pltpu.make_async_copy(
        x_hbm.at[:, pl.ds(pl.multiple_of(h * part, part), part), :], x, sem_x
    )
    own.start()
    fetch = []
    for r, (a, b) in enumerate(zip((wu0, wu1, wu2, wu3), (wd0, wd1, wd2, wd3))):
        fetch.append(
            (
                pltpu.make_async_copy(a, wu.at[r], sem_w.at[0, r]),
                pltpu.make_async_copy(b, wd.at[r], sem_w.at[1, r]),
            )
        )
    for r in range(nh):
        fetch[r][0].start()
    for r in range(nh):
        fetch[r][1].start()
    for r, (o, w) in enumerate(zip((o0, o1, o2, o3), (wo0, wo1, wo2, wo3))):
        ocat[:, r * width : (r + 1) * width] = o[...].reshape(tokens, width)
        wo[r * width : (r + 1) * width] = w[...]
    at = tile_a[...].T.astype(BF16)
    p4t, p8t, p9t = (at[m * RANK : (m + 1) * RANK] for m in (1, 2, 3))
    p3 = jnp.concatenate(
        [
            tile_a[pl.ds(pl.multiple_of(relative[r] * width, width), width), :]
            for r in range(nh)
        ],
        axis=0,
    )
    p3t = p3.T.astype(BF16)[0:RANK]
    bt[...] = tile_b[...].T.astype(BF16)

    def inner(q, r):
        return bt[pl.ds(pl.multiple_of(relative[r] * 2 * RANK, 2 * RANK) + q * RANK, RANK), :]

    z_o = nt(ocat[...], p3t).astype(BF16)
    acc[...] = nn(ocat[...], wo[...]) + nn(z_o, p8t) * LOWRANK
    own.wait()
    v = x[...].reshape(tokens, model).astype(F32) + acc[...] + shifts[0:1]
    n, inv = centred(v)
    n1[...] = n
    i1[...] = inv
    h1[...] = n * gains[0:1] + shifts[1:2]
    h1b[...] = h1[...].astype(BF16)
    z_up = nt(h1b[...], p4t).astype(BF16)
    chunk = 256
    z_d = jnp.zeros((tokens, RANK), F32)
    for r in range(nh):
        fetch[r][0].wait()

        def up(c, carry, r=r):
            cols = pl.ds(pl.multiple_of(c * chunk, chunk), chunk)
            q1 = bt[
                pl.ds(pl.multiple_of(relative[r] * 2 * RANK, 2 * RANK) + RANK, RANK), cols
            ]
            a = (
                nn(h1b[...], wu[r, :, cols])
                + nn(z_up, q1) * LOWRANK
                + up_bias[pl.ds(relative[r], 1), cols]
            )
            cdf, density = tail_density(a)
            f[r, :, cols] = (a * cdf).astype(BF16)
            slope[r, :, cols] = (cdf + a * density).astype(BF16)
            return carry

        lax.fori_loop(0, model // chunk, up, 0)
        z_d = z_d + nt(f[r], inner(0, r))
    z_d = z_d.astype(BF16)
    for r in range(nh):
        fetch[r][1].wait()
        term = nn(f[r], wd[r])
        if r == 0:
            acc[...] = term + nn(z_d, p9t) * LOWRANK
        else:
            acc[...] += term
    n2, i2 = centred(h1[...] + acc[...] + shifts[2:3])
    result[...] = (n2 * gains[1:2] + shifts[3:4]).astype(BF16).reshape(result.shape)
    e = gout[...].reshape(tokens, model).astype(F32) * gains[1:2]
    r2[...] = norm_back(e, n2, i2)
    gf[...] = r2[...].astype(BF16)
    gzd = (nt(gf[...], p9t) * LOWRANK).astype(BF16)
    g9 = tn(z_d, gf[...]) * LOWRANK
    gzu = jnp.zeros((tokens, RANK), F32)
    for r in range(nh):
        gbt[pl.ds(pl.multiple_of(relative[r] * 2 * RANK, 2 * RANK), RANK), :] = tn(gzd, f[r])

        def down(c, carry, r=r):
            cols = pl.ds(pl.multiple_of(c * chunk, chunk), chunk)
            q0 = bt[pl.ds(pl.multiple_of(relative[r] * 2 * RANK, 2 * RANK), RANK), cols]
            df = nt(gf[...], wd[r, cols, :]) + nn(gzd, q0)
            slope[r, :, cols] = (df * slope[r, :, cols].astype(F32)).astype(BF16)
            return carry

        lax.fori_loop(0, model // chunk, down, 0)
        ga = slope[r]
        gzu = gzu + nt(ga, inner(1, r))
        gbt[pl.ds(pl.multiple_of(relative[r] * 2 * RANK, 2 * RANK) + RANK, RANK), :] = (
            tn(z_up, ga) * LOWRANK
        )
        term = nt(ga, wu[r])
        if r == 0:
            acc[...] = r2[...] + term
        else:
            acc[...] += term
    gzu = (gzu * LOWRANK).astype(BF16)
    g4 = tn(gzu, h1b[...])
    e = (acc[...] + nn(gzu, p4t)) * gains[0:1]
    r1 = norm_back(e, n1[...], i1[...])
    first[...] = r1.reshape(first.shape)
    gat[...] = r1.astype(BF16)
    gzo = (nt(gat[...], p8t) * LOWRANK).astype(BF16)
    g8 = tn(z_o, gat[...]) * LOWRANK
    g3 = tn(gzo, ocat[...])
    for r, go in enumerate((go0, go1, go2, go3)):
        rows = slice(r * width, (r + 1) * width)
        go[...] = (nt(gat[...], wo[rows]) + nn(gzo, p3t[:, rows])).astype(BF16).reshape(go.shape)
    zeros = jnp.zeros((4 * RANK, model), F32)
    grad_a[...] = jnp.concatenate([g3, g4, g8, g9, zeros], axis=0).T
    for r in range(nh):
        rows = pl.ds(pl.multiple_of(relative[r] * width, width), width)
        grad_a[rows, 0:RANK] = g3[:, r * width : (r + 1) * width].T
    grad_b[...] = gbt[...].T


def token_side(o, hidden, gout, wo, wu, wd, tile_a, tile_b, shifts, gains, up_bias):
    pairs, part, model = gout.shape
    tokens = pairs * part
    nh = len(o)
    width = wo[0].shape[0]
    shape = jax.ShapeDtypeStruct
    return pl.pallas_call(
        functools.partial(token_kernel, nh),
        out_shape=[
            shape((pairs, part, model), BF16),
            shape((pairs, part, model), F32),
            *[shape((pairs, part, width), BF16)] * nh,
            shape((model, LANES), F32),
            shape((model, LANES), F32),
        ],
        in_specs=[vmem()] * nh
        + [anywhere(), vmem()]
        + [vmem()] * nh
        + [anywhere()] * (2 * nh)
        + [vmem()] * 5,
        out_specs=[vmem()] * (4 + nh),
        scratch_shapes=[
            pltpu.VMEM((pairs, part, model), BF16),
            pltpu.VMEM((model, model), BF16),
            pltpu.VMEM((tokens, model), BF16),
            pltpu.VMEM((nh, model, model), BF16),
            pltpu.VMEM((nh, model, model), BF16),
            pltpu.VMEM((nh, tokens, model), BF16),
            pltpu.VMEM((nh, tokens, model), BF16),
            pltpu.VMEM((tokens, model), F32),
            pltpu.VMEM((tokens, model), F32),
            pltpu.VMEM((tokens, 1), F32),
            pltpu.VMEM((tokens, model), BF16),
            pltpu.VMEM((tokens, model), F32),
            pltpu.VMEM((tokens, model), BF16),
            pltpu.VMEM((tokens, model), F32),
            pltpu.VMEM((tokens, model), BF16),
            pltpu.VMEM((LANES, model), BF16),
            pltpu.VMEM((LANES, model), F32),
            pltpu.SemaphoreType.DMA,
            pltpu.SemaphoreType.DMA((2, nh)),
        ],
        compiler_params=pltpu.CompilerParams(vmem_limit_bytes=60 << 20),
        name="token_side",
    )(*o, hidden, gout, *wo, *wu, *wd, tile_a, tile_b, shifts, gains, up_bias)


def attend_back_kernel(
    nh, x_ref, proj_ref, p_ref, inv_ref, go0, go1, go2, go3, wt, pn_ref,
    part0, part1, part2, part3, grad_out, got, gproj, down_t, grad_t,
):
    step = pl.program_id(0)
    h = lax.axis_index("head")
    relative = [jnp.bitwise_xor(h, r) for r in range(nh)]
    width = go0.shape[2]
    part = go0.shape[1]
    model = x_ref.shape[2]
    own_rows = pl.ds(pl.multiple_of(h * width, width), width)

    @pl.when(step == 0)
    def _():
        own = pn_ref[own_rows, :]
        down_t[...] = own.T.astype(BF16)
        grad_t[...] = jnp.zeros_like(grad_t)

    for r, go in enumerate((go0, go1, go2, go3)):
        got[:, pl.ds(pl.multiple_of(relative[r] * part, part), part)] = go[0].T
    scale = jnp.asarray(DH ** (-0.5), BF16)
    for head in range(width // DH):
        part_h = slice(head * DH, (head + 1) * DH)
        rows_k = slice(width + head * DH, width + (head + 1) * DH)
        rows_v = slice(2 * width + head * DH, 2 * width + (head + 1) * DH)
        inverse = inv_ref[0, head : head + 1]
        qt = proj_ref[0, part_h] * scale
        kt = proj_ref[0, rows_k] * scale
        vt = proj_ref[0, rows_v]
        gs = (got[part_h].astype(F32) * inverse).astype(BF16)
        et = p_ref[0, head]
        ef = et.astype(F32)
        dpt = tn(vt, gs)
        delta = jnp.sum(ef * dpt, axis=0, keepdims=True) * inverse
        gst = (ef * (dpt - delta)).astype(BF16)
        gproj[part_h] = nn(kt, gst).astype(BF16)
        gproj[rows_k] = nt(qt, gst).astype(BF16)
        gproj[rows_v] = nt(gs, et).astype(BF16)
    inner = []
    for j in range(3):
        block = gproj[j * width : (j + 1) * width]
        ut = proj_ref[0, 3 * width + j * RANK : 3 * width + (j + 1) * RANK]
        grad_t[(3 + j) * RANK : (4 + j) * RANK, 0:width] += nt(ut, block) * LOWRANK
        inner.append(nn(down_t[(3 + j) * RANK : (4 + j) * RANK], block) * LOWRANK)
    inner = jnp.concatenate(inner, axis=0).astype(BF16)
    grad_t[0 : 3 * RANK] += nn(inner, x_ref[0])
    whole = tn(gproj[...], wt[0 : 3 * width])
    got_rows = whole.astype(BF16)
    parts = (part0, part1, part2, part3)
    for r in range(nh):
        for block in range(nh):

            @pl.when(relative[r] == block)
            def _(r=r, block=block):
                parts[r][0] = got_rows[block * part : (block + 1) * part]

    @pl.when(step == pl.num_programs(0) - 1)
    def _():
        full = grad_t[...].T
        lane = lax.broadcasted_iota(jnp.int32, full.shape, 1)
        grad_out[...] = jnp.where(lane < 3 * RANK, full, 0.0)
        rows = full[0:width]
        lane = lax.broadcasted_iota(jnp.int32, rows.shape, 1)
        grad_out[own_rows, :] = jnp.where(
            lane < 3 * RANK, grad_out[own_rows, :], rows
        )


def attend_back(hidden, proj, p, inverse, go, wt, packed):
    count, keys, model = hidden.shape
    nh = len(go)
    part, width = go[0].shape[1:]
    heads = width // DH
    tall = 3 * width + 3 * RANK
    shape = jax.ShapeDtypeStruct
    return pl.pallas_call(
        functools.partial(attend_back_kernel, nh),
        grid=(count,),
        in_specs=[
            pl.BlockSpec((1, keys, model), lambda s: (s, 0, 0)),
            pl.BlockSpec((1, tall, keys), lambda s: (s, 0, 0)),
            pl.BlockSpec((1, heads, keys, keys), lambda s: (s, 0, 0, 0)),
            pl.BlockSpec((1, heads, keys), lambda s: (s, 0, 0)),
            *[pl.BlockSpec((1, part, width), lambda s: (s, 0, 0))] * nh,
            vmem(), vmem(),
        ],
        out_specs=[
            *[pl.BlockSpec((1, part, model), lambda s: (s, 0, 0))] * nh,
            vmem(),
        ],
        out_shape=[
            *[shape((count, part, model), BF16)] * nh,
            shape((model, LANES), F32),
        ],
        scratch_shapes=[
            pltpu.VMEM((width, keys), BF16),
            pltpu.VMEM((3 * width, keys), BF16),
            pltpu.VMEM((LANES, width), BF16),
            pltpu.VMEM((LANES, model), F32),
        ],
        compiler_params=pltpu.CompilerParams(vmem_limit_bytes=48 << 20),
        name="attend_back",
    )(hidden, proj, p, inverse, *go, wt, packed)


def optimizer_kernel(
    nh, g_ref, stats_m, stats_i, stats_r, roots_m, roots_i, roots_r,
    grad_m, grad_i, step_m, step_i, new_m, new_i, new_r, squares, gt,
):
    owner = lax.axis_index("dp") * nh + lax.axis_index("head")
    count, rows, model = stats_m.shape
    rows_i = stats_i.shape[1]
    for t in range(3):
        gt[t] = g_ref[t].T
    own = [g_ref[t, pl.ds(owner * rows, rows), :] for t in range(2)]

    def finish(m, u, where, j):
        u = nn(u, roots_r[m], HIGH)
        where[j] = u
        squares[m : m + 1] = jnp.broadcast_to(
            jnp.sum(jnp.sum(u * u, axis=0, keepdims=True), axis=1, keepdims=True), (1, LANES)
        )

    squares[...] = jnp.zeros_like(squares)
    for j in range(count):
        t, m = slot_of(j)
        lanes = slice(m * RANK, (m + 1) * RANK)
        mine = own[t][:, lanes]
        full = gt[t, lanes]
        grad_m[j] = mine
        new_m[j] = DECAY * stats_m[j] + (1.0 - DECAY) * nn(mine, full, HIGH)
        new_r[j] = DECAY * stats_r[j] + (1.0 - DECAY) * nt(full, full, HIGH)
        finish(j, nt(roots_m[j], full, HIGH), step_m, j)
    blocks = stats_i.shape[2] // model
    per = model // rows_i
    block = owner // per
    tall = g_ref[2, pl.ds((owner - block * per) * rows_i, rows_i), :]
    for q in range(2):
        mine = jnp.zeros((rows_i, RANK), F32)
        gram = jnp.zeros((RANK, RANK), F32)
        u = jnp.zeros((rows_i, RANK), F32)
        for k in range(blocks):
            lanes = slice((2 * k + q) * RANK, (2 * k + q + 1) * RANK)
            mine = jnp.where(block == k, tall[:, lanes], mine)
        grad_i[q] = mine
        for k in range(blocks):
            lanes = slice((2 * k + q) * RANK, (2 * k + q + 1) * RANK)
            cols = slice(k * model, (k + 1) * model)
            full = gt[2, lanes]
            gram = gram + nt(full, full, HIGH)
            u = u + nt(roots_i[q, :, cols], full, HIGH)
            new_i[q, :, cols] = DECAY * stats_i[q, :, cols] + (1.0 - DECAY) * nn(
                mine, full, HIGH
            )
        new_r[count + q] = DECAY * stats_r[count + q] + (1.0 - DECAY) * gram
        finish(count + q, u, step_i, q)


def optimizer(g, stats_m, stats_i, stats_r, roots_m, roots_i, roots_r, nh):
    shape = jax.ShapeDtypeStruct
    count, rows, model = stats_m.shape
    rows_i = stats_i.shape[1]
    return pl.pallas_call(
        functools.partial(optimizer_kernel, nh),
        in_specs=[vmem()] * 7,
        out_specs=[vmem()] * 8,
        out_shape=[
            shape((count, rows, RANK), F32),
            shape((2, rows_i, RANK), F32),
            shape((count, rows, RANK), F32),
            shape((2, rows_i, RANK), F32),
            shape(stats_m.shape, F32),
            shape(stats_i.shape, F32),
            shape(stats_r.shape, F32),
            shape((16, LANES), F32),
        ],
        scratch_shapes=[pltpu.VMEM((3, LANES, model), F32)],
        compiler_params=pltpu.CompilerParams(vmem_limit_bytes=48 << 20),
        name="optimizer",
    )(g, stats_m, stats_i, stats_r, roots_m, roots_i, roots_r)


def local(
    nd,
    nh,
    hidden_input,
    grad_out,
    pair_lengths,
    query_key_value_weight,
    qkv_bias,
    output_projection_weight,
    shifts,
    gains,
    up_projection_weight,
    up_bias,
    down_projection_weight,
    adapters_model,
    adapters_inner,
    stats_model,
    stats_inner,
    stats_rank,
    roots_model,
    roots_inner,
    roots_rank,
):
    owners = nd * nh
    count, rows, _ = adapters_model.shape
    rows_i = adapters_inner.shape[1]
    model = hidden_input.shape[2]
    split = rows_i // rows
    padded = -(-rows // 8) * 8

    def swap(values, r):
        return lax.ppermute(values, "head", [(i, i ^ r) for i in range(nh)])

    def lanes_of(which):
        part = jnp.stack([adapters_model[j] for j in which], axis=1)
        return jnp.pad(part.reshape(rows, -1), ((0, 0), (0, LANES - len(which) * RANK)))

    inner = adapters_inner.reshape(2, split, rows, RANK).transpose(2, 1, 0, 3).reshape(rows, -1)
    packed = jnp.stack([lanes_of(EARLY_SLOTS), lanes_of(LATE_SLOTS), inner])
    packed = packed.astype(BF16).astype(F32)
    packed = jnp.pad(packed, ((0, 0), (0, padded - rows), (0, 0)))
    everyone = gather_all(packed, nd, nh, 1, "gather_adapters")
    everyone = everyone[:, :, :, :rows].reshape(3, model, LANES)
    tile_b = (
        everyone[2]
        .reshape(split, owners // split, rows, split, 2 * RANK)
        .transpose(1, 3, 2, 0, 4)
        .reshape(model, LANES)
    )
    def others(weight):
        return [weight] + [swap(weight, r) for r in range(1, nh)]

    wo, wu, wd = map(
        others, (output_projection_weight, up_projection_weight, down_projection_weight)
    )
    proj, p, inverse, o, wt = attend(
        hidden_input, pair_lengths, query_key_value_weight, everyone[0], qkv_bias
    )
    part = grad_out.shape[1]
    h = lax.axis_index("head")

    def token_block(values, r):
        return lax.dynamic_slice_in_dim(values, (h ^ r) * part, part, 1)

    o = [token_block(o, 0)] + [swap(token_block(o, r), r) for r in range(1, nh)]
    out = token_side(
        o, hidden_input, grad_out, wo, wu, wd, everyone[1], tile_b, shifts, gains,
        up_bias.reshape(nh, model),
    )
    result, first = out[0], out[1]
    go = [out[2]] + [swap(out[2 + r], r) for r in range(1, nh)]
    grad_a, grad_b = out[2 + nh :]
    back = attend_back(hidden_input, proj, p, inverse, go, wt, everyone[0])
    near = [swap(back[1], 1), swap(back[3], 1)]
    far = (back[2].astype(F32) + near[1].astype(F32)).astype(BF16)
    far = swap(far, 2)
    grad_in = (
        first + back[0].astype(F32) + near[0].astype(F32) + far.astype(F32)
    ).astype(BF16)
    grads = jnp.stack([back[4], grad_a, grad_b]).reshape(3, nd, nh, rows, LANES)
    grads = jnp.pad(grads, ((0, 0),) * 3 + ((0, padded - rows), (0, 0)))
    grads = reduce_all(grads, 2, "reduce_gradients")
    grads = grads[:, :, :, :rows].reshape(3, model, LANES)
    grad_m, grad_i, step_m, step_i, new_m, new_i, new_r, squares = optimizer(
        grads, stats_model, stats_inner, stats_rank, roots_model, roots_inner, roots_rank, nh
    )
    squares = gather_all(squares[None], nd, nh, 3, "gather_squares")
    squares = jnp.sum(squares[0, :, :, :, 0], axis=(0, 1))
    rates_m = jnp.where(jnp.arange(count) < 5, RATE_FIRST, RATE_SECOND)
    rates_i = jnp.where(jnp.arange(2) < 1, RATE_FIRST, RATE_SECOND)
    scale_m = rates_m * lax.rsqrt(squares[:count] / (model * RANK) + 1e-6)
    scale_i = rates_i * lax.rsqrt(
        squares[count : count + 2] / (rows_i * owners * RANK) + 1e-6
    )
    return (
        result,
        grad_in,
        grad_m,
        grad_i,
        adapters_model - scale_m[:, None, None] * step_m,
        adapters_inner - scale_i[:, None, None] * step_i,
        new_m,
        new_i,
        new_r,
    )


def solution(mesh):
    rows = P(None, ("dp", "head"), None)
    in_specs = (
        P("dp", None, None),
        P("dp", "head", None),
        P("dp"),
        P(None, None, "head"),
        P(),
        P("head", None),
        P(),
        P(),
        P(None, "head"),
        P(),
        P("head", None),
        rows, rows, rows, rows,
        P(),
        rows, rows,
        P(),
    )
    out_specs = (
        P("dp", "head", None),
        P("dp", "head", None),
        rows, rows, rows, rows, rows, rows,
        P(),
    )
    body = functools.partial(local, mesh.shape["dp"], mesh.shape["head"])
    return jax.shard_map(body, mesh=mesh, in_specs=in_specs, out_specs=out_specs, check_vma=False)
```

```python
import functools

import jax
import jax.numpy as jnp
from jax import lax
from jax.experimental import pallas as pl
from jax.experimental.pallas import tpu as pltpu
from jax.sharding import PartitionSpec as P

DH = 64
RANK = 16
LANES = 128
LOWRANK = 2.0
RATE_FIRST = 0.01
RATE_SECOND = 0.16
DECAY = 0.5
EPS_NORM = 1e-5
MESH = pl.DeviceIdType.MESH
F32 = jnp.float32
BF16 = jnp.bfloat16
HIGH = lax.Precision.HIGHEST

EARLY_SLOTS = (0, 1, 2, 5, 6, 7)
LATE_SLOTS = (3, 4, 8, 9)


def slot_of(j):
    if j in EARLY_SLOTS:
        return 0, EARLY_SLOTS.index(j)
    return 1, LATE_SLOTS.index(j)


def nn(a, b, precision=None):
    return lax.dot_general(
        a, b, (((1,), (0,)), ((), ())), precision=precision, preferred_element_type=F32
    )


def nt(a, b, precision=None):
    return lax.dot_general(
        a, b, (((1,), (1,)), ((), ())), precision=precision, preferred_element_type=F32
    )


def tn(a, b, precision=None):
    return lax.dot_general(
        a, b, (((0,), (0,)), ((), ())), precision=precision, preferred_element_type=F32
    )


def vmem():
    return pl.BlockSpec(memory_space=pltpu.VMEM)


def anywhere():
    return pl.BlockSpec(memory_space=pl.ANY)


def greet(nd, nh):
    d, h = lax.axis_index("dp"), lax.axis_index("head")
    barrier = pltpu.get_barrier_semaphore()
    for k in range(1, nd):
        pl.semaphore_signal(
            barrier, inc=1, device_id=(lax.rem(d + k, nd), h), device_id_type=MESH
        )
    for k in range(1, nh):
        pl.semaphore_signal(
            barrier, inc=1, device_id=(d, lax.rem(h + k, nh)), device_id_type=MESH
        )
    pl.semaphore_wait(barrier, nd + nh - 2)


def spread(nd, nh, out_ref, own_copy, sems):
    send_d, recv_d, send_h, recv_h = sems
    d, h = lax.axis_index("dp"), lax.axis_index("head")
    own_copy()
    mine = out_ref.at[:, d, h]
    copies = []
    for k in range(1, nd):
        c = pltpu.make_async_remote_copy(
            mine, mine, send_d.at[k], recv_d.at[k],
            device_id=(lax.rem(d + k, nd), h), device_id_type=MESH,
        )
        c.start()
        copies.append(c)
    for c in copies:
        c.wait()
    column = out_ref.at[:, :, h]
    copies = []
    for k in range(1, nh):
        c = pltpu.make_async_remote_copy(
            column, column, send_h.at[k], recv_h.at[k],
            device_id=(d, lax.rem(h + k, nh)), device_id_type=MESH,
        )
        c.start()
        copies.append(c)
    for c in copies:
        c.wait()


def gather_kernel(nd, nh, x_ref, out_ref, *sems):
    greet(nd, nh)
    d, h = lax.axis_index("dp"), lax.axis_index("head")

    def own_copy():
        out_ref[:, d, h] = x_ref[...]

    spread(nd, nh, out_ref, own_copy, sems)


def gather_all(x, nd, nh, collective_id, name):
    tiles, rows, _ = x.shape
    return pl.pallas_call(
        functools.partial(gather_kernel, nd, nh),
        out_shape=jax.ShapeDtypeStruct((tiles, nd, nh, rows, LANES), F32),
        in_specs=[vmem()],
        out_specs=vmem(),
        scratch_shapes=[pltpu.SemaphoreType.DMA((nd,))] * 2
        + [pltpu.SemaphoreType.DMA((nh,))] * 2,
        compiler_params=pltpu.CompilerParams(
            collective_id=collective_id, has_side_effects=True, vmem_limit_bytes=40 << 20
        ),
        name=name,
    )(x)


def reduce_kernel(nd, nh, g_ref, out_ref, total, from_head, from_dp, send_a, recv_a, send_b, recv_b, *sems):
    greet(nd, nh)
    d, h = lax.axis_index("dp"), lax.axis_index("head")
    copies = []
    for k in range(1, nh):
        peer = lax.rem(h + k, nh)
        c = pltpu.make_async_remote_copy(
            g_ref.at[:, :, peer], from_head.at[k], send_a.at[k], recv_a.at[k],
            device_id=(d, peer), device_id_type=MESH,
        )
        c.start()
        copies.append(c)
    for c in copies:
        c.wait()
    held = g_ref[:, :, h]
    for k in range(1, nh):
        held = held + from_head[k]
    total[...] = held
    copies = []
    for k in range(1, nd):
        peer = lax.rem(d + k, nd)
        c = pltpu.make_async_remote_copy(
            total.at[:, peer], from_dp.at[k], send_b.at[k], recv_b.at[k],
            device_id=(peer, h), device_id_type=MESH,
        )
        c.start()
        copies.append(c)
    for c in copies:
        c.wait()

    def own_copy():
        mine = total[:, d]
        for k in range(1, nd):
            mine = mine + from_dp[k]
        out_ref[:, d, h] = mine

    spread(nd, nh, out_ref, own_copy, sems)


def reduce_all(g, collective_id, name):
    tiles, nd, nh, rows, _ = g.shape
    return pl.pallas_call(
        functools.partial(reduce_kernel, nd, nh),
        out_shape=jax.ShapeDtypeStruct(g.shape, F32),
        in_specs=[vmem()],
        out_specs=vmem(),
        scratch_shapes=[
            pltpu.VMEM((tiles, nd, rows, LANES), F32),
            pltpu.VMEM((nh, tiles, nd, rows, LANES), F32),
            pltpu.VMEM((nd, tiles, rows, LANES), F32),
        ]
        + [pltpu.SemaphoreType.DMA((nh,))] * 2
        + [pltpu.SemaphoreType.DMA((nd,))] * 4
        + [pltpu.SemaphoreType.DMA((nh,))] * 2,
        compiler_params=pltpu.CompilerParams(
            collective_id=collective_id, has_side_effects=True, vmem_limit_bytes=56 << 20
        ),
        name=name,
    )(g)


def attend_kernel(
    nd, nh, lengths, am, ai, x_ref, w_ref, bias_ref, wo, wu, wd,
    proj_ref, p_ref, inv_ref, o_all, go_w, gu_w, gd_w, wt, tile_a, bt, down_t,
    packed, every, obuf, bias_col, unpack,
    send_d, recv_d, send_h, recv_h, send_o, recv_o, keep_o, send_w, recv_w, send_s, recv_s,
):
    step = pl.program_id(0)
    d, h = lax.axis_index("dp"), lax.axis_index("head")
    count = o_all.shape[1]
    part = o_all.shape[2]
    width = w_ref.shape[1]
    keys = x_ref.shape[1]
    model = x_ref.shape[2]
    rows = am.shape[2]
    split = ai.shape[2] // rows
    owners = nd * nh
    quarter = lax.rem(d, 4)

    def at(a, b):
        return (jnp.bitwise_xor(d, a), jnp.bitwise_xor(h, b))

    def remote(src, dst, send, recv, device):
        return pltpu.make_async_remote_copy(
            src, dst, send, recv, device_id=device, device_id_type=MESH
        )

    own_w = (wo, wu, wd)
    all_w = (go_w, gu_w, gd_w)
    chunks = []
    for w in range(3):
        quarter_rows = own_w[w].shape[0] // 4
        pieces = 1 if w == 0 else 2
        for piece in range(pieces):
            chunks.append((w, quarter_rows, piece * quarter_rows // pieces, quarter_rows // pieces))

    def region(ref, c, who, half=None):
        w, quarter_rows, offset, size = chunks[c]
        base = jnp.bitwise_xor(quarter, who) * quarter_rows + offset
        if half is not None:
            first = -(-(size // 2) // 16) * 16
            base, size = (base, first) if half == 0 else (base + first, size - first)
        return ref.at[pl.ds(pl.multiple_of(base, 16), size)]

    def over_x(c):
        w = chunks[c][0]
        return remote(
            region(own_w[w], c, 0), region(all_w[w].at[1], c, 0),
            send_w.at[0, c], recv_w.at[0, c], at(0, 2),
        )

    def spread_w(c, axis):
        here = region(all_w[chunks[c][0]].at[1], c, 0)
        return remote(here, here, send_w.at[axis, c], recv_w.at[axis, c], at(axis, 0))

    def relay_w(c, axis):
        here = region(all_w[chunks[c][0]].at[1], c, 3 - axis, axis - 1)
        return remote(here, here, send_w.at[2 + axis, c], recv_w.at[2 + axis, c], at(axis, 0))

    def sibling_own(w):
        return remote(own_w[w], all_w[w].at[0], send_s.at[0, w], recv_s.at[0, w], at(0, 1))

    def sibling_far(w):
        return remote(
            all_w[w].at[1], all_w[w].at[2], send_s.at[1, w], recv_s.at[1, w], at(0, 1)
        )

    def forward(c):
        over_x(c).wait_recv()
        spread_w(c, 2).start()
        spread_w(c, 1).start()

    def relay(c):
        spread_w(c, 2).wait_recv()
        relay_w(c, 1).start()
        spread_w(c, 1).wait_recv()
        relay_w(c, 2).start()

    def arrived(c):
        relay_w(c, 1).wait_recv()
        relay_w(c, 2).wait_recv()

    def finish(w, which):
        for c in which:
            arrived(c)
        sibling_far(w).start()

    def to_dp(k, tiles, slot):
        return remote(
            packed.at[tiles], every.at[tiles, d, h], send_d.at[slot, k], recv_d.at[slot, k],
            (lax.rem(d + k, nd), h),
        )

    def to_head(b, tiles, slot):
        column = every.at[tiles, :, h]
        return remote(column, column, send_h.at[slot, b], recv_h.at[slot, b], at(0, b))

    def pass_on(tiles, slot):
        column = every.at[tiles, :, jnp.bitwise_xor(h, 2)]
        return remote(column, column, send_h.at[slot, 3], recv_h.at[slot, 3], at(0, 1))

    critical, later = pl.ds(0, 1), pl.ds(1, 2)

    def natural(t):
        if every.shape[3] == rows:
            return every[t].reshape(model, LANES)
        return jnp.concatenate(
            [every[t, i // nh, i % nh, 0:rows] for i in range(owners)], axis=0
        )

    @pl.when(step == 0)
    def _():
        greet(nd, nh)
        over_x(0).start()
        over_x(1).start()
        blank = jnp.zeros((LANES, rows), F32)
        packed[...] = jnp.zeros_like(packed)
        groups = [
            [am[j] for j in EARLY_SLOTS],
            [am[j] for j in LATE_SLOTS],
            [ai[q][:, k * rows : (k + 1) * rows] for k in range(split) for q in range(2)],
        ]
        for t, group in enumerate(groups):
            stacked = jnp.concatenate(group + [blank[len(group) * RANK :]], axis=0) if len(
                group
            ) * RANK < LANES else jnp.concatenate(group, axis=0)
            packed[t, 0:rows] = stacked.T.astype(BF16).astype(F32)
        for k in range(1, nd):
            to_dp(k, critical, 0).start()
        every[:, d, h] = packed[...]
        for k in range(1, nd):
            to_dp(k, critical, 0).wait_recv()
        to_head(2, critical, 0).start()
        to_head(1, critical, 0).start()
        for k in range(1, nd):
            to_dp(k, later, 1).start()
        sibling_own(0).start()
        bias_col[...] = jnp.concatenate(
            [bias_ref[...], jnp.zeros((5, model), F32)], axis=0
        ).T
        to_head(2, critical, 0).wait_recv()
        pass_on(critical, 0).start()
        for c in range(2, len(chunks)):
            over_x(c).start()
        sibling_own(1).start()
        sibling_own(2).start()
        to_head(1, critical, 0).wait_recv()
        pass_on(critical, 0).wait_recv()
        pn = natural(0)
        pt = pn.T.astype(BF16)
        wt[3 * width :] = pt[0 : 3 * RANK]
        tile_a[...] = pn
        own = tile_a[pl.ds(pl.multiple_of(h * width, width), width), :]
        down_t[...] = own.T.astype(BF16)
        own = own.astype(BF16)
        for j in range(3):
            delta = nn(own[:, (3 + j) * RANK : (4 + j) * RANK], pt[j * RANK : (j + 1) * RANK])
            wt[j * width : (j + 1) * width] = (w_ref[j].astype(F32) + LOWRANK * delta).astype(
                BF16
            )

    proj = nt(wt[...], x_ref[0])
    mine = pl.ds(pl.multiple_of(h * width, width), width)
    for j in range(3):
        proj_ref[0, j * width : (j + 1) * width] = (
            proj[j * width : (j + 1) * width] + bias_col[mine, j : j + 1]
        ).astype(BF16)
    proj_ref[0, 3 * width :] = proj[3 * width :].astype(BF16)
    valid = lax.broadcasted_iota(jnp.int32, (keys, 1), 0) < lengths[step]

    @pl.when(step == 0)
    def _():
        forward(0)
        forward(1)

    @pl.when(step == 2)
    def _():
        relay(2)
        forward(4)

    results = []
    for head in range(width // DH):
        rows_q = slice(head * DH, (head + 1) * DH)
        qt = proj_ref[0, rows_q] * jnp.asarray(DH ** (-0.5), BF16)
        kt = proj_ref[0, width + head * DH : width + (head + 1) * DH]
        vt = proj_ref[0, 2 * width + head * DH : 2 * width + (head + 1) * DH]
        st = jnp.where(valid, tn(kt, qt), -1e30)
        top = jnp.max(st, axis=0, keepdims=True)
        et = jnp.exp(st - top)
        inverse = 1.0 / jnp.sum(et, axis=0, keepdims=True)
        low = et.astype(BF16)
        p_ref[0, head] = low
        inv_ref[0, head : head + 1] = inverse
        results.append(nn(vt, low) * inverse)
    o = jnp.concatenate(results, axis=0).T.astype(BF16)
    obuf[step] = o.reshape(nh, part, width)

    def send_block(r, s):
        return remote(
            obuf.at[s, jnp.bitwise_xor(h, r)], o_all.at[r, s],
            send_o.at[r, s], recv_o.at[r, s], at(0, r),
        )

    def keep_block(s):
        return pltpu.make_async_copy(obuf.at[s, h], o_all.at[0, s], keep_o.at[s])

    for r in (2, 3, 1):
        send_block(r, step).start()
    keep_block(step).start()

    @pl.when(step == 0)
    def _():
        forward(2)
        relay(0)
        for k in range(1, nd):
            to_dp(k, later, 1).wait_recv()
        to_head(2, later, 1).start()
        to_head(1, later, 1).start()

    @pl.when(step == 1)
    def _():
        relay(1)
        forward(3)
        to_head(2, later, 1).wait_recv()
        pass_on(later, 1).start()
        finish(0, (0,))

    @pl.when(step == 2)
    def _():
        relay(3)

    @pl.when(step == 3)
    def _():
        finish(1, (1, 2))
        relay(4)
        to_head(1, later, 1).wait_recv()
        pass_on(later, 1).wait_recv()
        tile_a[...] = natural(1)
        per = owners // split
        for w in range(per):
            for k in range(split):
                blocks = [
                    every[2, (b * per + w) // nh, (b * per + w) % nh, 0:rows, :][
                        :, 2 * RANK * k : 2 * RANK * (k + 1)
                    ]
                    for b in range(split)
                ]
                base = (w * split + k) * rows
                joined = jnp.concatenate(blocks, axis=1)
                unpack[base : base + rows] = joined
        bt[...] = unpack[...].T.astype(BF16)

    @pl.when(step == count - 1)
    def _():
        finish(2, (3, 4))
        for c in range(len(chunks)):
            over_x(c).wait_send()
            for axis in (1, 2):
                spread_w(c, axis).wait_send()
                relay_w(c, axis).wait_send()
        for slot, tiles in enumerate((critical, later)):
            for k in range(1, nd):
                to_dp(k, tiles, slot).wait_send()
            for b in (1, 2):
                to_head(b, tiles, slot).wait_send()
            pass_on(tiles, slot).wait_send()
        for s in range(count):
            keep_block(s).wait()
            for r in range(1, nh):
                send_block(r, s).wait()
        for w in range(3):
            sibling_own(w).wait()
            sibling_far(w).wait()


def attend(nd, nh, hidden, lengths, adapters_m, adapters_i, weight, bias, wo, wu, wd):
    count, keys, model = hidden.shape
    width = weight.shape[1]
    heads = width // DH
    tall = 3 * width + 3 * RANK
    part = keys // nh
    rows = adapters_m.shape[2]
    padded = -(-rows // 8) * 8
    shape = jax.ShapeDtypeStruct
    dma = pltpu.SemaphoreType.DMA
    return pl.pallas_call(
        functools.partial(attend_kernel, nd, nh),
        grid=(count,),
        in_specs=[
            pl.BlockSpec(memory_space=pltpu.SMEM),
            vmem(), vmem(),
            pl.BlockSpec((1, keys, model), lambda s: (s, 0, 0)),
            vmem(), vmem(), anywhere(), anywhere(), anywhere(),
        ],
        out_specs=[
            pl.BlockSpec((1, tall, keys), lambda s: (s, 0, 0)),
            pl.BlockSpec((1, heads, keys, keys), lambda s: (s, 0, 0, 0)),
            pl.BlockSpec((1, heads, keys), lambda s: (s, 0, 0)),
            anywhere(), anywhere(), anywhere(), anywhere(),
            vmem(), vmem(), vmem(), vmem(),
        ],
        out_shape=[
            shape((count, tall, keys), BF16),
            shape((count, heads, keys, keys), BF16),
            shape((count, heads, keys), F32),
            shape((nh, count, part, width), BF16),
            *[shape((nh - 1, *w.shape), BF16) for w in (wo, wu, wd)],
            shape((tall, model), BF16),
            shape((model, LANES), F32),
            shape((LANES, model), BF16),
            shape((LANES, width), BF16),
        ],
        scratch_shapes=[
            pltpu.VMEM((3, padded, LANES), F32),
            pltpu.VMEM((3, nd, nh, padded, LANES), F32),
            pltpu.VMEM((count, nh, part, width), BF16),
            pltpu.VMEM((model, 8), F32),
            pltpu.VMEM((model, LANES), F32),
            dma((2, nd)), dma((2, nd)), dma((2, 4)), dma((2, 4)),
            dma((nh, count)), dma((nh, count)), dma((count,)),
            dma((5, 5)), dma((5, 5)), dma((2, 3)), dma((2, 3)),
        ],
        compiler_params=pltpu.CompilerParams(
            collective_id=1, has_side_effects=True, vmem_limit_bytes=48 << 20
        ),
        name="attend",
    )(lengths, adapters_m, adapters_i, hidden, weight, bias, wo, wu, wd)


def tail_density(a):
    e = jnp.exp(-0.5 * a * a)
    t = 1.0 / (1.0 + (0.3275911 * 0.7071067811865476) * jnp.abs(a))
    poly = 1.061405429 * t - 1.453152027
    poly = poly * t + 1.421413741
    poly = poly * t - 0.284496736
    poly = poly * t + 0.254829592
    q = (0.5 * poly * t) * e
    return jnp.where(a >= 0, 1.0 - q, q), e * 0.3989422804014327


def centred(v):
    c = v - jnp.mean(v, axis=-1, keepdims=True)
    inverse = lax.rsqrt(jnp.mean(c * c, axis=-1, keepdims=True) + EPS_NORM)
    return c * inverse, inverse


def norm_back(e, n, inverse):
    return inverse * (
        e - jnp.mean(e, axis=-1, keepdims=True) - n * jnp.mean(e * n, axis=-1, keepdims=True)
    )


def token_kernel(
    nh, o_all, x_hbm, gout, wo_own, wo_rest, wu_own, wu_rest, wd_own, wd_rest,
    tile_a, bt, shifts, gains, up_bias,
    result, first, go0, go1, go2, go3, grad_a, grad_b,
    x, wo, ocat, wu, wd, f, slope, h1, n1, i1, h1b, r2, gf, acc, gat, gbt, sem_x, sem_w,
):
    h = lax.axis_index("head")
    pairs, part, model = x.shape
    tokens = pairs * part
    width = wo_own.shape[0]
    relative = [jnp.bitwise_xor(h, r) for r in range(nh)]
    own = pltpu.make_async_copy(
        x_hbm.at[:, pl.ds(pl.multiple_of(h * part, part), part), :], x, sem_x
    )
    own.start()
    fetch = []
    for r in range(nh):
        a = wu_own if r == 0 else wu_rest.at[r - 1]
        b = wd_own if r == 0 else wd_rest.at[r - 1]
        fetch.append(
            (
                pltpu.make_async_copy(a, wu.at[r], sem_w.at[0, r]),
                pltpu.make_async_copy(b, wd.at[r], sem_w.at[1, r]),
            )
        )
    for r in range(nh):
        fetch[r][0].start()
    for r in range(nh):
        fetch[r][1].start()
    for r in range(nh):
        ocat[:, r * width : (r + 1) * width] = o_all[r].reshape(tokens, width)
        wo[r * width : (r + 1) * width] = wo_own[...] if r == 0 else wo_rest[r - 1]
    at = tile_a[...].T.astype(BF16)
    p4t, p8t, p9t = (at[m * RANK : (m + 1) * RANK] for m in (1, 2, 3))
    p3 = jnp.concatenate(
        [
            tile_a[pl.ds(pl.multiple_of(relative[r] * width, width), width), :]
            for r in range(nh)
        ],
        axis=0,
    )
    p3t = p3.T.astype(BF16)[0:RANK]

    def inner(q, r):
        return bt[pl.ds(pl.multiple_of(relative[r] * 2 * RANK, 2 * RANK) + q * RANK, RANK), :]

    z_o = nt(ocat[...], p3t).astype(BF16)
    acc[...] = nn(ocat[...], wo[...]) + nn(z_o, p8t) * LOWRANK
    own.wait()
    v = x[...].reshape(tokens, model).astype(F32) + acc[...] + shifts[0:1]
    n, inv = centred(v)
    n1[...] = n
    i1[...] = inv
    h1[...] = n * gains[0:1] + shifts[1:2]
    h1b[...] = h1[...].astype(BF16)
    z_up = nt(h1b[...], p4t).astype(BF16)
    chunk = 256
    z_d = jnp.zeros((tokens, RANK), F32)
    for r in range(nh):
        fetch[r][0].wait()

        def up(c, carry, r=r):
            cols = pl.ds(pl.multiple_of(c * chunk, chunk), chunk)
            q1 = bt[
                pl.ds(pl.multiple_of(relative[r] * 2 * RANK, 2 * RANK) + RANK, RANK), cols
            ]
            a = (
                nn(h1b[...], wu[r, :, cols])
                + nn(z_up, q1) * LOWRANK
                + up_bias[pl.ds(relative[r], 1), cols]
            )
            cdf, density = tail_density(a)
            f[r, :, cols] = (a * cdf).astype(BF16)
            slope[r, :, cols] = (cdf + a * density).astype(BF16)
            return carry

        lax.fori_loop(0, model // chunk, up, 0)
        z_d = z_d + nt(f[r], inner(0, r))
    z_d = z_d.astype(BF16)
    for r in range(nh):
        fetch[r][1].wait()
        term = nn(f[r], wd[r])
        if r == 0:
            acc[...] = term + nn(z_d, p9t) * LOWRANK
        else:
            acc[...] += term
    n2, i2 = centred(h1[...] + acc[...] + shifts[2:3])
    result[...] = (n2 * gains[1:2] + shifts[3:4]).astype(BF16).reshape(result.shape)
    e = gout[...].reshape(tokens, model).astype(F32) * gains[1:2]
    r2[...] = norm_back(e, n2, i2)
    gf[...] = r2[...].astype(BF16)
    gzd = (nt(gf[...], p9t) * LOWRANK).astype(BF16)
    g9 = tn(z_d, gf[...]) * LOWRANK
    gzu = jnp.zeros((tokens, RANK), F32)
    for r in range(nh):
        gbt[pl.ds(pl.multiple_of(relative[r] * 2 * RANK, 2 * RANK), RANK), :] = tn(gzd, f[r])

        def down(c, carry, r=r):
            cols = pl.ds(pl.multiple_of(c * chunk, chunk), chunk)
            q0 = bt[pl.ds(pl.multiple_of(relative[r] * 2 * RANK, 2 * RANK), RANK), cols]
            df = nt(gf[...], wd[r, cols, :]) + nn(gzd, q0)
            slope[r, :, cols] = (df * slope[r, :, cols].astype(F32)).astype(BF16)
            return carry

        lax.fori_loop(0, model // chunk, down, 0)
        ga = slope[r]
        gzu = gzu + nt(ga, inner(1, r))
        gbt[pl.ds(pl.multiple_of(relative[r] * 2 * RANK, 2 * RANK) + RANK, RANK), :] = (
            tn(z_up, ga) * LOWRANK
        )
        term = nt(ga, wu[r])
        if r == 0:
            acc[...] = r2[...] + term
        else:
            acc[...] += term
    gzu = (gzu * LOWRANK).astype(BF16)
    g4 = tn(gzu, h1b[...])
    e = (acc[...] + nn(gzu, p4t)) * gains[0:1]
    r1 = norm_back(e, n1[...], i1[...])
    first[...] = r1.reshape(first.shape)
    gat[...] = r1.astype(BF16)
    gzo = (nt(gat[...], p8t) * LOWRANK).astype(BF16)
    g8 = tn(z_o, gat[...]) * LOWRANK
    g3 = tn(gzo, ocat[...])
    for r, go in enumerate((go0, go1, go2, go3)):
        rows = slice(r * width, (r + 1) * width)
        go[...] = (nt(gat[...], wo[rows]) + nn(gzo, p3t[:, rows])).astype(BF16).reshape(go.shape)
    zeros = jnp.zeros((4 * RANK, model), F32)
    grad_a[...] = jnp.concatenate([g3, g4, g8, g9, zeros], axis=0).T
    for r in range(nh):
        rows = pl.ds(pl.multiple_of(relative[r] * width, width), width)
        grad_a[rows, 0:RANK] = g3[:, r * width : (r + 1) * width].T
    grad_b[...] = gbt[...].T


def token_side(o_all, hidden, gout, wo, wu, wd, tile_a, bt, shifts, gains, up_bias):
    pairs, part, model = gout.shape
    tokens = pairs * part
    nh = o_all.shape[0]
    width = wo[0].shape[0]
    shape = jax.ShapeDtypeStruct
    return pl.pallas_call(
        functools.partial(token_kernel, nh),
        out_shape=[
            shape((pairs, part, model), BF16),
            shape((pairs, part, model), F32),
            *[shape((pairs, part, width), BF16)] * nh,
            shape((model, LANES), F32),
            shape((model, LANES), F32),
        ],
        in_specs=[vmem(), anywhere(), vmem(), vmem(), vmem()] + [anywhere()] * 4 + [vmem()] * 5,
        out_specs=[vmem()] * (4 + nh),
        scratch_shapes=[
            pltpu.VMEM((pairs, part, model), BF16),
            pltpu.VMEM((model, model), BF16),
            pltpu.VMEM((tokens, model), BF16),
            pltpu.VMEM((nh, model, model), BF16),
            pltpu.VMEM((nh, model, model), BF16),
            pltpu.VMEM((nh, tokens, model), BF16),
            pltpu.VMEM((nh, tokens, model), BF16),
            pltpu.VMEM((tokens, model), F32),
            pltpu.VMEM((tokens, model), F32),
            pltpu.VMEM((tokens, 1), F32),
            pltpu.VMEM((tokens, model), BF16),
            pltpu.VMEM((tokens, model), F32),
            pltpu.VMEM((tokens, model), BF16),
            pltpu.VMEM((tokens, model), F32),
            pltpu.VMEM((tokens, model), BF16),
            pltpu.VMEM((LANES, model), F32),
            pltpu.SemaphoreType.DMA,
            pltpu.SemaphoreType.DMA((2, nh)),
        ],
        compiler_params=pltpu.CompilerParams(vmem_limit_bytes=60 << 20),
        name="token_side",
    )(o_all, hidden, gout, *wo, *wu, *wd, tile_a, bt, shifts, gains, up_bias)


def attend_back_kernel(
    nh, x_ref, proj_ref, p_ref, inv_ref, go0, go1, go2, go3, wt, down_t,
    part0, part1, part2, part3, grad_out, got, gproj, grad_t,
):
    step = pl.program_id(0)
    h = lax.axis_index("head")
    relative = [jnp.bitwise_xor(h, r) for r in range(nh)]
    width = go0.shape[2]
    part = go0.shape[1]
    model = x_ref.shape[2]
    own_rows = pl.ds(pl.multiple_of(h * width, width), width)

    @pl.when(step == 0)
    def _():
        grad_t[...] = jnp.zeros_like(grad_t)

    for r, go in enumerate((go0, go1, go2, go3)):
        got[:, pl.ds(pl.multiple_of(relative[r] * part, part), part)] = go[0].T
    scale = jnp.asarray(DH ** (-0.5), BF16)
    for head in range(width // DH):
        part_h = slice(head * DH, (head + 1) * DH)
        rows_k = slice(width + head * DH, width + (head + 1) * DH)
        rows_v = slice(2 * width + head * DH, 2 * width + (head + 1) * DH)
        inverse = inv_ref[0, head : head + 1]
        qt = proj_ref[0, part_h] * scale
        kt = proj_ref[0, rows_k] * scale
        vt = proj_ref[0, rows_v]
        gs = (got[part_h].astype(F32) * inverse).astype(BF16)
        et = p_ref[0, head]
        ef = et.astype(F32)
        dpt = tn(vt, gs)
        delta = jnp.sum(ef * dpt, axis=0, keepdims=True) * inverse
        gst = (ef * (dpt - delta)).astype(BF16)
        gproj[part_h] = nn(kt, gst).astype(BF16)
        gproj[rows_k] = nt(qt, gst).astype(BF16)
        gproj[rows_v] = nt(gs, et).astype(BF16)
    inner = []
    for j in range(3):
        block = gproj[j * width : (j + 1) * width]
        ut = proj_ref[0, 3 * width + j * RANK : 3 * width + (j + 1) * RANK]
        grad_t[(3 + j) * RANK : (4 + j) * RANK, 0:width] += nt(ut, block) * LOWRANK
        inner.append(nn(down_t[(3 + j) * RANK : (4 + j) * RANK], block) * LOWRANK)
    inner = jnp.concatenate(inner, axis=0).astype(BF16)
    grad_t[0 : 3 * RANK] += nn(inner, x_ref[0])
    whole = tn(gproj[...], wt[0 : 3 * width])
    got_rows = whole.astype(BF16)
    parts = (part0, part1, part2, part3)
    for r in range(nh):
        for block in range(nh):

            @pl.when(relative[r] == block)
            def _(r=r, block=block):
                parts[r][0] = got_rows[block * part : (block + 1) * part]

    @pl.when(step == pl.num_programs(0) - 1)
    def _():
        full = grad_t[...].T
        lane = lax.broadcasted_iota(jnp.int32, full.shape, 1)
        grad_out[...] = jnp.where(lane < 3 * RANK, full, 0.0)
        rows = full[0:width]
        lane = lax.broadcasted_iota(jnp.int32, rows.shape, 1)
        grad_out[own_rows, :] = jnp.where(
            lane < 3 * RANK, grad_out[own_rows, :], rows
        )


def attend_back(hidden, proj, p, inverse, go, wt, down_t):
    count, keys, model = hidden.shape
    nh = len(go)
    part, width = go[0].shape[1:]
    heads = width // DH
    tall = 3 * width + 3 * RANK
    shape = jax.ShapeDtypeStruct
    return pl.pallas_call(
        functools.partial(attend_back_kernel, nh),
        grid=(count,),
        in_specs=[
            pl.BlockSpec((1, keys, model), lambda s: (s, 0, 0)),
            pl.BlockSpec((1, tall, keys), lambda s: (s, 0, 0)),
            pl.BlockSpec((1, heads, keys, keys), lambda s: (s, 0, 0, 0)),
            pl.BlockSpec((1, heads, keys), lambda s: (s, 0, 0)),
            *[pl.BlockSpec((1, part, width), lambda s: (s, 0, 0))] * nh,
            vmem(), vmem(),
        ],
        out_specs=[
            *[pl.BlockSpec((1, part, model), lambda s: (s, 0, 0))] * nh,
            vmem(),
        ],
        out_shape=[
            *[shape((count, part, model), BF16)] * nh,
            shape((model, LANES), F32),
        ],
        scratch_shapes=[
            pltpu.VMEM((width, keys), BF16),
            pltpu.VMEM((3 * width, keys), BF16),
            pltpu.VMEM((LANES, model), F32),
        ],
        compiler_params=pltpu.CompilerParams(vmem_limit_bytes=48 << 20),
        name="attend_back",
    )(hidden, proj, p, inverse, *go, wt, down_t)


def optimizer_kernel(
    nh, g_ref, stats_m, stats_i, stats_r, roots_m, roots_i, roots_r,
    grad_m, grad_i, step_m, step_i, new_m, new_i, new_r, squares, gt,
):
    owner = lax.axis_index("dp") * nh + lax.axis_index("head")
    count, rows, model = stats_m.shape
    rows_i = stats_i.shape[1]
    for t in range(3):
        gt[t] = g_ref[t].T
    own = [g_ref[t, pl.ds(owner * rows, rows), :] for t in range(2)]

    def finish(m, u, where, j):
        u = nn(u, roots_r[m], HIGH)
        where[j] = u
        squares[m : m + 1] = jnp.broadcast_to(
            jnp.sum(jnp.sum(u * u, axis=0, keepdims=True), axis=1, keepdims=True), (1, LANES)
        )

    squares[...] = jnp.zeros_like(squares)
    for j in range(count):
        t, m = slot_of(j)
        lanes = slice(m * RANK, (m + 1) * RANK)
        mine = own[t][:, lanes]
        full = gt[t, lanes]
        grad_m[j] = mine
        new_m[j] = DECAY * stats_m[j] + (1.0 - DECAY) * nn(mine, full, HIGH)
        new_r[j] = DECAY * stats_r[j] + (1.0 - DECAY) * nt(full, full, HIGH)
        finish(j, nt(roots_m[j], full, HIGH), step_m, j)
    blocks = stats_i.shape[2] // model
    per = model // rows_i
    block = owner // per
    tall = g_ref[2, pl.ds((owner - block * per) * rows_i, rows_i), :]
    for q in range(2):
        mine = jnp.zeros((rows_i, RANK), F32)
        gram = jnp.zeros((RANK, RANK), F32)
        u = jnp.zeros((rows_i, RANK), F32)
        for k in range(blocks):
            lanes = slice((2 * k + q) * RANK, (2 * k + q + 1) * RANK)
            mine = jnp.where(block == k, tall[:, lanes], mine)
        grad_i[q] = mine
        for k in range(blocks):
            lanes = slice((2 * k + q) * RANK, (2 * k + q + 1) * RANK)
            cols = slice(k * model, (k + 1) * model)
            full = gt[2, lanes]
            gram = gram + nt(full, full, HIGH)
            u = u + nt(roots_i[q, :, cols], full, HIGH)
            new_i[q, :, cols] = DECAY * stats_i[q, :, cols] + (1.0 - DECAY) * nn(
                mine, full, HIGH
            )
        new_r[count + q] = DECAY * stats_r[count + q] + (1.0 - DECAY) * gram
        finish(count + q, u, step_i, q)


def optimizer(g, stats_m, stats_i, stats_r, roots_m, roots_i, roots_r, nh):
    shape = jax.ShapeDtypeStruct
    count, rows, model = stats_m.shape
    rows_i = stats_i.shape[1]
    return pl.pallas_call(
        functools.partial(optimizer_kernel, nh),
        in_specs=[vmem()] * 7,
        out_specs=[vmem()] * 8,
        out_shape=[
            shape((count, rows, RANK), F32),
            shape((2, rows_i, RANK), F32),
            shape((count, rows, RANK), F32),
            shape((2, rows_i, RANK), F32),
            shape(stats_m.shape, F32),
            shape(stats_i.shape, F32),
            shape(stats_r.shape, F32),
            shape((16, LANES), F32),
        ],
        scratch_shapes=[pltpu.VMEM((3, LANES, model), F32)],
        compiler_params=pltpu.CompilerParams(vmem_limit_bytes=48 << 20),
        name="optimizer",
    )(g, stats_m, stats_i, stats_r, roots_m, roots_i, roots_r)


def local(
    nd,
    nh,
    hidden_input,
    grad_out,
    pair_lengths,
    query_key_value_weight,
    qkv_bias,
    output_projection_weight,
    shifts,
    gains,
    up_projection_weight,
    up_bias,
    down_projection_weight,
    adapters_model,
    adapters_inner,
    stats_model,
    stats_inner,
    stats_rank,
    roots_model,
    roots_inner,
    roots_rank,
):
    owners = nd * nh
    count, rows, _ = adapters_model.shape
    rows_i = adapters_inner.shape[1]
    model = hidden_input.shape[2]
    split = rows_i // rows
    padded = -(-rows // 8) * 8

    def swap(values, r):
        return lax.ppermute(values, "head", [(i, i ^ r) for i in range(nh)])

    proj, p, inverse, o_all, wo_rest, wu_rest, wd_rest, wt, tile_a, bt, down_t = attend(
        nd, nh, hidden_input, pair_lengths,
        jnp.swapaxes(adapters_model, 1, 2), jnp.swapaxes(adapters_inner, 1, 2),
        jnp.swapaxes(query_key_value_weight, 1, 2), qkv_bias,
        output_projection_weight, up_projection_weight, down_projection_weight,
    )
    out = token_side(
        o_all, hidden_input, grad_out,
        (output_projection_weight, wo_rest), (up_projection_weight, wu_rest),
        (down_projection_weight, wd_rest), tile_a, bt, shifts, gains, up_bias.reshape(nh, model),
    )
    result, first = out[0], out[1]
    go = [out[2]] + [swap(out[2 + r], r) for r in range(1, nh)]
    grad_a, grad_b = out[2 + nh :]
    back = attend_back(hidden_input, proj, p, inverse, go, wt, down_t)
    near = [swap(back[1], 1), swap(back[3], 1)]
    far = (back[2].astype(F32) + near[1].astype(F32)).astype(BF16)
    far = swap(far, 2)
    grad_in = (
        first + back[0].astype(F32) + near[0].astype(F32) + far.astype(F32)
    ).astype(BF16)
    grads = jnp.stack([back[4], grad_a, grad_b]).reshape(3, nd, nh, rows, LANES)
    grads = jnp.pad(grads, ((0, 0),) * 3 + ((0, padded - rows), (0, 0)))
    grads = reduce_all(grads, 2, "reduce_gradients")
    grads = grads[:, :, :, :rows].reshape(3, model, LANES)
    grad_m, grad_i, step_m, step_i, new_m, new_i, new_r, squares = optimizer(
        grads, stats_model, stats_inner, stats_rank, roots_model, roots_inner, roots_rank, nh
    )
    squares = gather_all(squares[None], nd, nh, 3, "gather_squares")
    squares = jnp.sum(squares[0, :, :, :, 0], axis=(0, 1))
    rates_m = jnp.where(jnp.arange(count) < 5, RATE_FIRST, RATE_SECOND)
    rates_i = jnp.where(jnp.arange(2) < 1, RATE_FIRST, RATE_SECOND)
    scale_m = rates_m * lax.rsqrt(squares[:count] / (model * RANK) + 1e-6)
    scale_i = rates_i * lax.rsqrt(
        squares[count : count + 2] / (rows_i * owners * RANK) + 1e-6
    )
    return (
        result,
        grad_in,
        grad_m,
        grad_i,
        adapters_model - scale_m[:, None, None] * step_m,
        adapters_inner - scale_i[:, None, None] * step_i,
        new_m,
        new_i,
        new_r,
    )


def solution(mesh):
    rows = P(None, ("dp", "head"), None)
    in_specs = (
        P("dp", None, None),
        P("dp", "head", None),
        P("dp"),
        P(None, None, "head"),
        P(),
        P("head", None),
        P(),
        P(),
        P(None, "head"),
        P(),
        P("head", None),
        rows, rows, rows, rows,
        P(),
        rows, rows,
        P(),
    )
    out_specs = (
        P("dp", "head", None),
        P("dp", "head", None),
        rows, rows, rows, rows, rows, rows,
        P(),
    )
    body = functools.partial(local, mesh.shape["dp"], mesh.shape["head"])
    return jax.shard_map(body, mesh=mesh, in_specs=in_specs, out_specs=out_specs, check_vma=False)
```

```python
import functools

import jax
import jax.numpy as jnp
from jax import lax
from jax.experimental import pallas as pl
from jax.experimental.pallas import tpu as pltpu
from jax.sharding import PartitionSpec as P

DH = 64
RANK = 16
LANES = 128
LOWRANK = 2.0
RATE_FIRST = 0.01
RATE_SECOND = 0.16
DECAY = 0.5
EPS_NORM = 1e-5
MESH = pl.DeviceIdType.MESH
VMEM_LIMIT = 60 << 20
F32 = jnp.float32
BF16 = jnp.bfloat16
HIGH = lax.Precision.HIGHEST

EARLY_SLOTS = (0, 1, 2, 5, 6, 7)
LATE_SLOTS = (3, 4, 8, 9)


def slot_of(j):
    if j in EARLY_SLOTS:
        return 0, EARLY_SLOTS.index(j)
    return 1, LATE_SLOTS.index(j)


def nn(a, b, precision=None):
    return lax.dot_general(
        a, b, (((1,), (0,)), ((), ())), precision=precision, preferred_element_type=F32
    )


def nt(a, b, precision=None):
    return lax.dot_general(
        a, b, (((1,), (1,)), ((), ())), precision=precision, preferred_element_type=F32
    )


def tn(a, b, precision=None):
    return lax.dot_general(
        a, b, (((0,), (0,)), ((), ())), precision=precision, preferred_element_type=F32
    )


def vmem():
    return pl.BlockSpec(memory_space=pltpu.VMEM)


def anywhere():
    return pl.BlockSpec(memory_space=pl.ANY)


def greet_signal(nd, nh):
    d, h = lax.axis_index("dp"), lax.axis_index("head")
    barrier = pltpu.get_barrier_semaphore()
    for k in range(1, nd):
        pl.semaphore_signal(
            barrier, inc=1, device_id=(lax.rem(d + k, nd), h), device_id_type=MESH
        )
    for k in range(1, nh):
        pl.semaphore_signal(
            barrier, inc=1, device_id=(d, lax.rem(h + k, nh)), device_id_type=MESH
        )


def greet_wait(nd, nh):
    pl.semaphore_wait(pltpu.get_barrier_semaphore(), nd + nh - 2)


def greet(nd, nh):
    greet_signal(nd, nh)
    greet_wait(nd, nh)


def remote(src, dst, send, recv, device):
    return pltpu.make_async_remote_copy(
        src, dst, send, recv, device_id=device, device_id_type=MESH
    )


class Reduction:
    def __init__(self, nd, nh, bufs, sems):
        self.nd, self.nh = nd, nh
        self.out, self.part, self.near, self.full = bufs
        self.sems = sems
        self.d, self.h = lax.axis_index("dp"), lax.axis_index("head")

    @staticmethod
    def scratch(nd, nh, tiles, model):
        rows = -(-(model // nd) // 16) * 16
        dma = pltpu.SemaphoreType.DMA
        return (
            [
                pltpu.VMEM((nd, tiles, rows, LANES), BF16),
                pltpu.VMEM((nd, tiles, rows, LANES), BF16),
                pltpu.VMEM((4, tiles, rows, LANES), BF16),
                pltpu.VMEM((nd, tiles, rows, LANES), BF16),
            ],
            [dma((nd,)), dma((nd,)), dma((2,)), dma((2,)), dma((nd,)), dma((nd,))],
        )

    def to_owner(self, k):
        peer = lax.rem(self.d + k, self.nd)
        return remote(
            self.out.at[peer], self.part.at[k], self.sems[0].at[k], self.sems[1].at[k],
            (peer, self.h),
        )

    def across(self, i):
        return remote(
            self.near.at[2 * i], self.near.at[2 * i + 1], self.sems[2].at[i],
            self.sems[3].at[i], (self.d, jnp.bitwise_xor(self.h, i + 1)),
        )

    def to_all(self, k):
        here = self.full.at[self.d]
        return remote(
            here, here, self.sems[4].at[k], self.sems[5].at[k],
            (lax.rem(self.d + k, self.nd), self.h),
        )

    def start(self, values):
        size = values.shape[1] // self.nd
        for i in range(self.nd):
            self.out[i, :, 0:size] = values[:, i * size : (i + 1) * size].astype(BF16)
        for k in range(1, self.nd):
            self.to_owner(k).start()

    def over_dp(self):
        total = self.out[self.d].astype(F32)
        for k in range(1, self.nd):
            self.to_owner(k).wait_recv()
            total = total + self.part[k].astype(F32)
        self.near[0] = total.astype(BF16)
        self.across(0).start()

    def over_head(self, i):
        self.across(i).wait_recv()
        total = self.near[2 * i].astype(F32) + self.near[2 * i + 1].astype(F32)
        if i == 0:
            self.near[2] = total.astype(BF16)
            self.across(1).start()
        else:
            self.full[self.d] = total.astype(BF16)
            for k in range(1, self.nd):
                self.to_all(k).start()

    def finish(self, target):
        size = target.shape[1] // self.nd
        for k in range(1, self.nd):
            self.to_all(k).wait_recv()
        for i in range(self.nd):
            target[:, i * size : (i + 1) * size] = self.full[i, :, 0:size].astype(F32)
        for k in range(1, self.nd):
            self.to_owner(k).wait_send()
            self.to_all(k).wait_send()
        for i in range(2):
            self.across(i).wait_send()


def attend_kernel(
    nd, nh, lengths, am, ai, x_hbm, w_ref, bias_ref, wo, wu, wd,
    proj_ref, p_ref, inv_ref, o_all, go_w, gu_w, gd_w, wt, tile_a, bt, down_t,
    packed, first_tile, other_tiles, obuf, bias_col, unpack, x_ref, raw, up_t, pt,
    load_x,
    send_d, recv_d, send_h, recv_h, send_o, recv_o, keep_o, send_w, recv_w, send_s, recv_s,
):
    step = pl.program_id(0)
    d, h = lax.axis_index("dp"), lax.axis_index("head")
    count, keys, model = x_ref.shape
    part = keys // nh
    width = w_ref.shape[1]
    rows = am.shape[2]
    split = ai.shape[2] // rows
    owners = nd * nh
    quarter = lax.rem(d, 4)

    def at(a, b):
        return (jnp.bitwise_xor(d, a), jnp.bitwise_xor(h, b))

    own_w = (wo, wu, wd)
    all_w = (go_w, gu_w, gd_w)
    chunks = []
    for w in range(3):
        quarter_rows = own_w[w].shape[0] // 4
        pieces = 1 if w == 0 else 2
        for piece in range(pieces):
            chunks.append((w, quarter_rows, piece * quarter_rows // pieces, quarter_rows // pieces))

    def region(ref, c, who, half=None):
        w, quarter_rows, offset, size = chunks[c]
        base = jnp.bitwise_xor(quarter, who) * quarter_rows + offset
        if half is not None:
            first = -(-(size // 2) // 16) * 16
            base, size = (base, first) if half == 0 else (base + first, size - first)
        return ref.at[pl.ds(pl.multiple_of(base, 16), size)]

    def over_x(c):
        w = chunks[c][0]
        return remote(
            region(own_w[w], c, 0), region(all_w[w].at[1], c, 0),
            send_w.at[0, c], recv_w.at[0, c], at(0, 2),
        )

    def spread_w(c, axis):
        here = region(all_w[chunks[c][0]].at[1], c, 0)
        return remote(here, here, send_w.at[axis, c], recv_w.at[axis, c], at(axis, 0))

    def relay_w(c, axis):
        here = region(all_w[chunks[c][0]].at[1], c, 3 - axis, axis - 1)
        return remote(here, here, send_w.at[2 + axis, c], recv_w.at[2 + axis, c], at(axis, 0))

    def sibling_own(w):
        return remote(own_w[w], all_w[w].at[0], send_s.at[0, w], recv_s.at[0, w], at(0, 1))

    def sibling_far(w):
        return remote(
            all_w[w].at[1], all_w[w].at[2], send_s.at[1, w], recv_s.at[1, w], at(0, 1)
        )

    def forward(c):
        over_x(c).wait_recv()
        spread_w(c, 2).start()
        spread_w(c, 1).start()

    def relay(c):
        spread_w(c, 2).wait_recv()
        relay_w(c, 1).start()
        spread_w(c, 1).wait_recv()
        relay_w(c, 2).start()

    def arrived(c):
        relay_w(c, 1).wait_recv()
        relay_w(c, 2).wait_recv()

    def finish(w, which):
        for c in which:
            arrived(c)
        sibling_far(w).start()

    stores = (first_tile, other_tiles)
    sources = (packed.at[pl.ds(0, 1)], packed.at[pl.ds(1, 2)])
    critical, later = 0, 1

    def to_dp(k, slot):
        return remote(
            sources[slot], stores[slot].at[h, d], send_d.at[slot, k], recv_d.at[slot, k],
            (lax.rem(d + k, nd), h),
        )

    def to_head(b, slot):
        column = stores[slot].at[h]
        return remote(column, column, send_h.at[slot, b], recv_h.at[slot, b], at(0, b))

    def pass_on(slot):
        column = stores[slot].at[jnp.bitwise_xor(h, 2)]
        return remote(column, column, send_h.at[slot, 3], recv_h.at[slot, 3], at(0, 1))

    def entry(t, owner):
        if t == 0:
            return first_tile[owner % nh, owner // nh, 0, 0:rows]
        return other_tiles[owner % nh, owner // nh, t - 1, 0:rows]

    def natural(t):
        return jnp.concatenate([entry(t, i) for i in range(owners)], axis=0)

    def fetch_x(i):
        return pltpu.make_async_copy(x_hbm.at[i], x_ref.at[i], load_x.at[i])

    def project(i):
        fetch_x(i).wait()
        for j in range(3):
            raw[i, j * width : (j + 1) * width] = nt(w_ref[j], x_ref[i])

    @pl.when(step == 0)
    def _():
        for i in range(count):
            fetch_x(i).start()
        greet_signal(nd, nh)
        packed[...] = jnp.zeros_like(packed)
        groups = [
            [am[j] for j in EARLY_SLOTS],
            [am[j] for j in LATE_SLOTS],
            [ai[q][:, k * rows : (k + 1) * rows] for k in range(split) for q in range(2)],
        ]
        for t, group in enumerate(groups):
            short = LANES - len(group) * RANK
            if short:
                group = group + [jnp.zeros((short, rows), F32)]
            packed[t, 0:rows] = jnp.concatenate(group, axis=0).T.astype(BF16).astype(F32)
        first_tile[h, d] = packed[0:1]
        other_tiles[h, d] = packed[1:3]
        project(0)
        greet_wait(nd, nh)
        for k in range(1, nd):
            to_dp(k, critical).start()
        over_x(0).start()
        over_x(1).start()
        project(1)
        project(2)
        for k in range(1, nd):
            to_dp(k, critical).wait_recv()
        to_head(2, critical).start()
        to_head(1, critical).start()
        for c in range(2, len(chunks)):
            over_x(c).start()
        project(3)
        to_head(2, critical).wait_recv()
        pass_on(critical).start()
        sibling_own(0).start()
        sibling_own(1).start()
        sibling_own(2).start()
        project(4)
        bias_col[...] = jnp.concatenate(
            [bias_ref[...], jnp.zeros((5, model), F32)], axis=0
        ).T
        to_head(1, critical).wait_recv()
        pass_on(critical).wait_recv()
        pn = natural(0)
        pt[...] = pn.T.astype(BF16)
        tile_a[...] = pn
        own = tile_a[pl.ds(pl.multiple_of(h * width, width), width), :]
        down_t[...] = own.T.astype(BF16)
        own = own[:, 3 * RANK : 6 * RANK].astype(BF16)
        lane = lax.broadcasted_iota(jnp.int32, own.shape, 1)
        for j in range(3):
            inside = (lane >= j * RANK) & (lane < (j + 1) * RANK)
            up_t[j * width : (j + 1) * width] = jnp.where(inside, own, jnp.zeros_like(own))
        for k in range(1, nd):
            to_dp(k, later).start()

    inner = nt(pt[0 : 3 * RANK], x_ref[step]).astype(BF16)
    proj_ref[0, 3 * width :] = inner
    mine = pl.ds(pl.multiple_of(h * width, width), width)
    for j in range(3):
        part_j = slice(j * width, (j + 1) * width)
        proj_ref[0, part_j] = (
            raw[step, part_j] + LOWRANK * nn(up_t[part_j], inner) + bias_col[mine, j : j + 1]
        ).astype(BF16)
    valid = lax.broadcasted_iota(jnp.int32, (keys, 1), 0) < lengths[step]

    def slot(s, place):
        for action in plan.get((s, place), ()):
            action()

    def slots(place):
        for s in range(count):
            if (s, place) in plan:
                pl.when(step == s)(functools.partial(slot, s, place))

    def later_to_head():
        for k in range(1, nd):
            to_dp(k, later).wait_recv()
        to_head(2, later).start()
        to_head(1, later).start()

    def later_pass_on():
        to_head(2, later).wait_recv()
        pass_on(later).start()

    bind = functools.partial
    plan = {
        (0, 0): [bind(forward, 0)],
        (0, 1): [bind(forward, 1)],
        (1, 1): [bind(forward, 2), bind(relay, 0)],
        (1, 3): [later_to_head, bind(relay, 1)],
        (2, 1): [bind(forward, 3)],
        (2, 3): [bind(forward, 4), bind(relay, 2)],
        (3, 1): [bind(relay, 3), bind(finish, 0, (0,))],
        (3, 3): [later_pass_on, bind(relay, 4)],
        (4, 1): [bind(finish, 1, (1, 2))],
    }

    results = []
    for head in range(width // DH):
        slots(head)
        rows_q = slice(head * DH, (head + 1) * DH)
        qt = proj_ref[0, rows_q] * jnp.asarray(DH ** (-0.5), BF16)
        kt = proj_ref[0, width + head * DH : width + (head + 1) * DH]
        vt = proj_ref[0, 2 * width + head * DH : 2 * width + (head + 1) * DH]
        st = jnp.where(valid, tn(kt, qt), -1e30)
        top = jnp.max(st, axis=0, keepdims=True)
        et = jnp.exp(st - top)
        inverse = 1.0 / jnp.sum(et, axis=0, keepdims=True)
        low = et.astype(BF16)
        p_ref[0, head] = low
        inv_ref[0, head : head + 1] = inverse
        results.append(nn(vt, low) * inverse)
    obuf[step] = jnp.concatenate(results, axis=0).astype(BF16)

    def block_of(s, r):
        start = jnp.bitwise_xor(h, r) * part
        return obuf.at[s, :, pl.ds(pl.multiple_of(start, part), part)]

    def place_of(s, r):
        start = jnp.bitwise_xor(h, r) * width
        column = pl.ds(pl.multiple_of(s * part, part), part)
        return o_all.at[pl.ds(pl.multiple_of(start, width), width), column]

    def send_block(r, s):
        return remote(
            block_of(s, r), place_of(s, 0), send_o.at[r, s], recv_o.at[r, s], at(0, r)
        )

    def arrive_block(r, s):
        return remote(
            block_of(s, r), place_of(s, r), send_o.at[r, s], recv_o.at[r, s], at(0, r)
        )

    def keep_block(s):
        return pltpu.make_async_copy(block_of(s, 0), place_of(s, 0), keep_o.at[s])

    for r in (2, 3, 1):
        send_block(r, step).start()
    keep_block(step).start()

    slots(3)

    @pl.when(step == count - 1)
    def _():
        wt[3 * width :] = pt[0 : 3 * RANK]
        for j in range(3):
            part_j = slice(j * width, (j + 1) * width)
            delta = nn(up_t[part_j], pt[0 : 3 * RANK])
            wt[part_j] = (w_ref[j].astype(F32) + LOWRANK * delta).astype(BF16)
        to_head(1, later).wait_recv()
        pass_on(later).wait_recv()
        tile_a[...] = natural(1)
        per = owners // split
        for w in range(per):
            for k in range(split):
                blocks = [
                    entry(2, b * per + w)[:, 2 * RANK * k : 2 * RANK * (k + 1)]
                    for b in range(split)
                ]
                base = (w * split + k) * rows
                unpack[base : base + rows] = jnp.concatenate(blocks, axis=1)
        bt[...] = unpack[...].T.astype(BF16)
        finish(2, (3, 4))
        for c in range(len(chunks)):
            over_x(c).wait_send()
            for axis in (1, 2):
                spread_w(c, axis).wait_send()
                relay_w(c, axis).wait_send()
        for slot in (critical, later):
            for k in range(1, nd):
                to_dp(k, slot).wait_send()
            for b in (1, 2):
                to_head(b, slot).wait_send()
            pass_on(slot).wait_send()
        for s in range(count):
            keep_block(s).wait()
            for r in range(1, nh):
                send_block(r, s).wait_send()
                arrive_block(r, s).wait_recv()
        for w in range(3):
            sibling_own(w).wait()
            sibling_far(w).wait()


def attend(nd, nh, hidden, lengths, adapters_m, adapters_i, weight, bias, wo, wu, wd):
    count, keys, model = hidden.shape
    width = weight.shape[1]
    heads = width // DH
    tall = 3 * width + 3 * RANK
    part = keys // nh
    rows = adapters_m.shape[2]
    padded = -(-rows // 8) * 8
    shape = jax.ShapeDtypeStruct
    dma = pltpu.SemaphoreType.DMA
    return pl.pallas_call(
        functools.partial(attend_kernel, nd, nh),
        grid=(count,),
        in_specs=[
            pl.BlockSpec(memory_space=pltpu.SMEM),
            vmem(), vmem(), anywhere(), vmem(), vmem(), anywhere(), anywhere(), anywhere(),
        ],
        out_specs=[
            pl.BlockSpec((1, tall, keys), lambda s: (s, 0, 0)),
            pl.BlockSpec((1, heads, keys, keys), lambda s: (s, 0, 0, 0)),
            pl.BlockSpec((1, heads, keys), lambda s: (s, 0, 0)),
            anywhere(), anywhere(), anywhere(), anywhere(),
            vmem(), vmem(), vmem(), vmem(),
        ],
        out_shape=[
            shape((count, tall, keys), BF16),
            shape((count, heads, keys, keys), BF16),
            shape((count, heads, keys), F32),
            shape((nh * width, count * part), BF16),
            *[shape((nh - 1, *w.shape), BF16) for w in (wo, wu, wd)],
            shape((tall, model), BF16),
            shape((model, LANES), F32),
            shape((LANES, model), BF16),
            shape((LANES, width), BF16),
        ],
        scratch_shapes=[
            pltpu.VMEM((3, padded, LANES), F32),
            pltpu.VMEM((nh, nd, 1, padded, LANES), F32),
            pltpu.VMEM((nh, nd, 2, padded, LANES), F32),
            pltpu.VMEM((count, width, keys), BF16),
            pltpu.VMEM((model, 8), F32),
            pltpu.VMEM((model, LANES), F32),
            pltpu.VMEM((count, keys, model), BF16),
            pltpu.VMEM((count, 3 * width, keys), F32),
            pltpu.VMEM((3 * width, 3 * RANK), BF16),
            pltpu.VMEM((LANES, model), BF16),
            dma((count,)),
            dma((2, nd)), dma((2, nd)), dma((2, 4)), dma((2, 4)),
            dma((nh, count)), dma((nh, count)), dma((count,)),
            dma((5, 5)), dma((5, 5)), dma((2, 3)), dma((2, 3)),
        ],
        compiler_params=pltpu.CompilerParams(
            collective_id=1, has_side_effects=True, vmem_limit_bytes=VMEM_LIMIT
        ),
        name="attend",
    )(lengths, adapters_m, adapters_i, hidden, weight, bias, wo, wu, wd)


def tail_density(a):
    e = jnp.exp(-0.5 * a * a)
    t = 1.0 / (1.0 + (0.3275911 * 0.7071067811865476) * jnp.abs(a))
    poly = 1.061405429 * t - 1.453152027
    poly = poly * t + 1.421413741
    poly = poly * t - 0.284496736
    poly = poly * t + 0.254829592
    q = (0.5 * poly * t) * e
    return jnp.where(a >= 0, 1.0 - q, q), e * 0.3989422804014327


def centred(v):
    c = v - jnp.mean(v, axis=-1, keepdims=True)
    inverse = lax.rsqrt(jnp.mean(c * c, axis=-1, keepdims=True) + EPS_NORM)
    return c * inverse, inverse


def norm_back(e, n, inverse):
    return inverse * (
        e - jnp.mean(e, axis=-1, keepdims=True) - n * jnp.mean(e * n, axis=-1, keepdims=True)
    )


def token_kernel(
    nh, o_all, x_hbm, gout, wo_own, wo_rest, wu_own, wu_rest, wd_own, wd_rest,
    tile_a, bt, shifts, gains, up_bias,
    result, first, go, grads,
    x, wo, ocat, wu, wd, f, slope, h1, n1, i1, h1b, r2, gf, acc, gat, gbt, sem_x, sem_w,
):
    h = lax.axis_index("head")
    pairs, part, model = x.shape
    tokens = pairs * part
    width = wo_own.shape[0]
    relative = [jnp.bitwise_xor(h, r) for r in range(nh)]
    own = pltpu.make_async_copy(
        x_hbm.at[:, pl.ds(pl.multiple_of(h * part, part), part), :], x, sem_x
    )
    own.start()
    fetch = []
    for r in range(nh):
        a = wu_own if r == 0 else wu_rest.at[r - 1]
        b = wd_own if r == 0 else wd_rest.at[r - 1]
        fetch.append(
            (
                pltpu.make_async_copy(a, wu.at[r], sem_w.at[0, r]),
                pltpu.make_async_copy(b, wd.at[r], sem_w.at[1, r]),
            )
        )
    for r in range(nh):
        fetch[r][0].start()
    for r in range(nh):
        fetch[r][1].start()
    ocat[...] = o_all[...].T
    for r in range(nh):
        rows = pl.ds(pl.multiple_of(relative[r] * width, width), width)
        wo[rows] = wo_own[...] if r == 0 else wo_rest[r - 1]
    at = tile_a[...].T.astype(BF16)
    p3t, p4t, p8t, p9t = (at[m * RANK : (m + 1) * RANK] for m in range(4))
    p3 = tile_a[:, 0:RANK].astype(BF16)

    def inner(q, r):
        return bt[pl.ds(pl.multiple_of(relative[r] * 2 * RANK, 2 * RANK) + q * RANK, RANK), :]

    z_o = nt(ocat[...], p3t).astype(BF16)
    acc[...] = nn(ocat[...], wo[...]) + nn(z_o, p8t) * LOWRANK
    own.wait()
    v = x[...].reshape(tokens, model).astype(F32) + acc[...] + shifts[0:1]
    n, inv = centred(v)
    n1[...] = n
    i1[...] = inv
    h1[...] = n * gains[0:1] + shifts[1:2]
    h1b[...] = h1[...].astype(BF16)
    z_up = nt(h1b[...], p4t).astype(BF16)
    chunk = 256
    z_d = jnp.zeros((tokens, RANK), F32)
    for r in range(nh):
        fetch[r][0].wait()

        def up(c, carry, r=r):
            cols = pl.ds(pl.multiple_of(c * chunk, chunk), chunk)
            q1 = bt[
                pl.ds(pl.multiple_of(relative[r] * 2 * RANK, 2 * RANK) + RANK, RANK), cols
            ]
            a = (
                nn(h1b[...], wu[r, :, cols])
                + nn(z_up, q1) * LOWRANK
                + up_bias[pl.ds(relative[r], 1), cols]
            )
            cdf, density = tail_density(a)
            f[r, :, cols] = (a * cdf).astype(BF16)
            slope[r, :, cols] = (cdf + a * density).astype(BF16)
            return carry

        lax.fori_loop(0, model // chunk, up, 0)
        z_d = z_d + nt(f[r], inner(0, r))
    z_d = z_d.astype(BF16)
    for r in range(nh):
        fetch[r][1].wait()
        term = nn(f[r], wd[r])
        if r == 0:
            acc[...] = term + nn(z_d, p9t) * LOWRANK
        else:
            acc[...] += term
    n2, i2 = centred(h1[...] + acc[...] + shifts[2:3])
    result[...] = (n2 * gains[1:2] + shifts[3:4]).astype(BF16).reshape(result.shape)
    e = gout[...].reshape(tokens, model).astype(F32) * gains[1:2]
    r2[...] = norm_back(e, n2, i2)
    gf[...] = r2[...].astype(BF16)
    gzd = (nt(gf[...], p9t) * LOWRANK).astype(BF16)
    g9 = tn(z_d, gf[...]) * LOWRANK
    gzu = jnp.zeros((tokens, RANK), F32)
    for r in range(nh):
        gbt[pl.ds(pl.multiple_of(relative[r] * 2 * RANK, 2 * RANK), RANK), :] = tn(gzd, f[r])

        def down(c, carry, r=r):
            cols = pl.ds(pl.multiple_of(c * chunk, chunk), chunk)
            q0 = bt[pl.ds(pl.multiple_of(relative[r] * 2 * RANK, 2 * RANK), RANK), cols]
            df = nt(gf[...], wd[r, cols, :]) + nn(gzd, q0)
            slope[r, :, cols] = (df * slope[r, :, cols].astype(F32)).astype(BF16)
            return carry

        lax.fori_loop(0, model // chunk, down, 0)
        ga = slope[r]
        gzu = gzu + nt(ga, inner(1, r))
        gbt[pl.ds(pl.multiple_of(relative[r] * 2 * RANK, 2 * RANK) + RANK, RANK), :] = (
            tn(z_up, ga) * LOWRANK
        )
        term = nt(ga, wu[r])
        if r == 0:
            acc[...] = r2[...] + term
        else:
            acc[...] += term
    gzu = (gzu * LOWRANK).astype(BF16)
    g4 = tn(gzu, h1b[...])
    e = (acc[...] + nn(gzu, p4t)) * gains[0:1]
    r1 = norm_back(e, n1[...], i1[...])
    first[...] = r1.reshape(first.shape)
    gat[...] = r1.astype(BF16)
    gzo = (nt(gat[...], p8t) * LOWRANK).astype(BF16)
    g8 = tn(z_o, gat[...]) * LOWRANK
    g3 = tn(gzo, ocat[...])
    go[...] = (nt(wo[...], gat[...]) + nt(p3, gzo)).astype(BF16)
    zeros = jnp.zeros((4 * RANK, model), F32)
    grads[0] = jnp.concatenate([g3, g4, g8, g9, zeros], axis=0).T
    grads[1] = gbt[...].T


def token_side(o_all, hidden, gout, wo, wu, wd, tile_a, bt, shifts, gains, up_bias):
    pairs, part, model = gout.shape
    tokens = pairs * part
    width = wo[0].shape[0]
    nh = model // width
    shape = jax.ShapeDtypeStruct
    return pl.pallas_call(
        functools.partial(token_kernel, nh),
        out_shape=[
            shape((pairs, part, model), BF16),
            shape((pairs, part, model), F32),
            shape((model, tokens), BF16),
            shape((2, model, LANES), F32),
        ],
        in_specs=[vmem(), anywhere(), vmem(), vmem(), vmem()] + [anywhere()] * 4 + [vmem()] * 5,
        out_specs=[vmem()] * 4,
        scratch_shapes=[
            pltpu.VMEM((pairs, part, model), BF16),
            pltpu.VMEM((model, model), BF16),
            pltpu.VMEM((tokens, model), BF16),
            pltpu.VMEM((nh, model, model), BF16),
            pltpu.VMEM((nh, model, model), BF16),
            pltpu.VMEM((nh, tokens, model), BF16),
            pltpu.VMEM((nh, tokens, model), BF16),
            pltpu.VMEM((tokens, model), F32),
            pltpu.VMEM((tokens, model), F32),
            pltpu.VMEM((tokens, 1), F32),
            pltpu.VMEM((tokens, model), BF16),
            pltpu.VMEM((tokens, model), F32),
            pltpu.VMEM((tokens, model), BF16),
            pltpu.VMEM((tokens, model), F32),
            pltpu.VMEM((tokens, model), BF16),
            pltpu.VMEM((LANES, model), F32),
            pltpu.SemaphoreType.DMA,
            pltpu.SemaphoreType.DMA((2, nh)),
        ],
        compiler_params=pltpu.CompilerParams(vmem_limit_bytes=VMEM_LIMIT),
        name="token_side",
    )(o_all, hidden, gout, *wo, *wu, *wd, tile_a, bt, shifts, gains, up_bias)


def attend_back_kernel(
    nd, nh, x_ref, proj_ref, p_ref, inv_ref, go, first, early, wt, down_t,
    roots_m, roots_i, roots_r,
    grad_in, gradients, step_m, step_i, squares,
    got_all, gproj, grad_t, late, whole_buf, near, far, last, blocks, mixed, sq, sq_head, sq_dp,
    send_g, recv_g, keep_g, send_n, recv_n, send_f, recv_f,
    send_a, recv_a, send_b, recv_b, *rest,
):
    step = pl.program_id(0)
    d, h = lax.axis_index("dp"), lax.axis_index("head")
    relative = [jnp.bitwise_xor(h, r) for r in range(nh)]
    count, part, model = first.shape
    width = got_all.shape[1]
    own_rows = pl.ds(pl.multiple_of(h * width, width), width)
    one = Reduction(nd, nh, rest[0:4], rest[8:14])
    two = Reduction(nd, nh, rest[4:8], rest[14:20])

    def at(b):
        return (d, jnp.bitwise_xor(h, b))

    def block_of(r, s):
        return go.at[
            pl.ds(pl.multiple_of(relative[r] * width, width), width),
            pl.ds(pl.multiple_of(s * part, part), part),
        ]

    def place_of(r, s):
        return got_all.at[s, :, pl.ds(pl.multiple_of(relative[r] * part, part), part)]

    def bring(r, s):
        return remote(
            block_of(r, s), place_of(0, s), send_g.at[r, s], recv_g.at[r, s], at(r)
        )

    def brought(r, s):
        return remote(
            block_of(r, s), place_of(r, s), send_g.at[r, s], recv_g.at[r, s], at(r)
        )

    def keep(s):
        return pltpu.make_async_copy(block_of(0, s), place_of(0, s), keep_g.at[s])

    def to_near(i, s):
        return remote(
            whole_buf.at[s, relative[1 + 2 * i]], near.at[s, i], send_n.at[i, s],
            recv_n.at[i, s], at(1),
        )

    def to_far(s):
        return remote(far.at[s], last.at[s], send_f.at[s], recv_f.at[s], at(2))

    def pass_far(s):
        to_near(1, s).wait_recv()
        far[s] = (whole_buf[s, relative[2]].astype(F32) + near[s, 1].astype(F32)).astype(BF16)
        to_far(s).start()

    def complete(s):
        to_near(0, s).wait_recv()
        to_far(s).wait_recv()
        grad_in[s] = (
            first[s]
            + whole_buf[s, h].astype(F32)
            + near[s, 0].astype(F32)
            + last[s].astype(F32)
        ).astype(BF16)

    @pl.when(step == 0)
    def _():
        greet_signal(nd, nh)
        for s in range(count):
            keep(s).start()
        grad_t[...] = jnp.zeros_like(grad_t)
        greet_wait(nd, nh)
        for s in range(count):
            for r in (2, 3, 1):
                bring(r, s).start()
        two.start(early[...])

    keep(step).wait()
    for r in range(1, nh):
        brought(r, step).wait_recv()
    got = got_all.at[step]
    scale = jnp.asarray(DH ** (-0.5), BF16)
    for head in range(width // DH):
        part_h = slice(head * DH, (head + 1) * DH)
        rows_k = slice(width + head * DH, width + (head + 1) * DH)
        rows_v = slice(2 * width + head * DH, 2 * width + (head + 1) * DH)
        inverse = inv_ref[0, head : head + 1]
        qt = proj_ref[0, part_h] * scale
        kt = proj_ref[0, rows_k] * scale
        vt = proj_ref[0, rows_v]
        gs = (got[part_h].astype(F32) * inverse).astype(BF16)
        et = p_ref[0, head]
        ef = et.astype(F32)
        dpt = tn(vt, gs)
        delta = jnp.sum(ef * dpt, axis=0, keepdims=True) * inverse
        gst = (ef * (dpt - delta)).astype(BF16)
        gproj[part_h] = nn(kt, gst).astype(BF16)
        gproj[rows_k] = nt(qt, gst).astype(BF16)
        gproj[rows_v] = nt(gs, et).astype(BF16)
        if head == 1:

            @pl.when(step >= 1)
            def _():
                pass_far(jnp.maximum(step - 1, 0))

    inner = []
    for j in range(3):
        block = gproj[j * width : (j + 1) * width]
        ut = proj_ref[0, 3 * width + j * RANK : 3 * width + (j + 1) * RANK]
        grad_t[(3 + j) * RANK : (4 + j) * RANK, 0:width] += nt(ut, block) * LOWRANK
        inner.append(nn(down_t[(3 + j) * RANK : (4 + j) * RANK], block) * LOWRANK)
    inner = jnp.concatenate(inner, axis=0).astype(BF16)
    grad_t[0 : 3 * RANK] += nn(inner, x_ref[0])
    whole_buf[step] = tn(gproj[...], wt[0 : 3 * width]).astype(BF16).reshape(nh, part, model)
    to_near(1, step).start()
    to_near(0, step).start()

    @pl.when(step == 1)
    def _():
        two.over_dp()

    @pl.when(step == 2)
    def _():
        two.over_head(0)

    @pl.when(step == 3)
    def _():
        two.over_head(1)

    def preconditioned(j, u, where, i):
        where[i] = u
        sq[j : j + 1] = jnp.broadcast_to(
            jnp.sum(jnp.sum(u * u, axis=0, keepdims=True), axis=1, keepdims=True), (1, LANES)
        )

    def mix(t):
        mixed[t] = tn(blocks[t], gradients[t].T, HIGH).astype(BF16)

    def steps_model(t):
        for j in range(roots_m.shape[0]):
            tile, m = slot_of(j)
            if tile == t:
                g = mixed[t, m * RANK : (m + 1) * RANK]
                preconditioned(j, nt(g, roots_m[j].astype(BF16)), step_m, j)

    @pl.when(step == count - 1)
    def _():
        full = grad_t[...].T
        lane = lax.broadcasted_iota(jnp.int32, full.shape, 1)
        late[0] = jnp.where(lane < 3 * RANK, full, 0.0)
        rows = full[0:width]
        lane = lax.broadcasted_iota(jnp.int32, rows.shape, 1)
        late[0, own_rows, :] = jnp.where(lane < 3 * RANK, late[0, own_rows, :], rows)
        one.start(late[...])
        pass_far(count - 1)
        blocks[...] = jnp.zeros_like(blocks)
        sq[...] = jnp.zeros_like(sq)
        for j in range(roots_m.shape[0]):
            t, m = slot_of(j)
            blocks[t, m * RANK : (m + 1) * RANK, m * RANK : (m + 1) * RANK] = roots_r[j]
        split = roots_i.shape[2] // model
        for k in range(split):
            for q in range(2):
                m = 2 * k + q
                blocks[2, m * RANK : (m + 1) * RANK, m * RANK : (m + 1) * RANK] = roots_r[
                    roots_m.shape[0] + q
                ]
        two.finish(gradients.at[1:3])
        one.over_dp()
        mix(1)
        mix(2)
        for q in range(2):
            u = jnp.zeros((RANK, roots_i.shape[1]), F32)
            for k in range(split):
                m = 2 * k + q
                u = u + nt(
                    mixed[2, m * RANK : (m + 1) * RANK],
                    roots_i[q, :, k * model : (k + 1) * model].astype(BF16),
                )
            preconditioned(roots_m.shape[0] + q, u, step_i, q)
        one.over_head(0)
        steps_model(1)
        one.over_head(1)
        for s in range(count):
            complete(s)
        one.finish(gradients.at[0:1])
        mix(0)
        steps_model(0)

        def sq_over_head(k):
            return remote(
                sq, sq_head.at[k], send_a.at[k], recv_a.at[k], (d, lax.rem(h + k, nh))
            )

        def sq_over_dp(k):
            return remote(
                sq_dp.at[0], sq_dp.at[k], send_b.at[k], recv_b.at[k], (lax.rem(d + k, nd), h)
            )

        for k in range(1, nh):
            sq_over_head(k).start()
        total = sq[...]
        for k in range(1, nh):
            sq_over_head(k).wait_recv()
            total = total + sq_head[k]
        sq_dp[0] = total
        for k in range(1, nd):
            sq_over_dp(k).start()
        for k in range(1, nd):
            sq_over_dp(k).wait_recv()
            total = total + sq_dp[k]
        squares[...] = total
        for k in range(1, nh):
            sq_over_head(k).wait_send()
        for k in range(1, nd):
            sq_over_dp(k).wait_send()
        for s in range(count):
            to_far(s).wait_send()
            for i in range(2):
                to_near(i, s).wait_send()
            for r in range(1, nh):
                bring(r, s).wait_send()


def attend_back(
    nd, nh, hidden, proj, p, inverse, go, first, early, wt, down_t, roots_m, roots_i, roots_r
):
    count, keys, model = hidden.shape
    part, width = first.shape[1], model // nh
    heads = width // DH
    tall = 3 * width + 3 * RANK
    shape = jax.ShapeDtypeStruct
    dma = pltpu.SemaphoreType.DMA
    bufs_one, sems_one = Reduction.scratch(nd, nh, 1, model)
    bufs_two, sems_two = Reduction.scratch(nd, nh, 2, model)
    return pl.pallas_call(
        functools.partial(attend_back_kernel, nd, nh),
        grid=(count,),
        in_specs=[
            pl.BlockSpec((1, keys, model), lambda s: (s, 0, 0)),
            pl.BlockSpec((1, tall, keys), lambda s: (s, 0, 0)),
            pl.BlockSpec((1, heads, keys, keys), lambda s: (s, 0, 0, 0)),
            pl.BlockSpec((1, heads, keys), lambda s: (s, 0, 0)),
            anywhere(),
            *[vmem()] * 7,
        ],
        out_specs=[vmem()] * 5,
        out_shape=[
            shape((count, part, model), BF16),
            shape((3, model, LANES), F32),
            shape((roots_m.shape[0], RANK, roots_m.shape[1]), F32),
            shape((2, RANK, roots_i.shape[1]), F32),
            shape((16, LANES), F32),
        ],
        scratch_shapes=[
            pltpu.VMEM((count, width, keys), BF16),
            pltpu.VMEM((3 * width, keys), BF16),
            pltpu.VMEM((LANES, model), F32),
            pltpu.VMEM((1, model, LANES), F32),
            pltpu.VMEM((count, nh, part, model), BF16),
            pltpu.VMEM((count, 2, part, model), BF16),
            pltpu.VMEM((count, part, model), BF16),
            pltpu.VMEM((count, part, model), BF16),
            pltpu.VMEM((3, LANES, LANES), F32),
            pltpu.VMEM((3, LANES, model), BF16),
            pltpu.VMEM((16, LANES), F32),
            pltpu.VMEM((nh, 16, LANES), F32),
            pltpu.VMEM((nd, 16, LANES), F32),
            dma((nh, count)), dma((nh, count)), dma((count,)),
            dma((2, count)), dma((2, count)), dma((count,)), dma((count,)),
            dma((nh,)), dma((nh,)), dma((nd,)), dma((nd,)),
            *bufs_one, *bufs_two, *sems_one, *sems_two,
        ],
        compiler_params=pltpu.CompilerParams(
            collective_id=2, has_side_effects=True, vmem_limit_bytes=VMEM_LIMIT
        ),
        name="attend_back",
    )(hidden, proj, p, inverse, go, first, early, wt, down_t, roots_m, roots_i, roots_r)


def finish_kernel(
    nh, owners, grad_in, g_ref, stats_m, stats_i, stats_r, am, ai, step_m, step_i, squares,
    grad_out, grad_m, grad_i, adapt_m, adapt_i, new_m, new_i, new_r, gt,
):
    grad_out[...] = grad_in[...]
    owner = lax.axis_index("dp") * nh + lax.axis_index("head")
    count, rows, model = stats_m.shape
    rows_i = stats_i.shape[1]
    for t in range(3):
        gt[t] = g_ref[t].T.astype(BF16)
    own = [g_ref[t, pl.ds(owner * rows, rows), :] for t in range(2)]
    turned = [v.T for v in own]

    def update(j, old, u, rate):
        size = model if j < count else rows_i * owners
        mean = squares[j : j + 1, 0:1] * (1.0 / (size * RANK))
        return old - rate * lax.rsqrt(mean + 1e-6) * u

    for j in range(count):
        t, m = slot_of(j)
        lanes = slice(m * RANK, (m + 1) * RANK)
        full = gt[t, lanes]
        grad_m[j] = turned[t][lanes]
        new_m[j] = DECAY * stats_m[j] + (1.0 - DECAY) * nn(own[t][:, lanes].astype(BF16), full)
        new_r[j] = DECAY * stats_r[j] + (1.0 - DECAY) * nt(full, full)
        adapt_m[j] = update(j, am[j], step_m[j], RATE_FIRST if j < 5 else RATE_SECOND)
    blocks = stats_i.shape[2] // model
    per = model // rows_i
    block = owner // per
    tall = g_ref[2, pl.ds((owner - block * per) * rows_i, rows_i), :]
    tall_t = tall.T
    for q in range(2):
        mine = jnp.zeros((rows_i, RANK), F32)
        mine_t = jnp.zeros((RANK, rows_i), F32)
        gram = jnp.zeros((RANK, RANK), F32)
        for k in range(blocks):
            lanes = slice((2 * k + q) * RANK, (2 * k + q + 1) * RANK)
            mine = jnp.where(block == k, tall[:, lanes], mine)
            mine_t = jnp.where(block == k, tall_t[lanes], mine_t)
        grad_i[q] = mine_t
        mine = mine.astype(BF16)
        for k in range(blocks):
            lanes = slice((2 * k + q) * RANK, (2 * k + q + 1) * RANK)
            cols = slice(k * model, (k + 1) * model)
            full = gt[2, lanes]
            gram = gram + nt(full, full)
            new_i[q, :, cols] = DECAY * stats_i[q, :, cols] + (1.0 - DECAY) * nn(mine, full)
        new_r[count + q] = DECAY * stats_r[count + q] + (1.0 - DECAY) * gram
        adapt_i[q] = update(count + q, ai[q], step_i[q], RATE_FIRST if q < 1 else RATE_SECOND)


def finish(nd, nh, grad_in, g, stats_m, stats_i, stats_r, am, ai, step_m, step_i, squares):
    shape = jax.ShapeDtypeStruct
    model = stats_m.shape[2]
    return pl.pallas_call(
        functools.partial(finish_kernel, nh, nd * nh),
        in_specs=[vmem()] * 10,
        out_specs=[vmem()] * 8,
        out_shape=[
            shape(grad_in.shape, BF16),
            shape(am.shape, F32),
            shape(ai.shape, F32),
            shape(am.shape, F32),
            shape(ai.shape, F32),
            shape(stats_m.shape, F32),
            shape(stats_i.shape, F32),
            shape(stats_r.shape, F32),
        ],
        scratch_shapes=[pltpu.VMEM((3, LANES, model), BF16)],
        compiler_params=pltpu.CompilerParams(vmem_limit_bytes=VMEM_LIMIT),
        name="finish",
    )(grad_in, g, stats_m, stats_i, stats_r, am, ai, step_m, step_i, squares)


def local(
    nd,
    nh,
    hidden_input,
    grad_out,
    pair_lengths,
    query_key_value_weight,
    qkv_bias,
    output_projection_weight,
    shifts,
    gains,
    up_projection_weight,
    up_bias,
    down_projection_weight,
    adapters_model,
    adapters_inner,
    stats_model,
    stats_inner,
    stats_rank,
    roots_model,
    roots_inner,
    roots_rank,
):
    model = hidden_input.shape[2]
    turned_m = jnp.swapaxes(adapters_model, 1, 2)
    turned_i = jnp.swapaxes(adapters_inner, 1, 2)
    proj, p, inverse, o_all, wo_rest, wu_rest, wd_rest, wt, tile_a, bt, down_t = attend(
        nd, nh, hidden_input, pair_lengths, turned_m, turned_i,
        jnp.swapaxes(query_key_value_weight, 1, 2), qkv_bias,
        output_projection_weight, up_projection_weight, down_projection_weight,
    )
    result, first, go, early = token_side(
        o_all, hidden_input, grad_out,
        (output_projection_weight, wo_rest), (up_projection_weight, wu_rest),
        (down_projection_weight, wd_rest), tile_a, bt, shifts, gains, up_bias.reshape(nh, model),
    )
    grad_in, gradients, step_m, step_i, squares = attend_back(
        nd, nh, hidden_input, proj, p, inverse, go, first, early, wt, down_t,
        roots_model, roots_inner, roots_rank,
    )
    grad_in, grad_m, grad_i, adapt_m, adapt_i, new_m, new_i, new_r = finish(
        nd, nh, grad_in, gradients, stats_model, stats_inner, stats_rank, turned_m, turned_i,
        step_m, step_i, squares,
    )
    grad_m, grad_i, adapt_m, adapt_i = (
        jnp.swapaxes(v, 1, 2) for v in (grad_m, grad_i, adapt_m, adapt_i)
    )
    return (result, grad_in, grad_m, grad_i, adapt_m, adapt_i, new_m, new_i, new_r)


def solution(mesh):
    rows = P(None, ("dp", "head"), None)
    in_specs = (
        P("dp", None, None),
        P("dp", "head", None),
        P("dp"),
        P(None, None, "head"),
        P(),
        P("head", None),
        P(),
        P(),
        P(None, "head"),
        P(),
        P("head", None),
        rows, rows, rows, rows,
        P(),
        rows, rows,
        P(),
    )
    out_specs = (
        P("dp", "head", None),
        P("dp", "head", None),
        rows, rows, rows, rows, rows, rows,
        P(),
    )
    body = functools.partial(local, mesh.shape["dp"], mesh.shape["head"])
    return jax.shard_map(body, mesh=mesh, in_specs=in_specs, out_specs=out_specs, check_vma=False)
```

```python
import functools

import jax
import jax.numpy as jnp
from jax import lax
from jax.experimental import pallas as pl
from jax.experimental.pallas import tpu as pltpu
from jax.sharding import PartitionSpec as P

DH = 64
RANK = 16
LANES = 128
LOWRANK = 2.0
RATE_FIRST = 0.01
RATE_SECOND = 0.16
DECAY = 0.5
EPS_NORM = 1e-5
MESH = pl.DeviceIdType.MESH
VMEM_LIMIT = 60 << 20
F32 = jnp.float32
BF16 = jnp.bfloat16
HIGH = lax.Precision.HIGHEST

EARLY_SLOTS = (0, 1, 2, 5, 6, 7)
LATE_SLOTS = (3, 4, 8, 9)


def slot_of(j):
    if j in EARLY_SLOTS:
        return 0, EARLY_SLOTS.index(j)
    return 1, LATE_SLOTS.index(j)


def nn(a, b, precision=None):
    return lax.dot_general(
        a, b, (((1,), (0,)), ((), ())), precision=precision, preferred_element_type=F32
    )


def nt(a, b, precision=None):
    return lax.dot_general(
        a, b, (((1,), (1,)), ((), ())), precision=precision, preferred_element_type=F32
    )


def tn(a, b, precision=None):
    return lax.dot_general(
        a, b, (((0,), (0,)), ((), ())), precision=precision, preferred_element_type=F32
    )


def vmem():
    return pl.BlockSpec(memory_space=pltpu.VMEM)


def anywhere():
    return pl.BlockSpec(memory_space=pl.ANY)


def greet_signal(nd, nh):
    d, h = lax.axis_index("dp"), lax.axis_index("head")
    barrier = pltpu.get_barrier_semaphore()
    for k in range(1, nd):
        pl.semaphore_signal(
            barrier, inc=1, device_id=(lax.rem(d + k, nd), h), device_id_type=MESH
        )
    for k in range(1, nh):
        pl.semaphore_signal(
            barrier, inc=1, device_id=(d, lax.rem(h + k, nh)), device_id_type=MESH
        )


def greet_wait(nd, nh):
    pl.semaphore_wait(pltpu.get_barrier_semaphore(), nd + nh - 2)


def greet(nd, nh):
    greet_signal(nd, nh)
    greet_wait(nd, nh)


def remote(src, dst, send, recv, device):
    return pltpu.make_async_remote_copy(
        src, dst, send, recv, device_id=device, device_id_type=MESH
    )


class Reduction:
    def __init__(self, nd, nh, bufs, sems):
        self.nd, self.nh = nd, nh
        self.out, self.part, self.near, self.full = bufs
        self.sems = sems
        self.d, self.h = lax.axis_index("dp"), lax.axis_index("head")

    @staticmethod
    def scratch(nd, nh, tiles, model):
        rows = -(-(model // nd) // 16) * 16
        dma = pltpu.SemaphoreType.DMA
        return (
            [
                pltpu.VMEM((nd, tiles, rows, LANES), BF16),
                pltpu.VMEM((nd, tiles, rows, LANES), BF16),
                pltpu.VMEM((4, tiles, rows, LANES), BF16),
                pltpu.VMEM((nd, tiles, rows, LANES), BF16),
            ],
            [dma((nd,)), dma((nd,)), dma((2,)), dma((2,)), dma((nd,)), dma((nd,))],
        )

    def to_owner(self, k):
        peer = lax.rem(self.d + k, self.nd)
        return remote(
            self.out.at[peer], self.part.at[k], self.sems[0].at[k], self.sems[1].at[k],
            (peer, self.h),
        )

    def across(self, i):
        return remote(
            self.near.at[2 * i], self.near.at[2 * i + 1], self.sems[2].at[i],
            self.sems[3].at[i], (self.d, jnp.bitwise_xor(self.h, i + 1)),
        )

    def to_all(self, k):
        here = self.full.at[self.d]
        return remote(
            here, here, self.sems[4].at[k], self.sems[5].at[k],
            (lax.rem(self.d + k, self.nd), self.h),
        )

    def start(self, values):
        size = values.shape[1] // self.nd
        for i in range(self.nd):
            self.out[i, :, 0:size] = values[:, i * size : (i + 1) * size].astype(BF16)
        for k in range(1, self.nd):
            self.to_owner(k).start()

    def over_dp(self):
        total = self.out[self.d].astype(F32)
        for k in range(1, self.nd):
            self.to_owner(k).wait_recv()
            total = total + self.part[k].astype(F32)
        self.near[0] = total.astype(BF16)
        self.across(0).start()

    def over_head(self, i):
        self.across(i).wait_recv()
        total = self.near[2 * i].astype(F32) + self.near[2 * i + 1].astype(F32)
        if i == 0:
            self.near[2] = total.astype(BF16)
            self.across(1).start()
        else:
            self.full[self.d] = total.astype(BF16)
            for k in range(1, self.nd):
                self.to_all(k).start()

    def finish(self, target):
        size = target.shape[1] // self.nd
        for k in range(1, self.nd):
            self.to_all(k).wait_recv()
        for i in range(self.nd):
            target[:, i * size : (i + 1) * size] = self.full[i, :, 0:size].astype(F32)
        for k in range(1, self.nd):
            self.to_owner(k).wait_send()
            self.to_all(k).wait_send()
        for i in range(2):
            self.across(i).wait_send()


def cdf_and_density(a):
    cdf = 0.5 * (1.0 + lax.erf(a * 0.7071067811865476))
    return cdf, jnp.exp(-0.5 * a * a) * 0.3989422804014327


def centred(v):
    c = v - jnp.mean(v, axis=-1, keepdims=True)
    inverse = lax.rsqrt(jnp.mean(c * c, axis=-1, keepdims=True) + EPS_NORM)
    return c * inverse, inverse


def norm_back(e, n, inverse):
    return inverse * (
        e - jnp.mean(e, axis=-1, keepdims=True) - n * jnp.mean(e * n, axis=-1, keepdims=True)
    )


def forward_kernel(
    nd, nh, lengths, am, ai, x_ref, x_hbm, w_ref, bias_ref, wo_own, wu_own, wd_own,
    gout, shifts, gains, up_bias,
    proj_ref, p_ref, inv_ref, wt, down_t, result_out, gat_out, go_out, grads_out,
    packed, first_tile, other_tiles, obuf, bias_col, unpack, tile_a, bt,
    o_all, wo, wu, wd, x, ocat, f, slope, h1, n1, i1, h1b, r2, gf, acc, gat, gbt, result, go, grads,
    send_d, recv_d, send_h, recv_h, send_o, recv_o, keep_o, send_w, recv_w, send_s, recv_s,
    load, store,
):
    step = pl.program_id(0)
    last = pl.num_programs(0) - 1
    d, h = lax.axis_index("dp"), lax.axis_index("head")
    count, part, model = x.shape
    tokens = count * part
    width = w_ref.shape[1]
    keys = x_ref.shape[1]
    rows = am.shape[2]
    split = ai.shape[2] // rows
    owners = nd * nh
    quarter = lax.rem(d, 4)
    relative = [jnp.bitwise_xor(h, r) for r in range(nh)]

    def at(a, b):
        return (jnp.bitwise_xor(d, a), jnp.bitwise_xor(h, b))

    def window(start, size):
        return pl.ds(pl.multiple_of(start * size, size), size)

    own_w = (wo_own, wu_own, wd_own)

    def piece(w, source, slot):
        if w == 0:
            return wo.at[window(relative[source], width)]
        return (wu, wd)[w - 1].at[slot]

    chunks = []
    for w in range(3):
        quarter_rows = own_w[w].shape[0] // 4
        pieces = 1 if w == 0 else 2
        for n in range(pieces):
            chunks.append((w, quarter_rows, n * quarter_rows // pieces, quarter_rows // pieces))

    def region(ref, c, who, half=None):
        w, quarter_rows, offset, size = chunks[c]
        base = jnp.bitwise_xor(quarter, who) * quarter_rows + offset
        if half is not None:
            first = -(-(size // 2) // 16) * 16
            base, size = (base, first) if half == 0 else (base + first, size - first)
        return ref.at[pl.ds(pl.multiple_of(base, 16), size)]

    def over_x(c):
        w = chunks[c][0]
        return remote(
            region(own_w[w], c, 0), region(piece(w, 0, 2), c, 0),
            send_w.at[0, c], recv_w.at[0, c], at(0, 2),
        )

    def over_x_here(c):
        w = chunks[c][0]
        return remote(
            region(own_w[w], c, 0), region(piece(w, 2, 2), c, 0),
            send_w.at[0, c], recv_w.at[0, c], at(0, 2),
        )

    def spread_w(c, axis):
        here = region(piece(chunks[c][0], 2, 2), c, 0)
        return remote(here, here, send_w.at[axis, c], recv_w.at[axis, c], at(axis, 0))

    def relay_w(c, axis):
        here = region(piece(chunks[c][0], 2, 2), c, 3 - axis, axis - 1)
        return remote(here, here, send_w.at[2 + axis, c], recv_w.at[2 + axis, c], at(axis, 0))

    def sibling_own(w):
        return remote(
            own_w[w], piece(w, 0, 1), send_s.at[0, w], recv_s.at[0, w], at(0, 1)
        )

    def sibling_far(w):
        return remote(
            piece(w, 2, 2), piece(w, 2, 3), send_s.at[1, w], recv_s.at[1, w], at(0, 1)
        )

    def keep_w(w):
        return pltpu.make_async_copy(own_w[w], piece(w, 0, 0), load.at[w])

    def forward(c):
        over_x_here(c).wait_recv()
        spread_w(c, 2).start()
        spread_w(c, 1).start()

    def relay(c):
        spread_w(c, 2).wait_recv()
        relay_w(c, 1).start()
        spread_w(c, 1).wait_recv()
        relay_w(c, 2).start()

    def finish(w, which):
        for c in which:
            relay_w(c, 1).wait_recv()
            relay_w(c, 2).wait_recv()
        sibling_far(w).start()

    stores = (first_tile, other_tiles)
    sources = (packed.at[pl.ds(0, 1)], packed.at[pl.ds(1, 2)])
    critical, later = 0, 1

    def to_dp(k, slot):
        return remote(
            sources[slot], stores[slot].at[h, d], send_d.at[slot, k], recv_d.at[slot, k],
            (lax.rem(d + k, nd), h),
        )

    def to_head(b, slot):
        column = stores[slot].at[h]
        return remote(column, column, send_h.at[slot, b], recv_h.at[slot, b], at(0, b))

    def pass_on(slot):
        column = stores[slot].at[jnp.bitwise_xor(h, 2)]
        return remote(column, column, send_h.at[slot, 3], recv_h.at[slot, 3], at(0, 1))

    def entry(t, owner):
        if t == 0:
            return first_tile[owner % nh, owner // nh, 0, 0:rows]
        return other_tiles[owner % nh, owner // nh, t - 1, 0:rows]

    def natural(t):
        return jnp.concatenate([entry(t, i) for i in range(owners)], axis=0)

    def later_to_head():
        for k in range(1, nd):
            to_dp(k, later).wait_recv()
        to_head(2, later).start()
        to_head(1, later).start()

    def later_pass_on():
        to_head(2, later).wait_recv()
        pass_on(later).start()

    def own_rows():
        return pltpu.make_async_copy(x_hbm.at[:, window(h, part), :], x, load.at[3])

    @pl.when(step == 0)
    def _():
        greet_signal(nd, nh)
        packed[...] = jnp.zeros_like(packed)
        groups = [
            [am[j] for j in EARLY_SLOTS],
            [am[j] for j in LATE_SLOTS],
            [ai[q][:, k * rows : (k + 1) * rows] for k in range(split) for q in range(2)],
        ]
        for t, group in enumerate(groups):
            short = LANES - len(group) * RANK
            if short:
                group = group + [jnp.zeros((short, rows), F32)]
            packed[t, 0:rows] = jnp.concatenate(group, axis=0).T.astype(BF16).astype(F32)
        first_tile[h, d] = packed[0:1]
        other_tiles[h, d] = packed[1:3]
        greet_wait(nd, nh)
        for k in range(1, nd):
            to_dp(k, critical).start()
        over_x(0).start()
        over_x(1).start()
        bias_col[...] = jnp.concatenate(
            [bias_ref[...], jnp.zeros((5, model), F32)], axis=0
        ).T
        for k in range(1, nd):
            to_dp(k, critical).wait_recv()
        to_head(2, critical).start()
        to_head(1, critical).start()
        for c in range(2, len(chunks)):
            over_x(c).start()
        for w in range(3):
            sibling_own(w).start()
            keep_w(w).start()
        own_rows().start()
        to_head(2, critical).wait_recv()
        pass_on(critical).start()
        to_head(1, critical).wait_recv()
        pass_on(critical).wait_recv()
        pn = natural(0)
        pt = pn.T.astype(BF16)
        tile_a[...] = pn
        own = tile_a[window(h, width), :]
        down_t[...] = own.T.astype(BF16)
        own = own.astype(BF16)
        wt[3 * width :] = pt[0 : 3 * RANK]
        for j in range(3):
            delta = nn(own[:, (3 + j) * RANK : (4 + j) * RANK], pt[j * RANK : (j + 1) * RANK])
            wt[j * width : (j + 1) * width] = (w_ref[j].astype(F32) + LOWRANK * delta).astype(
                BF16
            )
        for k in range(1, nd):
            to_dp(k, later).start()

    proj = nt(wt[...], x_ref[0])
    mine = window(h, width)
    for j in range(3):
        proj_ref[0, j * width : (j + 1) * width] = (
            proj[j * width : (j + 1) * width] + bias_col[mine, j : j + 1]
        ).astype(BF16)
    proj_ref[0, 3 * width :] = proj[3 * width :].astype(BF16)
    valid = lax.broadcasted_iota(jnp.int32, (keys, 1), 0) < lengths[step]

    bind = functools.partial
    plan = {
        (0, 0): [bind(forward, 0)],
        (0, 1): [bind(forward, 1)],
        (1, 1): [bind(forward, 2), bind(relay, 0)],
        (1, 3): [later_to_head, bind(relay, 1)],
        (2, 1): [bind(finish, 0, (0,))],
        (2, 3): [bind(forward, 3), bind(relay, 2)],
        (3, 1): [later_pass_on],
        (3, 3): [bind(finish, 1, (1, 2)), bind(forward, 4)],
        (4, 1): [bind(relay, 3)],
    }

    def slots(place):
        for s in range(count):
            if (s, place) in plan:

                @pl.when(step == s)
                def _(s=s):
                    for action in plan[s, place]:
                        action()

    results = []
    for head in range(width // DH):
        slots(head)
        rows_q = slice(head * DH, (head + 1) * DH)
        qt = proj_ref[0, rows_q] * jnp.asarray(DH ** (-0.5), BF16)
        kt = proj_ref[0, width + head * DH : width + (head + 1) * DH]
        vt = proj_ref[0, 2 * width + head * DH : 2 * width + (head + 1) * DH]
        st = jnp.where(valid, tn(kt, qt), -1e30)
        top = jnp.max(st, axis=0, keepdims=True)
        et = jnp.exp(st - top)
        inverse = 1.0 / jnp.sum(et, axis=0, keepdims=True)
        low = et.astype(BF16)
        p_ref[0, head] = low
        inv_ref[0, head : head + 1] = inverse
        results.append(nn(vt, low) * inverse)
    obuf[step] = jnp.concatenate(results, axis=0).astype(BF16)

    def block_of(s, r):
        return obuf.at[s, :, window(relative[r], part)]

    def place_of(s, r):
        return o_all.at[window(relative[r], width), window(s, part)]

    def send_block(r, s):
        return remote(
            block_of(s, r), place_of(s, 0), send_o.at[r, s], recv_o.at[r, s], at(0, r)
        )

    def arrive_block(r, s):
        return remote(
            block_of(s, r), place_of(s, r), send_o.at[r, s], recv_o.at[r, s], at(0, r)
        )

    def keep_block(s):
        return pltpu.make_async_copy(block_of(s, 0), place_of(s, 0), keep_o.at[s])

    for r in (2, 3, 1):
        send_block(r, step).start()
    keep_block(step).start()
    slots(3)

    @pl.when(step == last)
    def _():
        to_head(1, later).wait_recv()
        pass_on(later).wait_recv()
        tile_a[...] = natural(1)
        per = owners // split
        for w in range(per):
            for k in range(split):
                blocks = [
                    entry(2, b * per + w)[:, 2 * RANK * k : 2 * RANK * (k + 1)]
                    for b in range(split)
                ]
                base = (w * split + k) * rows
                unpack[base : base + rows] = jnp.concatenate(blocks, axis=1)
        bt[...] = unpack[...].T.astype(BF16)
        ta = tile_a[...].T.astype(BF16)
        p3t, p4t, p8t, p9t = (ta[m * RANK : (m + 1) * RANK] for m in range(4))
        p3 = tile_a[:, 0:RANK].astype(BF16)

        def inner_at(q, r):
            start = pl.multiple_of(relative[r] * 2 * RANK, 2 * RANK) + q * RANK
            return pl.ds(start, RANK)

        for w in range(3):
            keep_w(w).wait()
        own_rows().wait()
        for w in range(3):
            sibling_own(w).wait_recv()
        sibling_far(0).wait_recv()

        def project(first, pairs):
            tokens_here = slice(first * part, (first + pairs) * part)
            for s in range(first, first + pairs):
                keep_block(s).wait()
                for r in range(1, nh):
                    arrive_block(r, s).wait_recv()
            ocat[tokens_here] = o_all[:, tokens_here].T
            z = nt(ocat[tokens_here], p3t).astype(BF16)
            v = (
                x[first : first + pairs].reshape(pairs * part, model).astype(F32)
                + nn(ocat[tokens_here], wo[...])
                + nn(z, p8t) * LOWRANK
                + shifts[0:1]
            )
            n, inv = centred(v)
            n1[tokens_here] = n
            i1[tokens_here] = inv
            h1[tokens_here] = n * gains[0:1] + shifts[1:2]
            h1b[tokens_here] = h1[tokens_here].astype(BF16)
            return z

        z_o = jnp.concatenate([project(0, count - 1), project(count - 1, 1)], axis=0)
        relay(4)
        z_up = nt(h1b[...], p4t).astype(BF16)
        chunk = 256
        z_d = jnp.zeros((tokens, RANK), F32)
        for r in range(nh):
            if r == 2:
                finish(2, (3, 4))
            if r == 3:
                sibling_far(1).wait_recv()

            def up(c, carry, r=r):
                cols = window(c, chunk)
                q1 = bt[inner_at(1, r), cols] * jnp.asarray(LOWRANK, BF16)
                bias_at = pl.ds(
                    pl.multiple_of(relative[r] * model + c * chunk, chunk), chunk
                )
                a = nn(h1b[...], wu[r, :, cols]) + nn(z_up, q1) + up_bias[0:1, bias_at]
                cdf, density = cdf_and_density(a)
                f[r, :, cols] = (a * cdf).astype(BF16)
                slope[r, :, cols] = (cdf + a * density).astype(BF16)
                return carry

            lax.fori_loop(0, model // chunk, up, 0)
            z_d = z_d + nt(f[r], bt[inner_at(0, r), :])
        z_d = z_d.astype(BF16)
        for r in range(nh):
            if r == 3:
                sibling_far(2).wait_recv()
            term = nn(f[r], wd[r])
            if r == 0:
                acc[...] = term + nn(z_d, p9t) * LOWRANK
            else:
                acc[...] += term
        n2, i2 = centred(h1[...] + acc[...] + shifts[2:3])
        result[...] = (n2 * gains[1:2] + shifts[3:4]).astype(BF16).reshape(result.shape)
        give_result = pltpu.make_async_copy(result, result_out, store.at[0])
        give_result.start()
        e = gout[...].reshape(tokens, model).astype(F32) * gains[1:2]
        r2[...] = norm_back(e, n2, i2)
        gf[...] = r2[...].astype(BF16)
        gzd = (nt(gf[...], p9t) * LOWRANK).astype(BF16)
        g9 = tn(z_d, gf[...]) * LOWRANK
        gzu = jnp.zeros((tokens, RANK), F32)
        for r in range(nh):
            gbt[inner_at(0, r), :] = tn(gzd, f[r])

            def down(c, carry, r=r):
                cols = window(c, chunk)
                df = nt(gf[...], wd[r, cols, :]) + nn(gzd, bt[inner_at(0, r), cols])
                slope[r, :, cols] = (df * slope[r, :, cols].astype(F32)).astype(BF16)
                return carry

            lax.fori_loop(0, model // chunk, down, 0)
            ga = slope[r]
            gzu = gzu + nt(ga, bt[inner_at(1, r), :])
            gbt[inner_at(1, r), :] = tn(z_up, ga) * LOWRANK
            term = nt(ga, wu[r])
            if r == 0:
                acc[...] = r2[...] + term
            else:
                acc[...] += term
        gzu = (gzu * LOWRANK).astype(BF16)
        g4 = tn(gzu, h1b[...])
        e = (acc[...] + nn(gzu, p4t)) * gains[0:1]
        gat[...] = norm_back(e, n1[...], i1[...]).astype(BF16)
        give_gat = pltpu.make_async_copy(gat, gat_out, store.at[1])
        give_gat.start()
        gzo = (nt(gat[...], p8t) * LOWRANK).astype(BF16)
        go[...] = (nt(wo[...], gat[...]) + nt(p3, gzo)).astype(BF16)
        give_go = pltpu.make_async_copy(go, go_out, store.at[2])
        give_go.start()
        g8 = tn(z_o, gat[...]) * LOWRANK
        g3 = tn(gzo, ocat[...])
        zeros = jnp.zeros((4 * RANK, model), F32)
        grads[0] = jnp.concatenate([g3, g4, g8, g9, zeros], axis=0).T
        grads[1] = gbt[...].T
        give_grads = pltpu.make_async_copy(grads, grads_out, store.at[3])
        give_grads.start()
        for c in range(len(chunks)):
            over_x(c).wait_send()
            for axis in (1, 2):
                spread_w(c, axis).wait_send()
                relay_w(c, axis).wait_send()
        for slot in (critical, later):
            for k in range(1, nd):
                to_dp(k, slot).wait_send()
            for b in (1, 2):
                to_head(b, slot).wait_send()
            pass_on(slot).wait_send()
        for s in range(count):
            for r in range(1, nh):
                send_block(r, s).wait_send()
        for w in range(3):
            sibling_own(w).wait_send()
            sibling_far(w).wait_send()
        for give in (give_result, give_gat, give_go, give_grads):
            give.wait()


def forward(
    nd, nh, hidden, lengths, adapters_m, adapters_i, weight, bias, wo, wu, wd, gout, shifts,
    gains, up_bias,
):
    count, keys, model = hidden.shape
    width = weight.shape[1]
    heads = width // DH
    tall = 3 * width + 3 * RANK
    part = keys // nh
    tokens = count * part
    rows = adapters_m.shape[2]
    padded = -(-rows // 8) * 8
    shape = jax.ShapeDtypeStruct
    dma = pltpu.SemaphoreType.DMA
    return pl.pallas_call(
        functools.partial(forward_kernel, nd, nh),
        grid=(count,),
        in_specs=[
            pl.BlockSpec(memory_space=pltpu.SMEM),
            vmem(), vmem(),
            pl.BlockSpec((1, keys, model), lambda s: (s, 0, 0)),
            anywhere(), vmem(), vmem(), anywhere(), anywhere(), anywhere(),
            vmem(), vmem(), vmem(), vmem(),
        ],
        out_specs=[
            pl.BlockSpec((1, tall, keys), lambda s: (s, 0, 0)),
            pl.BlockSpec((1, heads, keys, keys), lambda s: (s, 0, 0, 0)),
            pl.BlockSpec((1, heads, keys), lambda s: (s, 0, 0)),
            vmem(), vmem(),
            anywhere(), anywhere(), anywhere(), anywhere(),
        ],
        out_shape=[
            shape((count, tall, keys), BF16),
            shape((count, heads, keys, keys), BF16),
            shape((count, heads, keys), F32),
            shape((tall, model), BF16),
            shape((LANES, width), BF16),
            shape((count, part, model), BF16),
            shape((tokens, model), BF16),
            shape((model, tokens), BF16),
            shape((2, model, LANES), F32),
        ],
        scratch_shapes=[
            pltpu.VMEM((3, padded, LANES), F32),
            pltpu.VMEM((nh, nd, 1, padded, LANES), F32),
            pltpu.VMEM((nh, nd, 2, padded, LANES), F32),
            pltpu.VMEM((count, width, keys), BF16),
            pltpu.VMEM((model, 8), F32),
            pltpu.VMEM((model, LANES), F32),
            pltpu.VMEM((model, LANES), F32),
            pltpu.VMEM((LANES, model), BF16),
            pltpu.VMEM((model, tokens), BF16),
            pltpu.VMEM((model, model), BF16),
            pltpu.VMEM((nh, model, model), BF16),
            pltpu.VMEM((nh, model, model), BF16),
            pltpu.VMEM((count, part, model), BF16),
            pltpu.VMEM((tokens, model), BF16),
            pltpu.VMEM((nh, tokens, model), BF16),
            pltpu.VMEM((nh, tokens, model), BF16),
            pltpu.VMEM((tokens, model), F32),
            pltpu.VMEM((tokens, model), F32),
            pltpu.VMEM((tokens, 1), F32),
            pltpu.VMEM((tokens, model), BF16),
            pltpu.VMEM((tokens, model), F32),
            pltpu.VMEM((tokens, model), BF16),
            pltpu.VMEM((tokens, model), F32),
            pltpu.VMEM((tokens, model), BF16),
            pltpu.VMEM((LANES, model), F32),
            pltpu.VMEM((count, part, model), BF16),
            pltpu.VMEM((model, tokens), BF16),
            pltpu.VMEM((2, model, LANES), F32),
            dma((2, nd)), dma((2, nd)), dma((2, 4)), dma((2, 4)),
            dma((nh, count)), dma((nh, count)), dma((count,)),
            dma((5, 5)), dma((5, 5)), dma((2, 3)), dma((2, 3)),
            dma((4,)), dma((4,)),
        ],
        compiler_params=pltpu.CompilerParams(
            collective_id=1, has_side_effects=True, vmem_limit_bytes=VMEM_LIMIT
        ),
        name="forward",
    )(
        lengths, adapters_m, adapters_i, hidden, hidden, weight, bias, wo, wu, wd, gout, shifts,
        gains, up_bias,
    )


def attend_back_kernel(
    nd, nh, x_ref, proj_ref, p_ref, inv_ref, go, first, early, wt, down_t,
    roots_m, roots_i, roots_r,
    grad_in, gradients, step_m, step_i, squares,
    got_all, gproj, grad_t, late, whole_buf, near, far, last, blocks, mixed, sq, sq_head, sq_dp,
    send_g, recv_g, keep_g, send_n, recv_n, send_f, recv_f,
    send_a, recv_a, send_b, recv_b, *rest,
):
    step = pl.program_id(0)
    d, h = lax.axis_index("dp"), lax.axis_index("head")
    relative = [jnp.bitwise_xor(h, r) for r in range(nh)]
    count, part, model = first.shape
    width = got_all.shape[1]
    own_rows = pl.ds(pl.multiple_of(h * width, width), width)
    one = Reduction(nd, nh, rest[0:4], rest[8:14])
    two = Reduction(nd, nh, rest[4:8], rest[14:20])

    def at(b):
        return (d, jnp.bitwise_xor(h, b))

    def block_of(r, s):
        return go.at[
            pl.ds(pl.multiple_of(relative[r] * width, width), width),
            pl.ds(pl.multiple_of(s * part, part), part),
        ]

    def place_of(r, s):
        return got_all.at[s, :, pl.ds(pl.multiple_of(relative[r] * part, part), part)]

    def bring(r, s):
        return remote(
            block_of(r, s), place_of(0, s), send_g.at[r, s], recv_g.at[r, s], at(r)
        )

    def brought(r, s):
        return remote(
            block_of(r, s), place_of(r, s), send_g.at[r, s], recv_g.at[r, s], at(r)
        )

    def keep(s):
        return pltpu.make_async_copy(block_of(0, s), place_of(0, s), keep_g.at[s])

    def to_near(i, s):
        return remote(
            whole_buf.at[s, relative[1 + 2 * i]], near.at[s, i], send_n.at[i, s],
            recv_n.at[i, s], at(1),
        )

    def to_far(s):
        return remote(far.at[s], last.at[s], send_f.at[s], recv_f.at[s], at(2))

    def pass_far(s):
        to_near(1, s).wait_recv()
        far[s] = (whole_buf[s, relative[2]].astype(F32) + near[s, 1].astype(F32)).astype(BF16)
        to_far(s).start()

    def complete(s):
        to_near(0, s).wait_recv()
        to_far(s).wait_recv()
        grad_in[s] = (
            first[s].astype(F32)
            + whole_buf[s, h].astype(F32)
            + near[s, 0].astype(F32)
            + last[s].astype(F32)
        ).astype(BF16)

    @pl.when(step == 0)
    def _():
        greet_signal(nd, nh)
        for s in range(count):
            keep(s).start()
        grad_t[...] = jnp.zeros_like(grad_t)
        greet_wait(nd, nh)
        for s in range(count):
            for r in (2, 3, 1):
                bring(r, s).start()
        two.start(early[...])

    keep(step).wait()
    for r in range(1, nh):
        brought(r, step).wait_recv()
    got = got_all.at[step]
    scale = jnp.asarray(DH ** (-0.5), BF16)
    for head in range(width // DH):
        part_h = slice(head * DH, (head + 1) * DH)
        rows_k = slice(width + head * DH, width + (head + 1) * DH)
        rows_v = slice(2 * width + head * DH, 2 * width + (head + 1) * DH)
        inverse = inv_ref[0, head : head + 1]
        qt = proj_ref[0, part_h] * scale
        kt = proj_ref[0, rows_k] * scale
        vt = proj_ref[0, rows_v]
        gs = (got[part_h].astype(F32) * inverse).astype(BF16)
        et = p_ref[0, head]
        ef = et.astype(F32)
        dpt = tn(vt, gs)
        delta = jnp.sum(ef * dpt, axis=0, keepdims=True) * inverse
        gst = (ef * (dpt - delta)).astype(BF16)
        gproj[part_h] = nn(kt, gst).astype(BF16)
        gproj[rows_k] = nt(qt, gst).astype(BF16)
        gproj[rows_v] = nt(gs, et).astype(BF16)
        if head == 0:

            @pl.when(step == 2)
            def _():
                two.over_head(0)

        if head == 1:

            @pl.when(step >= 1)
            def _():
                pass_far(jnp.maximum(step - 1, 0))

    inner = []
    for j in range(3):
        block = gproj[j * width : (j + 1) * width]
        ut = proj_ref[0, 3 * width + j * RANK : 3 * width + (j + 1) * RANK]
        grad_t[(3 + j) * RANK : (4 + j) * RANK, 0:width] += nt(ut, block) * LOWRANK
        inner.append(nn(down_t[(3 + j) * RANK : (4 + j) * RANK], block) * LOWRANK)
    inner = jnp.concatenate(inner, axis=0).astype(BF16)
    grad_t[0 : 3 * RANK] += nn(inner, x_ref[0])
    whole_buf[step] = tn(gproj[...], wt[0 : 3 * width]).astype(BF16).reshape(nh, part, model)
    to_near(1, step).start()
    to_near(0, step).start()

    @pl.when(step == 1)
    def _():
        two.over_dp()

    @pl.when(step == 2)
    def _():
        two.over_head(1)

    def preconditioned(j, u, where, i):
        where[i] = u
        sq[j : j + 1] = jnp.broadcast_to(
            jnp.sum(jnp.sum(u * u, axis=0, keepdims=True), axis=1, keepdims=True), (1, LANES)
        )

    def mix(t):
        mixed[t] = tn(blocks[t], gradients[t].T, HIGH).astype(BF16)

    def steps_model(t):
        for j in range(roots_m.shape[0]):
            tile, m = slot_of(j)
            if tile == t:
                g = mixed[t, m * RANK : (m + 1) * RANK]
                preconditioned(j, nt(g, roots_m[j].astype(BF16)), step_m, j)

    @pl.when(step == count - 1)
    def _():
        full = grad_t[...].T
        lane = lax.broadcasted_iota(jnp.int32, full.shape, 1)
        late[0] = jnp.where(lane < 3 * RANK, full, 0.0)
        rows = full[0:width]
        lane = lax.broadcasted_iota(jnp.int32, rows.shape, 1)
        late[0, own_rows, :] = jnp.where(lane < 3 * RANK, late[0, own_rows, :], rows)
        one.start(late[...])
        pass_far(count - 1)
        blocks[...] = jnp.zeros_like(blocks)
        sq[...] = jnp.zeros_like(sq)
        for j in range(roots_m.shape[0]):
            t, m = slot_of(j)
            blocks[t, m * RANK : (m + 1) * RANK, m * RANK : (m + 1) * RANK] = roots_r[j]
        split = roots_i.shape[2] // model
        for k in range(split):
            for q in range(2):
                m = 2 * k + q
                blocks[2, m * RANK : (m + 1) * RANK, m * RANK : (m + 1) * RANK] = roots_r[
                    roots_m.shape[0] + q
                ]
        one.over_dp()
        two.finish(gradients.at[1:3])
        one.over_head(0)
        mix(1)
        mix(2)
        for q in range(2):
            u = jnp.zeros((RANK, roots_i.shape[1]), F32)
            for k in range(split):
                m = 2 * k + q
                u = u + nt(
                    mixed[2, m * RANK : (m + 1) * RANK],
                    roots_i[q, :, k * model : (k + 1) * model].astype(BF16),
                )
            preconditioned(roots_m.shape[0] + q, u, step_i, q)
        one.over_head(1)
        steps_model(1)
        for s in range(count):
            complete(s)
        one.finish(gradients.at[0:1])
        mix(0)
        steps_model(0)

        def sq_over_head(k):
            return remote(
                sq, sq_head.at[k], send_a.at[k], recv_a.at[k], (d, lax.rem(h + k, nh))
            )

        def sq_over_dp(k):
            return remote(
                sq_dp.at[0], sq_dp.at[k], send_b.at[k], recv_b.at[k], (lax.rem(d + k, nd), h)
            )

        for k in range(1, nh):
            sq_over_head(k).start()
        total = sq[...]
        for k in range(1, nh):
            sq_over_head(k).wait_recv()
            total = total + sq_head[k]
        sq_dp[0] = total
        for k in range(1, nd):
            sq_over_dp(k).start()
        for k in range(1, nd):
            sq_over_dp(k).wait_recv()
            total = total + sq_dp[k]
        squares[...] = total
        for k in range(1, nh):
            sq_over_head(k).wait_send()
        for k in range(1, nd):
            sq_over_dp(k).wait_send()
        for s in range(count):
            to_far(s).wait_send()
            for i in range(2):
                to_near(i, s).wait_send()
            for r in range(1, nh):
                bring(r, s).wait_send()


def attend_back(
    nd, nh, hidden, proj, p, inverse, go, first, early, wt, down_t, roots_m, roots_i, roots_r
):
    count, keys, model = hidden.shape
    part, width = first.shape[1], model // nh
    heads = width // DH
    tall = 3 * width + 3 * RANK
    shape = jax.ShapeDtypeStruct
    dma = pltpu.SemaphoreType.DMA
    bufs_one, sems_one = Reduction.scratch(nd, nh, 1, model)
    bufs_two, sems_two = Reduction.scratch(nd, nh, 2, model)
    return pl.pallas_call(
        functools.partial(attend_back_kernel, nd, nh),
        grid=(count,),
        in_specs=[
            pl.BlockSpec((1, keys, model), lambda s: (s, 0, 0)),
            pl.BlockSpec((1, tall, keys), lambda s: (s, 0, 0)),
            pl.BlockSpec((1, heads, keys, keys), lambda s: (s, 0, 0, 0)),
            pl.BlockSpec((1, heads, keys), lambda s: (s, 0, 0)),
            anywhere(),
            *[vmem()] * 7,
        ],
        out_specs=[vmem()] * 5,
        out_shape=[
            shape((count, part, model), BF16),
            shape((3, model, LANES), F32),
            shape((roots_m.shape[0], RANK, roots_m.shape[1]), F32),
            shape((2, RANK, roots_i.shape[1]), F32),
            shape((16, LANES), F32),
        ],
        scratch_shapes=[
            pltpu.VMEM((count, width, keys), BF16),
            pltpu.VMEM((3 * width, keys), BF16),
            pltpu.VMEM((LANES, model), F32),
            pltpu.VMEM((1, model, LANES), F32),
            pltpu.VMEM((count, nh, part, model), BF16),
            pltpu.VMEM((count, 2, part, model), BF16),
            pltpu.VMEM((count, part, model), BF16),
            pltpu.VMEM((count, part, model), BF16),
            pltpu.VMEM((3, LANES, LANES), F32),
            pltpu.VMEM((3, LANES, model), BF16),
            pltpu.VMEM((16, LANES), F32),
            pltpu.VMEM((nh, 16, LANES), F32),
            pltpu.VMEM((nd, 16, LANES), F32),
            dma((nh, count)), dma((nh, count)), dma((count,)),
            dma((2, count)), dma((2, count)), dma((count,)), dma((count,)),
            dma((nh,)), dma((nh,)), dma((nd,)), dma((nd,)),
            *bufs_one, *bufs_two, *sems_one, *sems_two,
        ],
        compiler_params=pltpu.CompilerParams(
            collective_id=2, has_side_effects=True, vmem_limit_bytes=VMEM_LIMIT
        ),
        name="attend_back",
    )(hidden, proj, p, inverse, go, first, early, wt, down_t, roots_m, roots_i, roots_r)


def finish_kernel(
    nh, owners, grad_in, g_ref, stats_m, stats_i, stats_r, am, ai, step_m, step_i, squares,
    grad_out, grad_m, grad_i, adapt_m, adapt_i, new_m, new_i, new_r, gt,
):
    grad_out[...] = grad_in[...]
    owner = lax.axis_index("dp") * nh + lax.axis_index("head")
    count, rows, model = stats_m.shape
    rows_i = stats_i.shape[1]
    for t in range(3):
        gt[t] = g_ref[t].T.astype(BF16)
    own = [g_ref[t, pl.ds(owner * rows, rows), :] for t in range(2)]
    turned = [v.T for v in own]

    def update(j, old, u, rate):
        size = model if j < count else rows_i * owners
        mean = squares[j : j + 1, 0:1] * (1.0 / (size * RANK))
        return old - rate * lax.rsqrt(mean + 1e-6) * u

    for j in range(count):
        t, m = slot_of(j)
        lanes = slice(m * RANK, (m + 1) * RANK)
        full = gt[t, lanes]
        grad_m[j] = turned[t][lanes]
        new_m[j] = DECAY * stats_m[j] + (1.0 - DECAY) * nn(own[t][:, lanes].astype(BF16), full)
        new_r[j] = DECAY * stats_r[j] + (1.0 - DECAY) * nt(full, full)
        adapt_m[j] = update(j, am[j], step_m[j], RATE_FIRST if j < 5 else RATE_SECOND)
    blocks = stats_i.shape[2] // model
    per = model // rows_i
    block = owner // per
    tall = g_ref[2, pl.ds((owner - block * per) * rows_i, rows_i), :]
    tall_t = tall.T
    for q in range(2):
        mine = jnp.zeros((rows_i, RANK), F32)
        mine_t = jnp.zeros((RANK, rows_i), F32)
        gram = jnp.zeros((RANK, RANK), F32)
        for k in range(blocks):
            lanes = slice((2 * k + q) * RANK, (2 * k + q + 1) * RANK)
            mine = jnp.where(block == k, tall[:, lanes], mine)
            mine_t = jnp.where(block == k, tall_t[lanes], mine_t)
        grad_i[q] = mine_t
        mine = mine.astype(BF16)
        for k in range(blocks):
            lanes = slice((2 * k + q) * RANK, (2 * k + q + 1) * RANK)
            cols = slice(k * model, (k + 1) * model)
            full = gt[2, lanes]
            gram = gram + nt(full, full)
            new_i[q, :, cols] = DECAY * stats_i[q, :, cols] + (1.0 - DECAY) * nn(mine, full)
        new_r[count + q] = DECAY * stats_r[count + q] + (1.0 - DECAY) * gram
        adapt_i[q] = update(count + q, ai[q], step_i[q], RATE_FIRST if q < 1 else RATE_SECOND)


def finish(nd, nh, grad_in, g, stats_m, stats_i, stats_r, am, ai, step_m, step_i, squares):
    shape = jax.ShapeDtypeStruct
    model = stats_m.shape[2]
    return pl.pallas_call(
        functools.partial(finish_kernel, nh, nd * nh),
        in_specs=[vmem()] * 10,
        out_specs=[vmem()] * 8,
        out_shape=[
            shape(grad_in.shape, BF16),
            shape(am.shape, F32),
            shape(ai.shape, F32),
            shape(am.shape, F32),
            shape(ai.shape, F32),
            shape(stats_m.shape, F32),
            shape(stats_i.shape, F32),
            shape(stats_r.shape, F32),
        ],
        scratch_shapes=[pltpu.VMEM((3, LANES, model), BF16)],
        compiler_params=pltpu.CompilerParams(vmem_limit_bytes=VMEM_LIMIT),
        name="finish",
    )(grad_in, g, stats_m, stats_i, stats_r, am, ai, step_m, step_i, squares)


def local(
    nd,
    nh,
    hidden_input,
    grad_out,
    pair_lengths,
    query_key_value_weight,
    qkv_bias,
    output_projection_weight,
    shifts,
    gains,
    up_projection_weight,
    up_bias,
    down_projection_weight,
    adapters_model,
    adapters_inner,
    stats_model,
    stats_inner,
    stats_rank,
    roots_model,
    roots_inner,
    roots_rank,
):
    model = hidden_input.shape[2]
    turned_m = jnp.swapaxes(adapters_model, 1, 2)
    turned_i = jnp.swapaxes(adapters_inner, 1, 2)
    proj, p, inverse, wt, down_t, result, gat, go, early = forward(
        nd, nh, hidden_input, pair_lengths, turned_m, turned_i,
        jnp.swapaxes(query_key_value_weight, 1, 2), qkv_bias,
        output_projection_weight, up_projection_weight, down_projection_weight,
        grad_out, shifts, gains, up_bias.reshape(1, -1),
    )
    grad_in, gradients, step_m, step_i, squares = attend_back(
        nd, nh, hidden_input, proj, p, inverse, go, gat.reshape(grad_out.shape), early, wt, down_t,
        roots_model, roots_inner, roots_rank,
    )
    grad_in, grad_m, grad_i, adapt_m, adapt_i, new_m, new_i, new_r = finish(
        nd, nh, grad_in, gradients, stats_model, stats_inner, stats_rank, turned_m, turned_i,
        step_m, step_i, squares,
    )
    grad_m, grad_i, adapt_m, adapt_i = (
        jnp.swapaxes(v, 1, 2) for v in (grad_m, grad_i, adapt_m, adapt_i)
    )
    return (result, grad_in, grad_m, grad_i, adapt_m, adapt_i, new_m, new_i, new_r)


def solution(mesh):
    rows = P(None, ("dp", "head"), None)
    in_specs = (
        P("dp", None, None),
        P("dp", "head", None),
        P("dp"),
        P(None, None, "head"),
        P(),
        P("head", None),
        P(),
        P(),
        P(None, "head"),
        P(),
        P("head", None),
        rows, rows, rows, rows,
        P(),
        rows, rows,
        P(),
    )
    out_specs = (
        P("dp", "head", None),
        P("dp", "head", None),
        rows, rows, rows, rows, rows, rows,
        P(),
    )
    body = functools.partial(local, mesh.shape["dp"], mesh.shape["head"])
    return jax.shard_map(body, mesh=mesh, in_specs=in_specs, out_specs=out_specs, check_vma=False)
```

```python
import functools

import jax
import jax.numpy as jnp
from jax import lax
from jax.experimental import pallas as pl
from jax.experimental.pallas import tpu as pltpu
from jax.sharding import PartitionSpec as P

DH = 64
RANK = 16
LANES = 128
LOWRANK = 2.0
RATE_FIRST = 0.01
RATE_SECOND = 0.16
DECAY = 0.5
EPS_NORM = 1e-5
MESH = pl.DeviceIdType.MESH
VMEM_LIMIT = 60 << 20
AHEAD = 3
F32 = jnp.float32
BF16 = jnp.bfloat16
HIGH = lax.Precision.HIGHEST

EARLY_SLOTS = (0, 1, 2, 5, 6, 7)
LATE_SLOTS = (3, 4, 8, 9)


def slot_of(j):
    if j in EARLY_SLOTS:
        return 0, EARLY_SLOTS.index(j)
    return 1, LATE_SLOTS.index(j)


def nn(a, b, precision=None):
    return lax.dot_general(
        a, b, (((1,), (0,)), ((), ())), precision=precision, preferred_element_type=F32
    )


def nt(a, b, precision=None):
    return lax.dot_general(
        a, b, (((1,), (1,)), ((), ())), precision=precision, preferred_element_type=F32
    )


def tn(a, b, precision=None):
    return lax.dot_general(
        a, b, (((0,), (0,)), ((), ())), precision=precision, preferred_element_type=F32
    )


def vmem():
    return pl.BlockSpec(memory_space=pltpu.VMEM)


def anywhere():
    return pl.BlockSpec(memory_space=pl.ANY)


def greet_signal(nd, nh):
    d, h = lax.axis_index("dp"), lax.axis_index("head")
    barrier = pltpu.get_barrier_semaphore()
    for k in range(1, nd):
        pl.semaphore_signal(
            barrier, inc=1, device_id=(lax.rem(d + k, nd), h), device_id_type=MESH
        )
    for k in range(1, nh):
        pl.semaphore_signal(
            barrier, inc=1, device_id=(d, lax.rem(h + k, nh)), device_id_type=MESH
        )


def greet_wait(nd, nh):
    pl.semaphore_wait(pltpu.get_barrier_semaphore(), nd + nh - 2)


def greet(nd, nh):
    greet_signal(nd, nh)
    greet_wait(nd, nh)


def remote(src, dst, send, recv, device):
    return pltpu.make_async_remote_copy(
        src, dst, send, recv, device_id=device, device_id_type=MESH
    )


class Reduction:
    def __init__(self, nd, nh, bufs, sems):
        self.nd, self.nh = nd, nh
        self.out, self.part, self.near, self.full = bufs
        self.sems = sems
        self.d, self.h = lax.axis_index("dp"), lax.axis_index("head")

    @staticmethod
    def scratch(nd, nh, tiles, model):
        rows = -(-(model // nd) // 16) * 16
        dma = pltpu.SemaphoreType.DMA
        return (
            [
                pltpu.VMEM((nd, tiles, rows, LANES), BF16),
                pltpu.VMEM((nd, tiles, rows, LANES), BF16),
                pltpu.VMEM((nh, tiles, rows, LANES), BF16),
                pltpu.VMEM((nd, tiles, rows, LANES), BF16),
            ],
            [dma((nd,)), dma((nd,)), dma((nh,)), dma((nh,)), dma((nd,)), dma((nd,))],
        )

    def to_owner(self, k):
        peer = lax.rem(self.d + k, self.nd)
        return remote(
            self.out.at[peer], self.part.at[k], self.sems[0].at[k], self.sems[1].at[k],
            (peer, self.h),
        )

    def across(self, r):
        here = self.near.at[self.h]
        return remote(
            here, here, self.sems[2].at[r], self.sems[3].at[r],
            (self.d, jnp.bitwise_xor(self.h, r)),
        )

    def to_all(self, k):
        here = self.full.at[self.d]
        return remote(
            here, here, self.sems[4].at[k], self.sems[5].at[k],
            (lax.rem(self.d + k, self.nd), self.h),
        )

    def start(self, values):
        size = values.shape[1] // self.nd
        for i in range(self.nd):
            self.out[i, :, 0:size] = values[:, i * size : (i + 1) * size].astype(BF16)
        for k in range(1, self.nd):
            self.to_owner(k).start()

    def over_dp(self):
        total = self.out[self.d].astype(F32)
        for k in range(1, self.nd):
            self.to_owner(k).wait_recv()
            total = total + self.part[k].astype(F32)
        self.near[self.h] = total.astype(BF16)
        for r in range(self.nh - 1, 0, -1):
            self.across(r).start()

    def over_head(self):
        for r in range(1, self.nh):
            self.across(r).wait_recv()
        total = self.near[0].astype(F32)
        for source in range(1, self.nh):
            total = total + self.near[source].astype(F32)
        self.full[self.d] = total.astype(BF16)
        for k in range(1, self.nd):
            self.to_all(k).start()

    def finish(self, target):
        size = target.shape[1] // self.nd
        for k in range(1, self.nd):
            self.to_all(k).wait_recv()
        for i in range(self.nd):
            target[:, i * size : (i + 1) * size] = self.full[i, :, 0:size].astype(F32)
        for k in range(1, self.nd):
            self.to_owner(k).wait_send()
            self.to_all(k).wait_send()
        for r in range(1, self.nh):
            self.across(r).wait_send()


def cdf_and_density(a):
    cdf = 0.5 * (1.0 + lax.erf(a * 0.7071067811865476))
    return cdf, jnp.exp(-0.5 * a * a) * 0.3989422804014327


def centred(v):
    c = v - jnp.mean(v, axis=-1, keepdims=True)
    inverse = lax.rsqrt(jnp.mean(c * c, axis=-1, keepdims=True) + EPS_NORM)
    return c * inverse, inverse


def norm_back(e, n, inverse):
    return inverse * (
        e - jnp.mean(e, axis=-1, keepdims=True) - n * jnp.mean(e * n, axis=-1, keepdims=True)
    )


def forward_kernel(
    nd, nh, lengths, am, ai, x_ref, x_hbm, w_ref, bias_ref, wo_own, wu_own, wd_own,
    gout, shifts, gains, up_bias,
    proj_ref, p_ref, inv_ref, wt, down_t, result_out, gat_out, go_out, grads_out, got_out,
    packed, packed_more, first_tile, other_tiles, obuf, bias_col, unpack, tile_a, bt,
    o_all, wo, wu, wd, x, ocat, f, slope, h1, n1, i1, h1b, r2, gf, acc, gat, gbt, result, go, grads,
    send_d, recv_d, send_h, recv_h, send_o, recv_o, keep_o, send_w, recv_w, send_s, recv_s,
    load, store, send_g, recv_g, keep_g,
):
    step = pl.program_id(0)
    last = pl.num_programs(0) - 1
    d, h = lax.axis_index("dp"), lax.axis_index("head")
    count, part, model = x.shape
    tokens = count * part
    width = w_ref.shape[1]
    keys = x_ref.shape[1]
    rows = am.shape[2]
    split = ai.shape[2] // rows
    owners = nd * nh
    quarter = lax.rem(d, 4)
    relative = [jnp.bitwise_xor(h, r) for r in range(nh)]

    def at(a, b):
        return (jnp.bitwise_xor(d, a), jnp.bitwise_xor(h, b))

    def window(start, size):
        return pl.ds(pl.multiple_of(start * size, size), size)

    own_w = (wo_own, wu_own, wd_own)

    def piece(w, source, slot):
        if w == 0:
            return wo.at[window(relative[source], width)]
        return (wu, wd)[w - 1].at[slot]

    chunks = []
    for w in range(3):
        quarter_rows = own_w[w].shape[0] // 4
        pieces = 1 if w == 0 else 2
        for n in range(pieces):
            chunks.append((w, quarter_rows, n * quarter_rows // pieces, quarter_rows // pieces))

    def region(ref, c, who, half=None):
        w, quarter_rows, offset, size = chunks[c]
        base = jnp.bitwise_xor(quarter, who) * quarter_rows + offset
        if half is not None:
            first = -(-(size // 2) // 16) * 16
            base, size = (base, first) if half == 0 else (base + first, size - first)
        return ref.at[pl.ds(pl.multiple_of(base, 16), size)]

    def over_x(c):
        w = chunks[c][0]
        return remote(
            region(own_w[w], c, 0), region(piece(w, 0, 2), c, 0),
            send_w.at[0, c], recv_w.at[0, c], at(0, 2),
        )

    def over_x_here(c):
        w = chunks[c][0]
        return remote(
            region(own_w[w], c, 0), region(piece(w, 2, 2), c, 0),
            send_w.at[0, c], recv_w.at[0, c], at(0, 2),
        )

    def spread_w(c, axis):
        here = region(piece(chunks[c][0], 2, 2), c, 0)
        return remote(here, here, send_w.at[axis, c], recv_w.at[axis, c], at(axis, 0))

    def relay_w(c, axis):
        here = region(piece(chunks[c][0], 2, 2), c, 3 - axis, axis - 1)
        return remote(here, here, send_w.at[2 + axis, c], recv_w.at[2 + axis, c], at(axis, 0))

    def sibling_own(w):
        return remote(
            own_w[w], piece(w, 0, 1), send_s.at[0, w], recv_s.at[0, w], at(0, 1)
        )

    def sibling_far(w):
        return remote(
            piece(w, 2, 2), piece(w, 2, 3), send_s.at[1, w], recv_s.at[1, w], at(0, 1)
        )

    def keep_w(w):
        return pltpu.make_async_copy(own_w[w], piece(w, 0, 0), load.at[w])

    def forward(c):
        over_x_here(c).wait_recv()
        spread_w(c, 2).start()
        spread_w(c, 1).start()

    def relay(c):
        spread_w(c, 2).wait_recv()
        relay_w(c, 1).start()
        spread_w(c, 1).wait_recv()
        relay_w(c, 2).start()

    def finish(w, which):
        for c in which:
            relay_w(c, 1).wait_recv()
            relay_w(c, 2).wait_recv()
        sibling_far(w).start()

    stores = (first_tile, other_tiles)
    sources = (packed, packed_more)
    critical, later = 0, 1

    def to_dp(k, slot):
        return remote(
            sources[slot], stores[slot].at[h, d], send_d.at[slot, k], recv_d.at[slot, k],
            (lax.rem(d + k, nd), h),
        )

    def to_head(b, slot):
        column = stores[slot].at[h]
        return remote(column, column, send_h.at[slot, b], recv_h.at[slot, b], at(0, b))

    def pass_on(slot):
        column = stores[slot].at[jnp.bitwise_xor(h, 2)]
        return remote(column, column, send_h.at[slot, 3], recv_h.at[slot, 3], at(0, 1))

    def entry(t, owner):
        if t == 0:
            return first_tile[owner % nh, owner // nh].astype(F32)[0:rows]
        both = other_tiles[owner % nh, owner // nh].astype(F32)
        return both[(t - 1) * rows : t * rows]

    def natural(t):
        return jnp.concatenate([entry(t, i) for i in range(owners)], axis=0)

    def later_to_head():
        for k in range(1, nd):
            to_dp(k, later).wait_recv()
        to_head(2, later).start()
        to_head(1, later).start()

    def later_pass_on():
        to_head(2, later).wait_recv()
        pass_on(later).start()

    def own_rows():
        return pltpu.make_async_copy(x_hbm.at[:, window(h, part), :], x, load.at[3])

    @pl.when(step == 0)
    def _():
        greet_signal(nd, nh)
        groups = [
            [am[j] for j in EARLY_SLOTS],
            [am[j] for j in LATE_SLOTS],
            [ai[q][:, k * rows : (k + 1) * rows] for k in range(split) for q in range(2)],
        ]
        turned = []
        for group in groups:
            short = LANES - len(group) * RANK
            if short:
                group = group + [jnp.zeros((short, rows), F32)]
            turned.append(jnp.concatenate(group, axis=0).T)
        for target, parts in ((packed, turned[0:1]), (packed_more, turned[1:3])):
            short = target.shape[0] - len(parts) * rows
            if short:
                parts = parts + [jnp.zeros((short, LANES), F32)]
            target[...] = jnp.concatenate(parts, axis=0).astype(BF16)
        first_tile[h, d] = packed[...]
        other_tiles[h, d] = packed_more[...]
        greet_wait(nd, nh)
        for k in range(1, nd):
            to_dp(k, critical).start()
        over_x(0).start()
        bias_col[...] = jnp.concatenate(
            [bias_ref[...], jnp.zeros((5, model), F32)], axis=0
        ).T
        for k in range(1, nd):
            to_dp(k, critical).wait_recv()
        to_head(2, critical).start()
        to_head(1, critical).start()
        to_head(2, critical).wait_recv()
        pass_on(critical).start()
        to_head(1, critical).wait_recv()
        pass_on(critical).wait_recv()
        over_x(1).start()
        over_x(2).start()
        pn = natural(0)
        pt = pn.T.astype(BF16)
        tile_a[...] = pn
        own = tile_a[window(h, width), :]
        down_t[...] = own.T.astype(BF16)
        own = own.astype(BF16)
        wt[3 * width :] = pt[0 : 3 * RANK]
        for j in range(3):
            delta = nn(own[:, (3 + j) * RANK : (4 + j) * RANK], pt[j * RANK : (j + 1) * RANK])
            wt[j * width : (j + 1) * width] = (w_ref[j].astype(F32) + LOWRANK * delta).astype(
                BF16
            )
        for k in range(1, nd):
            to_dp(k, later).start()
        for w in range(3):
            sibling_own(w).start()
            keep_w(w).start()
        own_rows().start()

    proj = nt(wt[...], x_ref[0])
    mine = window(h, width)
    for j in range(3):
        proj_ref[0, j * width : (j + 1) * width] = (
            proj[j * width : (j + 1) * width] + bias_col[mine, j : j + 1]
        ).astype(BF16)
    proj_ref[0, 3 * width :] = proj[3 * width :].astype(BF16)
    valid = lax.broadcasted_iota(jnp.int32, (keys, 1), 0) < lengths[step]

    bind = functools.partial
    plan = {
        (0, 3): [bind(forward, 0), bind(forward, 1)],
        (1, 3): [later_to_head, bind(relay, 0), bind(forward, 2)],
        (2, 3): [bind(relay, 1), bind(finish, 0, (0,))],
        (3, 3): [later_pass_on, bind(relay, 2)],
        (4, 3): [bind(finish, 1, (1, 2)), over_x(3).start, over_x(4).start],
    }

    def slots(place):
        for s in range(count):
            if (s, place) in plan:

                @pl.when(step == s)
                def _(s=s):
                    for action in plan[s, place]:
                        action()

    results = []
    for head in range(width // DH):
        rows_q = slice(head * DH, (head + 1) * DH)
        qt = proj_ref[0, rows_q] * jnp.asarray(DH ** (-0.5), BF16)
        kt = proj_ref[0, width + head * DH : width + (head + 1) * DH]
        vt = proj_ref[0, 2 * width + head * DH : 2 * width + (head + 1) * DH]
        st = jnp.where(valid, tn(kt, qt), -1e30)
        top = jnp.max(st, axis=0, keepdims=True)
        et = jnp.exp(st - top)
        inverse = 1.0 / jnp.sum(et, axis=0, keepdims=True)
        low = et.astype(BF16)
        p_ref[0, head] = low
        inv_ref[0, head : head + 1] = inverse
        results.append(nn(vt, low) * inverse)
    obuf[step] = jnp.concatenate(results, axis=0).astype(BF16)

    def block_of(s, r):
        return obuf.at[s, :, window(relative[r], part)]

    def place_of(s, r):
        return o_all.at[window(relative[r], width), window(s, part)]

    def send_block(r, s):
        return remote(
            block_of(s, r), place_of(s, 0), send_o.at[r, s], recv_o.at[r, s], at(0, r)
        )

    def arrive_block(r, s):
        return remote(
            block_of(s, r), place_of(s, r), send_o.at[r, s], recv_o.at[r, s], at(0, r)
        )

    def keep_block(s):
        return pltpu.make_async_copy(block_of(s, 0), place_of(s, 0), keep_o.at[s])

    for r in (2, 3, 1):
        send_block(r, step).start()
    keep_block(step).start()
    slots(3)


    @pl.when(step == last)
    def _():
        to_head(1, later).wait_recv()
        pass_on(later).wait_recv()
        tile_a[...] = natural(1)
        per = owners // split
        for w in range(per):
            for k in range(split):
                blocks = [
                    entry(2, b * per + w)[:, 2 * RANK * k : 2 * RANK * (k + 1)]
                    for b in range(split)
                ]
                base = (w * split + k) * rows
                unpack[base : base + rows] = jnp.concatenate(blocks, axis=1)
        bt[...] = unpack[...].T.astype(BF16)
        ta = tile_a[...].T.astype(BF16)
        p3t, p4t, p8t, p9t = (ta[m * RANK : (m + 1) * RANK] for m in range(4))
        p3 = tile_a[:, 0:RANK].astype(BF16)

        def inner_at(q, r):
            start = pl.multiple_of(relative[r] * 2 * RANK, 2 * RANK) + q * RANK
            return pl.ds(start, RANK)

        for w in range(3):
            keep_w(w).wait()
        own_rows().wait()
        for w in range(3):
            sibling_own(w).wait_recv()
        sibling_far(0).wait_recv()

        def project(first, pairs):
            tokens_here = slice(first * part, (first + pairs) * part)
            for s in range(first, first + pairs):
                keep_block(s).wait()
                for r in range(1, nh):
                    arrive_block(r, s).wait_recv()
            ocat[tokens_here] = o_all[:, tokens_here].T
            z = nt(ocat[tokens_here], p3t).astype(BF16)
            v = (
                x[first : first + pairs].reshape(pairs * part, model).astype(F32)
                + nn(ocat[tokens_here], wo[...])
                + nn(z, p8t) * LOWRANK
                + shifts[0:1]
            )
            n, inv = centred(v)
            n1[tokens_here] = n
            i1[tokens_here] = inv
            h1[tokens_here] = n * gains[0:1] + shifts[1:2]
            h1b[tokens_here] = h1[tokens_here].astype(BF16)
            return z

        z_o = project(0, count - 1)
        z_o = jnp.concatenate([z_o, project(count - 1, 1)], axis=0)
        forward(3)
        z_up = nt(h1b[...], p4t).astype(BF16)
        chunk = 256
        z_d = jnp.zeros((tokens, RANK), F32)
        for r in range(nh):
            if r == 1:
                forward(4)
            if r == 2:
                relay(3)
            if r == 3:
                relay(4)
                sibling_far(1).wait_recv()

            def up(c, carry, r=r):
                cols = window(c, chunk)
                q1 = bt[inner_at(1, r), cols] * jnp.asarray(LOWRANK, BF16)
                bias_at = pl.ds(
                    pl.multiple_of(relative[r] * model + c * chunk, chunk), chunk
                )
                a = nn(h1b[...], wu[r, :, cols]) + nn(z_up, q1) + up_bias[0:1, bias_at]
                cdf, density = cdf_and_density(a)
                f[r, :, cols] = (a * cdf).astype(BF16)
                slope[r, :, cols] = (cdf + a * density).astype(BF16)
                return carry

            lax.fori_loop(0, model // chunk, up, 0, unroll=True)
            z_d = z_d + nt(f[r], bt[inner_at(0, r), :])
        finish(2, (3, 4))
        z_d = z_d.astype(BF16)
        for r in range(nh):
            if r == 3:
                sibling_far(2).wait_recv()
            term = nn(f[r], wd[r])
            if r == 0:
                acc[...] = term + nn(z_d, p9t) * LOWRANK
            else:
                acc[...] += term
        n2, i2 = centred(h1[...] + acc[...] + shifts[2:3])
        result[...] = (n2 * gains[1:2] + shifts[3:4]).astype(BF16).reshape(result.shape)
        give_result = pltpu.make_async_copy(result, result_out, store.at[0])
        give_result.start()
        e = gout[...].reshape(tokens, model).astype(F32) * gains[1:2]
        r2[...] = norm_back(e, n2, i2)
        gf[...] = r2[...].astype(BF16)
        gzd = (nt(gf[...], p9t) * LOWRANK).astype(BF16)
        g9 = tn(z_d, gf[...]) * LOWRANK
        for r in range(nh):
            gbt[inner_at(0, r), :] = tn(gzd, f[r])

        def send_go(r, s):
            return remote(
                go.at[window(relative[r], width), window(s, part)],
                got_out.at[s, :, window(h, part)],
                send_g.at[r, s], recv_g.at[r, s], at(0, r),
            )

        def keep_go(s):
            return pltpu.make_async_copy(
                go.at[window(h, width), window(s, part)],
                got_out.at[s, :, window(h, part)],
                keep_g.at[s],
            )

        g3, g4, g8 = (jnp.zeros((RANK, model), F32) for _ in range(3))
        for first_pair, end_pair in ((0, AHEAD), (AHEAD, count)):
            here = slice(first_pair * part, end_pair * part)
            size = (end_pair - first_pair) * part
            gzu = jnp.zeros((size, RANK), F32)
            for r in range(nh):

                def down(c, carry, r=r, here=here):
                    cols = window(c, chunk)
                    df = nt(gf[here], wd[r, cols, :]) + nn(gzd[here], bt[inner_at(0, r), cols])
                    slope[r, here, cols] = (df * slope[r, here, cols].astype(F32)).astype(BF16)
                    return carry

                lax.fori_loop(0, model // chunk, down, 0, unroll=True)
                ga = slope[r, here]
                gzu = gzu + nt(ga, bt[inner_at(1, r), :])
                term = nt(ga, wu[r])
                if r == 0:
                    acc[here] = r2[here] + term
                else:
                    acc[here] += term
            gzu = (gzu * LOWRANK).astype(BF16)
            g4 = g4 + tn(gzu, h1b[here])
            e = (acc[here] + nn(gzu, p4t)) * gains[0:1]
            gat[here] = norm_back(e, n1[here], i1[here]).astype(BF16)
            gzo = (nt(gat[here], p8t) * LOWRANK).astype(BF16)
            go[:, here] = (nt(wo[...], gat[here]) + nt(p3, gzo)).astype(BF16)
            if first_pair == 0:
                for s in range(AHEAD):
                    for r in (2, 3, 1):
                        send_go(r, s).start()
                    keep_go(s).start()
            g8 = g8 + tn(z_o[here], gat[here]) * LOWRANK
            g3 = g3 + tn(gzo, ocat[here])
        give_gat = pltpu.make_async_copy(gat, gat_out, store.at[1])
        give_gat.start()
        rest = pl.ds(AHEAD * part, (count - AHEAD) * part)
        give_go = pltpu.make_async_copy(go.at[:, rest], go_out, store.at[2])
        give_go.start()
        for r in range(nh):
            gbt[inner_at(1, r), :] = tn(z_up, slope[r]) * LOWRANK
        zeros = jnp.zeros((4 * RANK, model), F32)
        grads[0] = jnp.concatenate([g3, g4, g8, g9, zeros], axis=0).T
        grads[1] = gbt[...].T
        give_grads = pltpu.make_async_copy(grads, grads_out, store.at[3])
        give_grads.start()
        for c in range(len(chunks)):
            over_x(c).wait_send()
            for axis in (1, 2):
                spread_w(c, axis).wait_send()
                relay_w(c, axis).wait_send()
        for slot in (critical, later):
            for k in range(1, nd):
                to_dp(k, slot).wait_send()
            for b in (1, 2):
                to_head(b, slot).wait_send()
            pass_on(slot).wait_send()
        for s in range(count):
            for r in range(1, nh):
                send_block(r, s).wait_send()
        for w in range(3):
            sibling_own(w).wait_send()
            sibling_far(w).wait_send()
        for s in range(AHEAD):
            keep_go(s).wait()
            for r in range(1, nh):
                send_go(r, s).wait()
        for give in (give_result, give_gat, give_go, give_grads):
            give.wait()


def forward(
    nd, nh, hidden, lengths, adapters_m, adapters_i, weight, bias, wo, wu, wd, gout, shifts,
    gains, up_bias,
):
    count, keys, model = hidden.shape
    width = weight.shape[1]
    heads = width // DH
    tall = 3 * width + 3 * RANK
    part = keys // nh
    tokens = count * part
    rows = adapters_m.shape[2]
    padded, padded_more = (-(-k * rows // 16) * 16 for k in (1, 2))
    shape = jax.ShapeDtypeStruct
    dma = pltpu.SemaphoreType.DMA
    return pl.pallas_call(
        functools.partial(forward_kernel, nd, nh),
        grid=(count,),
        in_specs=[
            pl.BlockSpec(memory_space=pltpu.SMEM),
            vmem(), vmem(),
            pl.BlockSpec((1, keys, model), lambda s: (s, 0, 0)),
            anywhere(), vmem(), vmem(), anywhere(), anywhere(), anywhere(),
            vmem(), vmem(), vmem(), vmem(),
        ],
        out_specs=[
            pl.BlockSpec((1, tall, keys), lambda s: (s, 0, 0)),
            pl.BlockSpec((1, heads, keys, keys), lambda s: (s, 0, 0, 0)),
            pl.BlockSpec((1, heads, keys), lambda s: (s, 0, 0)),
            vmem(), vmem(),
            anywhere(), anywhere(), anywhere(), anywhere(), anywhere(),
        ],
        out_shape=[
            shape((count, tall, keys), BF16),
            shape((count, heads, keys, keys), BF16),
            shape((count, heads, keys), F32),
            shape((tall, model), BF16),
            shape((LANES, width), BF16),
            shape((count, part, model), BF16),
            shape((tokens, model), BF16),
            shape((model, (count - AHEAD) * part), BF16),
            shape((2, model, LANES), F32),
            shape((AHEAD, width, keys), BF16),
        ],
        scratch_shapes=[
            pltpu.VMEM((padded, LANES), BF16),
            pltpu.VMEM((padded_more, LANES), BF16),
            pltpu.VMEM((nh, nd, padded, LANES), BF16),
            pltpu.VMEM((nh, nd, padded_more, LANES), BF16),
            pltpu.VMEM((count, width, keys), BF16),
            pltpu.VMEM((model, 8), F32),
            pltpu.VMEM((model, LANES), F32),
            pltpu.VMEM((model, LANES), F32),
            pltpu.VMEM((LANES, model), BF16),
            pltpu.VMEM((model, tokens), BF16),
            pltpu.VMEM((model, model), BF16),
            pltpu.VMEM((nh, model, model), BF16),
            pltpu.VMEM((nh, model, model), BF16),
            pltpu.VMEM((count, part, model), BF16),
            pltpu.VMEM((tokens, model), BF16),
            pltpu.VMEM((nh, tokens, model), BF16),
            pltpu.VMEM((nh, tokens, model), BF16),
            pltpu.VMEM((tokens, model), F32),
            pltpu.VMEM((tokens, model), F32),
            pltpu.VMEM((tokens, 1), F32),
            pltpu.VMEM((tokens, model), BF16),
            pltpu.VMEM((tokens, model), F32),
            pltpu.VMEM((tokens, model), BF16),
            pltpu.VMEM((tokens, model), F32),
            pltpu.VMEM((tokens, model), BF16),
            pltpu.VMEM((LANES, model), F32),
            pltpu.VMEM((count, part, model), BF16),
            pltpu.VMEM((model, tokens), BF16),
            pltpu.VMEM((2, model, LANES), F32),
            dma((2, nd)), dma((2, nd)), dma((2, 4)), dma((2, 4)),
            dma((nh, count)), dma((nh, count)), dma((count,)),
            dma((5, 5)), dma((5, 5)), dma((2, 3)), dma((2, 3)),
            dma((4,)), dma((4,)),
            dma((nh, AHEAD)), dma((nh, AHEAD)), dma((AHEAD,)),
        ],
        compiler_params=pltpu.CompilerParams(
            collective_id=1, has_side_effects=True, vmem_limit_bytes=VMEM_LIMIT
        ),
        name="forward",
    )(
        lengths, adapters_m, adapters_i, hidden, hidden, weight, bias, wo, wu, wd, gout, shifts,
        gains, up_bias,
    )


def attend_back_kernel(
    nd, nh, x_ref, proj_ref, p_ref, inv_ref, go, got_ready, first_hbm, early, wt, down_t,
    roots_m_hbm, roots_i_hbm, roots_r,
    grad_in, gradients, step_m, step_i, squares,
    roots_m, roots_i, first, load, got_all, gproj, grad_t, late, whole_buf, near, far, last, blocks, mixed, sq, sq_head, sq_dp,
    send_g, recv_g, keep_g, send_n, recv_n, send_f, recv_f,
    send_a, recv_a, send_b, recv_b, *rest,
):
    step = pl.program_id(0)
    d, h = lax.axis_index("dp"), lax.axis_index("head")
    relative = [jnp.bitwise_xor(h, r) for r in range(nh)]
    count, part, model = first.shape
    width = got_all.shape[1]
    own_rows = pl.ds(pl.multiple_of(h * width, width), width)
    one = Reduction(nd, nh, rest[0:4], rest[8:14])
    two = Reduction(nd, nh, rest[4:8], rest[14:20])

    def at(b):
        return (d, jnp.bitwise_xor(h, b))

    def fetch(w):
        source, target = (
            (roots_i_hbm, roots_i), (roots_m_hbm, roots_m), (first_hbm, first)
        )[w]
        return pltpu.make_async_copy(source, target, load.at[w])

    def block_of(r, s):
        return go.at[
            pl.ds(pl.multiple_of(relative[r] * width, width), width),
            pl.ds((s - AHEAD) * part, part),
        ]

    def place_of(r, s):
        return got_all.at[s, :, pl.ds(pl.multiple_of(relative[r] * part, part), part)]

    def bring(r, s):
        return remote(
            block_of(r, s), place_of(0, s), send_g.at[r, s], recv_g.at[r, s], at(r)
        )

    def brought(r, s):
        return remote(
            block_of(r, s), place_of(r, s), send_g.at[r, s], recv_g.at[r, s], at(r)
        )

    def keep(s):
        if s < AHEAD:
            return pltpu.make_async_copy(got_ready.at[s], got_all.at[s], keep_g.at[s])
        return pltpu.make_async_copy(block_of(0, s), place_of(0, s), keep_g.at[s])

    def to_near(i, s):
        return remote(
            whole_buf.at[s, relative[1 + 2 * i]], near.at[s, i], send_n.at[i, s],
            recv_n.at[i, s], at(1),
        )

    def to_far(s):
        return remote(far.at[s], last.at[s], send_f.at[s], recv_f.at[s], at(2))

    def pass_far(s):
        to_near(1, s).wait_recv()
        far[s] = (whole_buf[s, relative[2]].astype(F32) + near[s, 1].astype(F32)).astype(BF16)
        to_far(s).start()

    def complete(s):
        to_near(0, s).wait_recv()
        to_far(s).wait_recv()
        grad_in[s] = (
            first[s].astype(F32)
            + whole_buf[s, h].astype(F32)
            + near[s, 0].astype(F32)
            + last[s].astype(F32)
        ).astype(BF16)

    @pl.when(step == 0)
    def _():
        greet_signal(nd, nh)
        for s in range(count):
            keep(s).start()
        for w in range(3):
            fetch(w).start()
        grad_t[...] = jnp.zeros_like(grad_t)

    for s in range(count):

        @pl.when(step == s)
        def _(s=s):
            keep(s).wait()
            if s >= AHEAD:
                for r in range(1, nh):
                    brought(r, s).wait_recv()

    got = got_all.at[step]
    scale = jnp.asarray(DH ** (-0.5), BF16)
    for head in range(width // DH):
        part_h = slice(head * DH, (head + 1) * DH)
        rows_k = slice(width + head * DH, width + (head + 1) * DH)
        rows_v = slice(2 * width + head * DH, 2 * width + (head + 1) * DH)
        inverse = inv_ref[0, head : head + 1]
        qt = proj_ref[0, part_h] * scale
        kt = proj_ref[0, rows_k] * scale
        vt = proj_ref[0, rows_v]
        gs = (got[part_h].astype(F32) * inverse).astype(BF16)
        et = p_ref[0, head]
        ef = et.astype(F32)
        dpt = tn(vt, gs)
        delta = jnp.sum(ef * dpt, axis=0, keepdims=True) * inverse
        gst = (ef * (dpt - delta)).astype(BF16)
        gproj[part_h] = nn(kt, gst).astype(BF16)
        gproj[rows_k] = nt(qt, gst).astype(BF16)
        gproj[rows_v] = nt(gs, et).astype(BF16)

    @pl.when(step == 0)
    def _():
        greet_wait(nd, nh)
        for s in range(AHEAD, count):
            for r in (2, 3, 1):
                bring(r, s).start()
        two.start(early[...])

    @pl.when(step >= 1)
    def _():
        pass_far(jnp.maximum(step - 1, 0))

    inner = []
    for j in range(3):
        block = gproj[j * width : (j + 1) * width]
        ut = proj_ref[0, 3 * width + j * RANK : 3 * width + (j + 1) * RANK]
        grad_t[(3 + j) * RANK : (4 + j) * RANK, 0:width] += nt(ut, block) * LOWRANK
        inner.append(nn(down_t[(3 + j) * RANK : (4 + j) * RANK], block) * LOWRANK)
    inner = jnp.concatenate(inner, axis=0).astype(BF16)
    grad_t[0 : 3 * RANK] += nn(inner, x_ref[0])

    @pl.when(step == count - 1)
    def _():
        full = grad_t[...].T
        lane = lax.broadcasted_iota(jnp.int32, full.shape, 1)
        late[0] = jnp.where(lane < 3 * RANK, full, 0.0)
        rows = full[0:width]
        lane = lax.broadcasted_iota(jnp.int32, rows.shape, 1)
        late[0, own_rows, :] = jnp.where(lane < 3 * RANK, late[0, own_rows, :], rows)
        one.start(late[...])

    whole_buf[step] = tn(gproj[...], wt[0 : 3 * width]).astype(BF16).reshape(nh, part, model)
    to_near(1, step).start()
    to_near(0, step).start()

    @pl.when(step == 1)
    def _():
        two.over_dp()

    @pl.when(step == 2)
    def _():
        two.over_head()

    def preconditioned(j, u, where, i):
        where[i] = u
        sq[j : j + 1] = jnp.broadcast_to(
            jnp.sum(jnp.sum(u * u, axis=0, keepdims=True), axis=1, keepdims=True), (1, LANES)
        )

    def mix(t):
        mixed[t] = tn(blocks[t], gradients[t].T, HIGH).astype(BF16)

    def steps_model(t):
        for j in range(roots_m.shape[0]):
            tile, m = slot_of(j)
            if tile == t:
                g = mixed[t, m * RANK : (m + 1) * RANK]
                preconditioned(j, nt(g, roots_m[j].astype(BF16)), step_m, j)

    @pl.when(step == count - 1)
    def _():
        blocks[...] = jnp.zeros_like(blocks)
        sq[...] = jnp.zeros_like(sq)
        for j in range(roots_m.shape[0]):
            t, m = slot_of(j)
            blocks[t, m * RANK : (m + 1) * RANK, m * RANK : (m + 1) * RANK] = roots_r[j]
        split = roots_i.shape[2] // model
        for k in range(split):
            for q in range(2):
                m = 2 * k + q
                blocks[2, m * RANK : (m + 1) * RANK, m * RANK : (m + 1) * RANK] = roots_r[
                    roots_m.shape[0] + q
                ]
        one.over_dp()
        pass_far(count - 1)
        two.finish(gradients.at[1:3])
        for w in range(3):
            fetch(w).wait()
        one.over_head()
        mix(1)
        mix(2)
        for q in range(2):
            u = jnp.zeros((RANK, roots_i.shape[1]), F32)
            for k in range(split):
                m = 2 * k + q
                u = u + nt(
                    mixed[2, m * RANK : (m + 1) * RANK],
                    roots_i[q, :, k * model : (k + 1) * model].astype(BF16),
                )
            preconditioned(roots_m.shape[0] + q, u, step_i, q)
        steps_model(1)
        one.finish(gradients.at[0:1])
        mix(0)
        steps_model(0)

        def sq_over_head(k):
            return remote(
                sq, sq_head.at[k], send_a.at[k], recv_a.at[k], (d, lax.rem(h + k, nh))
            )

        def sq_over_dp(k):
            return remote(
                sq_dp.at[0], sq_dp.at[k], send_b.at[k], recv_b.at[k], (lax.rem(d + k, nd), h)
            )

        for k in range(1, nh):
            sq_over_head(k).start()
        total = sq[...]
        for k in range(1, nh):
            sq_over_head(k).wait_recv()
            total = total + sq_head[k]
        sq_dp[0] = total
        for k in range(1, nd):
            sq_over_dp(k).start()
        for s in range(count):
            complete(s)
        for k in range(1, nd):
            sq_over_dp(k).wait_recv()
            total = total + sq_dp[k]
        squares[...] = total
        for k in range(1, nh):
            sq_over_head(k).wait_send()
        for k in range(1, nd):
            sq_over_dp(k).wait_send()
        for s in range(count):
            to_far(s).wait_send()
            for i in range(2):
                to_near(i, s).wait_send()
            if s >= AHEAD:
                for r in range(1, nh):
                    bring(r, s).wait_send()


def attend_back(
    nd, nh, hidden, proj, p, inverse, go, got, first, early, wt, down_t, roots_m, roots_i, roots_r
):
    count, keys, model = hidden.shape
    part, width = first.shape[1], model // nh
    heads = width // DH
    tall = 3 * width + 3 * RANK
    shape = jax.ShapeDtypeStruct
    dma = pltpu.SemaphoreType.DMA
    bufs_one, sems_one = Reduction.scratch(nd, nh, 1, model)
    bufs_two, sems_two = Reduction.scratch(nd, nh, 2, model)
    return pl.pallas_call(
        functools.partial(attend_back_kernel, nd, nh),
        grid=(count,),
        in_specs=[
            pl.BlockSpec((1, keys, model), lambda s: (s, 0, 0)),
            pl.BlockSpec((1, tall, keys), lambda s: (s, 0, 0)),
            pl.BlockSpec((1, heads, keys, keys), lambda s: (s, 0, 0, 0)),
            pl.BlockSpec((1, heads, keys), lambda s: (s, 0, 0)),
            anywhere(), anywhere(), anywhere(), vmem(), vmem(), vmem(), anywhere(), anywhere(),
            vmem(),
        ],
        out_specs=[vmem()] * 5,
        out_shape=[
            shape((count, part, model), BF16),
            shape((3, model, LANES), F32),
            shape((roots_m.shape[0], RANK, roots_m.shape[1]), F32),
            shape((2, RANK, roots_i.shape[1]), F32),
            shape((16, LANES), F32),
        ],
        scratch_shapes=[
            pltpu.VMEM(roots_m.shape, F32),
            pltpu.VMEM(roots_i.shape, F32),
            pltpu.VMEM((count, part, model), BF16),
            dma((3,)),
            pltpu.VMEM((count, width, keys), BF16),
            pltpu.VMEM((3 * width, keys), BF16),
            pltpu.VMEM((LANES, model), F32),
            pltpu.VMEM((1, model, LANES), F32),
            pltpu.VMEM((count, nh, part, model), BF16),
            pltpu.VMEM((count, 2, part, model), BF16),
            pltpu.VMEM((count, part, model), BF16),
            pltpu.VMEM((count, part, model), BF16),
            pltpu.VMEM((3, LANES, LANES), F32),
            pltpu.VMEM((3, LANES, model), BF16),
            pltpu.VMEM((16, LANES), F32),
            pltpu.VMEM((nh, 16, LANES), F32),
            pltpu.VMEM((nd, 16, LANES), F32),
            dma((nh, count)), dma((nh, count)), dma((count,)),
            dma((2, count)), dma((2, count)), dma((count,)), dma((count,)),
            dma((nh,)), dma((nh,)), dma((nd,)), dma((nd,)),
            *bufs_one, *bufs_two, *sems_one, *sems_two,
        ],
        compiler_params=pltpu.CompilerParams(
            collective_id=2, has_side_effects=True, vmem_limit_bytes=VMEM_LIMIT
        ),
        name="attend_back",
    )(hidden, proj, p, inverse, go, got, first, early, wt, down_t, roots_m, roots_i, roots_r)


def finish_kernel(
    nh, owners, grad_in, g_ref, stats_m, stats_i, stats_r, am, ai, step_m, step_i, squares,
    grad_out, grad_m, grad_i, adapt_m, adapt_i, new_m, new_i, new_r, gt,
):
    grad_out[...] = grad_in[...]
    owner = lax.axis_index("dp") * nh + lax.axis_index("head")
    count, rows, model = stats_m.shape
    rows_i = stats_i.shape[1]
    for t in range(3):
        gt[t] = g_ref[t].T.astype(BF16)
    own = [g_ref[t, pl.ds(owner * rows, rows), :] for t in range(2)]
    turned = [v.T for v in own]

    def update(j, old, u, rate):
        size = model if j < count else rows_i * owners
        mean = squares[j : j + 1, 0:1] * (1.0 / (size * RANK))
        return old - rate * lax.rsqrt(mean + 1e-6) * u

    for j in range(count):
        t, m = slot_of(j)
        lanes = slice(m * RANK, (m + 1) * RANK)
        full = gt[t, lanes]
        grad_m[j] = turned[t][lanes]
        new_m[j] = DECAY * stats_m[j] + (1.0 - DECAY) * nn(own[t][:, lanes].astype(BF16), full)
        new_r[j] = DECAY * stats_r[j] + (1.0 - DECAY) * nt(full, full)
        adapt_m[j] = update(j, am[j], step_m[j], RATE_FIRST if j < 5 else RATE_SECOND)
    blocks = stats_i.shape[2] // model
    per = model // rows_i
    block = owner // per
    tall = g_ref[2, pl.ds((owner - block * per) * rows_i, rows_i), :]
    tall_t = tall.T
    for q in range(2):
        mine = jnp.zeros((rows_i, RANK), F32)
        mine_t = jnp.zeros((RANK, rows_i), F32)
        gram = jnp.zeros((RANK, RANK), F32)
        for k in range(blocks):
            lanes = slice((2 * k + q) * RANK, (2 * k + q + 1) * RANK)
            mine = jnp.where(block == k, tall[:, lanes], mine)
            mine_t = jnp.where(block == k, tall_t[lanes], mine_t)
        grad_i[q] = mine_t
        mine = mine.astype(BF16)
        for k in range(blocks):
            lanes = slice((2 * k + q) * RANK, (2 * k + q + 1) * RANK)
            cols = slice(k * model, (k + 1) * model)
            full = gt[2, lanes]
            gram = gram + nt(full, full)
            new_i[q, :, cols] = DECAY * stats_i[q, :, cols] + (1.0 - DECAY) * nn(mine, full)
        new_r[count + q] = DECAY * stats_r[count + q] + (1.0 - DECAY) * gram
        adapt_i[q] = update(count + q, ai[q], step_i[q], RATE_FIRST if q < 1 else RATE_SECOND)


def finish(nd, nh, grad_in, g, stats_m, stats_i, stats_r, am, ai, step_m, step_i, squares):
    shape = jax.ShapeDtypeStruct
    model = stats_m.shape[2]
    return pl.pallas_call(
        functools.partial(finish_kernel, nh, nd * nh),
        in_specs=[vmem()] * 10,
        out_specs=[vmem()] * 8,
        out_shape=[
            shape(grad_in.shape, BF16),
            shape(am.shape, F32),
            shape(ai.shape, F32),
            shape(am.shape, F32),
            shape(ai.shape, F32),
            shape(stats_m.shape, F32),
            shape(stats_i.shape, F32),
            shape(stats_r.shape, F32),
        ],
        scratch_shapes=[pltpu.VMEM((3, LANES, model), BF16)],
        compiler_params=pltpu.CompilerParams(vmem_limit_bytes=VMEM_LIMIT),
        name="finish",
    )(grad_in, g, stats_m, stats_i, stats_r, am, ai, step_m, step_i, squares)


def local(
    nd,
    nh,
    hidden_input,
    grad_out,
    pair_lengths,
    query_key_value_weight,
    qkv_bias,
    output_projection_weight,
    shifts,
    gains,
    up_projection_weight,
    up_bias,
    down_projection_weight,
    adapters_model,
    adapters_inner,
    stats_model,
    stats_inner,
    stats_rank,
    roots_model,
    roots_inner,
    roots_rank,
):
    model = hidden_input.shape[2]
    turned_m = jnp.swapaxes(adapters_model, 1, 2)
    turned_i = jnp.swapaxes(adapters_inner, 1, 2)
    proj, p, inverse, wt, down_t, result, gat, go, early, got = forward(
        nd, nh, hidden_input, pair_lengths, turned_m, turned_i,
        jnp.swapaxes(query_key_value_weight, 1, 2), qkv_bias,
        output_projection_weight, up_projection_weight, down_projection_weight,
        grad_out, shifts, gains, up_bias.reshape(1, -1),
    )
    grad_in, gradients, step_m, step_i, squares = attend_back(
        nd, nh, hidden_input, proj, p, inverse, go, got, gat.reshape(grad_out.shape), early, wt, down_t,
        roots_model, roots_inner, roots_rank,
    )
    grad_in, grad_m, grad_i, adapt_m, adapt_i, new_m, new_i, new_r = finish(
        nd, nh, grad_in, gradients, stats_model, stats_inner, stats_rank, turned_m, turned_i,
        step_m, step_i, squares,
    )
    grad_m, grad_i, adapt_m, adapt_i = (
        jnp.swapaxes(v, 1, 2) for v in (grad_m, grad_i, adapt_m, adapt_i)
    )
    return (result, grad_in, grad_m, grad_i, adapt_m, adapt_i, new_m, new_i, new_r)


def solution(mesh):
    rows = P(None, ("dp", "head"), None)
    in_specs = (
        P("dp", None, None),
        P("dp", "head", None),
        P("dp"),
        P(None, None, "head"),
        P(),
        P("head", None),
        P(),
        P(),
        P(None, "head"),
        P(),
        P("head", None),
        rows, rows, rows, rows,
        P(),
        rows, rows,
        P(),
    )
    out_specs = (
        P("dp", "head", None),
        P("dp", "head", None),
        rows, rows, rows, rows, rows, rows,
        P(),
    )
    body = functools.partial(local, mesh.shape["dp"], mesh.shape["head"])
    return jax.shard_map(body, mesh=mesh, in_specs=in_specs, out_specs=out_specs, check_vma=False)
```

```python
import functools

import jax
import jax.numpy as jnp
from jax import lax
from jax.experimental import pallas as pl
from jax.experimental.pallas import tpu as pltpu
from jax.sharding import PartitionSpec as P

DH = 64
RANK = 16
LANES = 128
LOWRANK = 2.0
RATE_FIRST = 0.01
RATE_SECOND = 0.16
DECAY = 0.5
EPS_NORM = 1e-5
MESH = pl.DeviceIdType.MESH
VMEM_LIMIT = 60 << 20
AHEAD = 3
F32 = jnp.float32
BF16 = jnp.bfloat16
HIGH = lax.Precision.HIGHEST

EARLY_SLOTS = (0, 1, 2, 5, 6, 7)
LATE_SLOTS = (3, 4, 8, 9)


def slot_of(j):
    if j in EARLY_SLOTS:
        return 0, EARLY_SLOTS.index(j)
    return 1, LATE_SLOTS.index(j)


def nn(a, b, precision=None):
    return lax.dot_general(
        a, b, (((1,), (0,)), ((), ())), precision=precision, preferred_element_type=F32
    )


def nt(a, b, precision=None):
    return lax.dot_general(
        a, b, (((1,), (1,)), ((), ())), precision=precision, preferred_element_type=F32
    )


def tn(a, b, precision=None):
    return lax.dot_general(
        a, b, (((0,), (0,)), ((), ())), precision=precision, preferred_element_type=F32
    )


def vmem():
    return pl.BlockSpec(memory_space=pltpu.VMEM)


def anywhere():
    return pl.BlockSpec(memory_space=pl.ANY)


def greet_signal(nd, nh):
    d, h = lax.axis_index("dp"), lax.axis_index("head")
    barrier = pltpu.get_barrier_semaphore()
    for k in range(1, nd):
        pl.semaphore_signal(
            barrier, inc=1, device_id=(lax.rem(d + k, nd), h), device_id_type=MESH
        )
    for k in range(1, nh):
        pl.semaphore_signal(
            barrier, inc=1, device_id=(d, lax.rem(h + k, nh)), device_id_type=MESH
        )


def greet_wait(nd, nh):
    pl.semaphore_wait(pltpu.get_barrier_semaphore(), nd + nh - 2)


def greet(nd, nh):
    greet_signal(nd, nh)
    greet_wait(nd, nh)


def remote(src, dst, send, recv, device):
    return pltpu.make_async_remote_copy(
        src, dst, send, recv, device_id=device, device_id_type=MESH
    )


class Reduction:
    def __init__(self, nd, nh, bufs, sems):
        self.nd, self.nh = nd, nh
        self.out, self.part, self.near, self.full = bufs
        self.sems = sems
        self.d, self.h = lax.axis_index("dp"), lax.axis_index("head")

    @staticmethod
    def scratch(nd, nh, tiles, model):
        rows = -(-(model // nd) // 16) * 16
        dma = pltpu.SemaphoreType.DMA
        return (
            [
                pltpu.VMEM((nd, tiles, rows, LANES), BF16),
                pltpu.VMEM((nd, tiles, rows, LANES), BF16),
                pltpu.VMEM((nh, tiles, rows, LANES), BF16),
                pltpu.VMEM((nd, tiles, rows, LANES), BF16),
            ],
            [dma((nd,)), dma((nd,)), dma((nh,)), dma((nh,)), dma((nd,)), dma((nd,))],
        )

    def to_owner(self, k):
        peer = lax.rem(self.d + k, self.nd)
        return remote(
            self.out.at[peer], self.part.at[k], self.sems[0].at[k], self.sems[1].at[k],
            (peer, self.h),
        )

    def across(self, r):
        here = self.near.at[self.h]
        return remote(
            here, here, self.sems[2].at[r], self.sems[3].at[r],
            (self.d, jnp.bitwise_xor(self.h, r)),
        )

    def to_all(self, k):
        here = self.full.at[self.d]
        return remote(
            here, here, self.sems[4].at[k], self.sems[5].at[k],
            (lax.rem(self.d + k, self.nd), self.h),
        )

    def start(self, values):
        size = values.shape[1] // self.nd
        for i in range(self.nd):
            self.out[i, :, 0:size] = values[:, i * size : (i + 1) * size].astype(BF16)
        for k in range(1, self.nd):
            self.to_owner(k).start()

    def over_dp(self):
        total = self.out[self.d].astype(F32)
        for k in range(1, self.nd):
            self.to_owner(k).wait_recv()
            total = total + self.part[k].astype(F32)
        self.near[self.h] = total.astype(BF16)
        for r in range(self.nh - 1, 0, -1):
            self.across(r).start()

    def over_head(self):
        for r in range(1, self.nh):
            self.across(r).wait_recv()
        total = self.near[0].astype(F32)
        for source in range(1, self.nh):
            total = total + self.near[source].astype(F32)
        self.full[self.d] = total.astype(BF16)
        for k in range(1, self.nd):
            self.to_all(k).start()

    def finish(self, target):
        size = target.shape[1] // self.nd
        for k in range(1, self.nd):
            self.to_all(k).wait_recv()
        for i in range(self.nd):
            target[:, i * size : (i + 1) * size] = self.full[i, :, 0:size].astype(F32)
        for k in range(1, self.nd):
            self.to_owner(k).wait_send()
            self.to_all(k).wait_send()
        for r in range(1, self.nh):
            self.across(r).wait_send()


def cdf_and_density(a):
    cdf = 0.5 * (1.0 + lax.erf(a * 0.7071067811865476))
    return cdf, jnp.exp(-0.5 * a * a) * 0.3989422804014327


def centred(v):
    c = v - jnp.mean(v, axis=-1, keepdims=True)
    inverse = lax.rsqrt(jnp.mean(c * c, axis=-1, keepdims=True) + EPS_NORM)
    return c * inverse, inverse


def norm_back(e, n, inverse):
    return inverse * (
        e - jnp.mean(e, axis=-1, keepdims=True) - n * jnp.mean(e * n, axis=-1, keepdims=True)
    )


def forward_kernel(
    nd, nh, lengths, am, ai, x_ref, x_hbm, w_ref, bias_ref, wo_own, wu_own, wd_own,
    gout, shifts, gains, up_bias,
    proj_ref, p_ref, inv_ref, wt, down_t, result_out, gat_out, go_out, grads_out, got_out,
    packed, packed_more, first_tile, other_tiles, obuf, bias_col, unpack, tile_a, bt,
    o_all, wo, wu, wd, x, ocat, f, slope, h1, n1, i1, h1b, r2, gf, acc, gat, gbt, result, go, grads,
    send_d, recv_d, send_h, recv_h, send_o, recv_o, keep_o, send_w, recv_w, send_s, recv_s,
    load, store, send_g, recv_g, keep_g,
):
    step = pl.program_id(0)
    last = pl.num_programs(0) - 1
    d, h = lax.axis_index("dp"), lax.axis_index("head")
    count, part, model = x.shape
    tokens = count * part
    width = w_ref.shape[1]
    keys = x_ref.shape[1]
    rows = am.shape[2]
    split = ai.shape[2] // rows
    owners = nd * nh
    quarter = lax.rem(d, 4)
    relative = [jnp.bitwise_xor(h, r) for r in range(nh)]

    def at(a, b):
        return (jnp.bitwise_xor(d, a), jnp.bitwise_xor(h, b))

    def window(start, size):
        return pl.ds(pl.multiple_of(start * size, size), size)

    own_w = (wo_own, wu_own, wd_own)

    def piece(w, source, slot):
        if w == 0:
            return wo.at[window(relative[source], width)]
        return (wu, wd)[w - 1].at[slot]

    chunks = []
    for w in range(3):
        quarter_rows = own_w[w].shape[0] // 4
        pieces = 1 if w == 0 else 2
        for n in range(pieces):
            chunks.append((w, quarter_rows, n * quarter_rows // pieces, quarter_rows // pieces))

    def region(ref, c, who, half=None):
        w, quarter_rows, offset, size = chunks[c]
        base = jnp.bitwise_xor(quarter, who) * quarter_rows + offset
        if half is not None:
            first = -(-(size // 2) // 16) * 16
            base, size = (base, first) if half == 0 else (base + first, size - first)
        return ref.at[pl.ds(pl.multiple_of(base, 16), size)]

    def over_x(c):
        w = chunks[c][0]
        return remote(
            region(own_w[w], c, 0), region(piece(w, 0, 2), c, 0),
            send_w.at[0, c], recv_w.at[0, c], at(0, 2),
        )

    def over_x_here(c):
        w = chunks[c][0]
        return remote(
            region(own_w[w], c, 0), region(piece(w, 2, 2), c, 0),
            send_w.at[0, c], recv_w.at[0, c], at(0, 2),
        )

    def spread_w(c, axis):
        here = region(piece(chunks[c][0], 2, 2), c, 0)
        return remote(here, here, send_w.at[axis, c], recv_w.at[axis, c], at(axis, 0))

    def relay_w(c, axis):
        here = region(piece(chunks[c][0], 2, 2), c, 3 - axis, axis - 1)
        return remote(here, here, send_w.at[2 + axis, c], recv_w.at[2 + axis, c], at(axis, 0))

    def sibling_own(w):
        return remote(
            own_w[w], piece(w, 0, 1), send_s.at[0, w], recv_s.at[0, w], at(0, 1)
        )

    def sibling_far(w):
        return remote(
            piece(w, 2, 2), piece(w, 2, 3), send_s.at[1, w], recv_s.at[1, w], at(0, 1)
        )

    def keep_w(w):
        return pltpu.make_async_copy(own_w[w], piece(w, 0, 0), load.at[w])

    def forward(c):
        over_x_here(c).wait_recv()
        spread_w(c, 2).start()
        spread_w(c, 1).start()

    def relay(c):
        spread_w(c, 2).wait_recv()
        relay_w(c, 1).start()
        spread_w(c, 1).wait_recv()
        relay_w(c, 2).start()

    def finish(w, which):
        for c in which:
            relay_w(c, 1).wait_recv()
            relay_w(c, 2).wait_recv()
        sibling_far(w).start()

    stores = (first_tile, other_tiles)
    sources = (packed, packed_more)
    critical, later = 0, 1

    def to_dp(k, slot):
        return remote(
            sources[slot], stores[slot].at[h, d], send_d.at[slot, k], recv_d.at[slot, k],
            (lax.rem(d + k, nd), h),
        )

    def to_head(b, slot):
        column = stores[slot].at[h]
        return remote(column, column, send_h.at[slot, b], recv_h.at[slot, b], at(0, b))

    def pass_on(slot):
        column = stores[slot].at[jnp.bitwise_xor(h, 2)]
        return remote(column, column, send_h.at[slot, 3], recv_h.at[slot, 3], at(0, 1))

    def entry(t, owner):
        if t == 0:
            return first_tile[owner % nh, owner // nh].astype(F32)[0:rows]
        both = other_tiles[owner % nh, owner // nh].astype(F32)
        return both[(t - 1) * rows : t * rows]

    def natural(t):
        return jnp.concatenate([entry(t, i) for i in range(owners)], axis=0)

    def later_to_head():
        for k in range(1, nd):
            to_dp(k, later).wait_recv()
        to_head(2, later).start()
        to_head(1, later).start()

    def later_pass_on():
        to_head(2, later).wait_recv()
        pass_on(later).start()

    def own_rows():
        return pltpu.make_async_copy(x_hbm.at[:, window(h, part), :], x, load.at[3])

    @pl.when(step == 0)
    def _():
        greet_signal(nd, nh)
        groups = [
            [am[j] for j in EARLY_SLOTS],
            [am[j] for j in LATE_SLOTS],
            [ai[q][:, k * rows : (k + 1) * rows] for k in range(split) for q in range(2)],
        ]
        turned = []
        for group in groups:
            short = LANES - len(group) * RANK
            if short:
                group = group + [jnp.zeros((short, rows), F32)]
            turned.append(jnp.concatenate(group, axis=0).T)
        for target, parts in ((packed, turned[0:1]), (packed_more, turned[1:3])):
            short = target.shape[0] - len(parts) * rows
            if short:
                parts = parts + [jnp.zeros((short, LANES), F32)]
            target[...] = jnp.concatenate(parts, axis=0).astype(BF16)
        first_tile[h, d] = packed[...]
        other_tiles[h, d] = packed_more[...]
        greet_wait(nd, nh)
        for k in range(1, nd):
            to_dp(k, critical).start()
        over_x(0).start()
        bias_col[...] = jnp.concatenate(
            [bias_ref[...], jnp.zeros((5, model), F32)], axis=0
        ).T
        for k in range(1, nd):
            to_dp(k, critical).wait_recv()
        to_head(2, critical).start()
        to_head(1, critical).start()
        to_head(2, critical).wait_recv()
        pass_on(critical).start()
        to_head(1, critical).wait_recv()
        pass_on(critical).wait_recv()
        over_x(1).start()
        over_x(2).start()
        pn = natural(0)
        pt = pn.T.astype(BF16)
        tile_a[...] = pn
        own = tile_a[window(h, width), :]
        down_t[...] = own.T.astype(BF16)
        own = own.astype(BF16)
        wt[3 * width :] = pt[0 : 3 * RANK]
        for j in range(3):
            delta = nn(own[:, (3 + j) * RANK : (4 + j) * RANK], pt[j * RANK : (j + 1) * RANK])
            wt[j * width : (j + 1) * width] = (w_ref[j].astype(F32) + LOWRANK * delta).astype(
                BF16
            )
        for k in range(1, nd):
            to_dp(k, later).start()
        for w in range(3):
            sibling_own(w).start()
            keep_w(w).start()
        own_rows().start()

    proj = nt(wt[...], x_ref[0])
    mine = window(h, width)
    for j in range(3):
        proj_ref[0, j * width : (j + 1) * width] = (
            proj[j * width : (j + 1) * width] + bias_col[mine, j : j + 1]
        ).astype(BF16)
    proj_ref[0, 3 * width :] = proj[3 * width :].astype(BF16)
    valid = lax.broadcasted_iota(jnp.int32, (keys, 1), 0) < lengths[step]

    bind = functools.partial
    plan = {
        (0, 3): [bind(forward, 0), bind(forward, 1)],
        (1, 3): [later_to_head, bind(relay, 0), bind(forward, 2)],
        (2, 3): [bind(relay, 1), bind(finish, 0, (0,))],
        (3, 3): [later_pass_on, bind(relay, 2)],
        (4, 3): [bind(finish, 1, (1, 2)), over_x(3).start, over_x(4).start],
    }

    def slots(place):
        for s in range(count):
            if (s, place) in plan:

                @pl.when(step == s)
                def _(s=s):
                    for action in plan[s, place]:
                        action()

    results = []
    for head in range(width // DH):
        rows_q = slice(head * DH, (head + 1) * DH)
        qt = proj_ref[0, rows_q] * jnp.asarray(DH ** (-0.5), BF16)
        kt = proj_ref[0, width + head * DH : width + (head + 1) * DH]
        vt = proj_ref[0, 2 * width + head * DH : 2 * width + (head + 1) * DH]
        st = jnp.where(valid, tn(kt, qt), -1e30)
        top = jnp.max(st, axis=0, keepdims=True)
        et = jnp.exp(st - top)
        inverse = 1.0 / jnp.sum(et, axis=0, keepdims=True)
        low = et.astype(BF16)
        p_ref[0, head] = low
        inv_ref[0, head : head + 1] = inverse
        results.append(nn(vt, low) * inverse)
    obuf[step] = jnp.concatenate(results, axis=0).astype(BF16)

    def block_of(s, r):
        return obuf.at[s, :, window(relative[r], part)]

    def place_of(s, r):
        return o_all.at[window(relative[r], width), window(s, part)]

    def send_block(r, s):
        return remote(
            block_of(s, r), place_of(s, 0), send_o.at[r, s], recv_o.at[r, s], at(0, r)
        )

    def arrive_block(r, s):
        return remote(
            block_of(s, r), place_of(s, r), send_o.at[r, s], recv_o.at[r, s], at(0, r)
        )

    def keep_block(s):
        return pltpu.make_async_copy(block_of(s, 0), place_of(s, 0), keep_o.at[s])

    for r in (2, 3, 1):
        send_block(r, step).start()
    keep_block(step).start()
    slots(3)


    @pl.when(step == last)
    def _():
        to_head(1, later).wait_recv()
        pass_on(later).wait_recv()
        tile_a[...] = natural(1)
        per = owners // split
        for w in range(per):
            for k in range(split):
                blocks = [
                    entry(2, b * per + w)[:, 2 * RANK * k : 2 * RANK * (k + 1)]
                    for b in range(split)
                ]
                base = (w * split + k) * rows
                unpack[base : base + rows] = jnp.concatenate(blocks, axis=1)
        bt[...] = unpack[...].T.astype(BF16)
        ta = tile_a[...].T.astype(BF16)
        p3t, p4t, p8t, p9t = (ta[m * RANK : (m + 1) * RANK] for m in range(4))
        p3 = tile_a[:, 0:RANK].astype(BF16)

        def inner_at(q, r):
            start = pl.multiple_of(relative[r] * 2 * RANK, 2 * RANK) + q * RANK
            return pl.ds(start, RANK)

        for w in range(3):
            keep_w(w).wait()
        own_rows().wait()
        for w in range(3):
            sibling_own(w).wait_recv()
        sibling_far(0).wait_recv()

        def project(first, pairs):
            tokens_here = slice(first * part, (first + pairs) * part)
            for s in range(first, first + pairs):
                keep_block(s).wait()
                for r in range(1, nh):
                    arrive_block(r, s).wait_recv()
            ocat[tokens_here] = o_all[:, tokens_here].T
            z = nt(ocat[tokens_here], p3t).astype(BF16)
            v = (
                x[first : first + pairs].reshape(pairs * part, model).astype(F32)
                + nn(ocat[tokens_here], wo[...])
                + nn(z, p8t) * LOWRANK
                + shifts[0:1]
            )
            n, inv = centred(v)
            n1[tokens_here] = n
            i1[tokens_here] = inv
            h1[tokens_here] = n * gains[0:1] + shifts[1:2]
            h1b[tokens_here] = h1[tokens_here].astype(BF16)
            return z

        z_o = project(0, count - 1)
        z_o = jnp.concatenate([z_o, project(count - 1, 1)], axis=0)
        forward(3)
        z_up = nt(h1b[...], p4t).astype(BF16)
        chunk = 256
        z_d = jnp.zeros((tokens, RANK), F32)
        for r in range(nh):
            if r == 1:
                forward(4)
            if r == 2:
                relay(3)
            if r == 3:
                relay(4)
                sibling_far(1).wait_recv()

            def up(c, carry, r=r):
                cols = window(c, chunk)
                q1 = bt[inner_at(1, r), cols] * jnp.asarray(LOWRANK, BF16)
                bias_at = pl.ds(
                    pl.multiple_of(relative[r] * model + c * chunk, chunk), chunk
                )
                a = nn(h1b[...], wu[r, :, cols]) + nn(z_up, q1) + up_bias[0:1, bias_at]
                cdf, density = cdf_and_density(a)
                f[r, :, cols] = (a * cdf).astype(BF16)
                slope[r, :, cols] = (cdf + a * density).astype(BF16)
                return carry

            lax.fori_loop(0, model // chunk, up, 0, unroll=True)
            z_d = z_d + nt(f[r], bt[inner_at(0, r), :])
        finish(2, (3, 4))
        z_d = z_d.astype(BF16)
        for r in range(nh):
            if r == 3:
                sibling_far(2).wait_recv()
            term = nn(f[r], wd[r])
            if r == 0:
                acc[...] = term + nn(z_d, p9t) * LOWRANK
            else:
                acc[...] += term
        n2, i2 = centred(h1[...] + acc[...] + shifts[2:3])
        result[...] = (n2 * gains[1:2] + shifts[3:4]).astype(BF16).reshape(result.shape)
        give_result = pltpu.make_async_copy(result, result_out, store.at[0])
        give_result.start()
        e = gout[...].reshape(tokens, model).astype(F32) * gains[1:2]
        r2[...] = norm_back(e, n2, i2)
        gf[...] = r2[...].astype(BF16)
        gzd = (nt(gf[...], p9t) * LOWRANK).astype(BF16)
        g9 = tn(z_d, gf[...]) * LOWRANK
        for r in range(nh):
            gbt[inner_at(0, r), :] = tn(gzd, f[r])

        def send_go(r, s):
            return remote(
                go.at[window(relative[r], width), window(s, part)],
                got_out.at[s, :, window(h, part)],
                send_g.at[r, s], recv_g.at[r, s], at(0, r),
            )

        def keep_go(s):
            return pltpu.make_async_copy(
                go.at[window(h, width), window(s, part)],
                got_out.at[s, :, window(h, part)],
                keep_g.at[s],
            )

        give_gat = pltpu.make_async_copy(gat, gat_out, store.at[1])
        rest = pl.ds(AHEAD * part, (count - AHEAD) * part)
        give_go = pltpu.make_async_copy(go.at[:, rest], go_out, store.at[2])
        g3, g4, g8 = (jnp.zeros((RANK, model), F32) for _ in range(3))
        for first_pair, end_pair in ((0, AHEAD), (AHEAD, count)):
            here = slice(first_pair * part, end_pair * part)
            size = (end_pair - first_pair) * part
            gzu = jnp.zeros((size, RANK), F32)
            for r in range(nh):

                def down(c, carry, r=r, here=here):
                    cols = window(c, chunk)
                    df = nt(gf[here], wd[r, cols, :]) + nn(gzd[here], bt[inner_at(0, r), cols])
                    slope[r, here, cols] = (df * slope[r, here, cols].astype(F32)).astype(BF16)
                    return carry

                lax.fori_loop(0, model // chunk, down, 0, unroll=True)
                ga = slope[r, here]
                gzu = gzu + nt(ga, bt[inner_at(1, r), :])
                term = nt(ga, wu[r])
                if r == 0:
                    acc[here] = r2[here] + term
                else:
                    acc[here] += term
            gzu = (gzu * LOWRANK).astype(BF16)
            g4 = g4 + tn(gzu, h1b[here])
            e = (acc[here] + nn(gzu, p4t)) * gains[0:1]
            gat[here] = norm_back(e, n1[here], i1[here]).astype(BF16)
            gzo = (nt(gat[here], p8t) * LOWRANK).astype(BF16)
            go[:, here] = (nt(wo[...], gat[here]) + nt(p3, gzo)).astype(BF16)
            if first_pair == 0:
                for s in range(AHEAD):
                    for r in (2, 3, 1):
                        send_go(r, s).start()
                    keep_go(s).start()
            else:
                give_gat.start()
                give_go.start()
            g8 = g8 + tn(z_o[here], gat[here]) * LOWRANK
            g3 = g3 + tn(gzo, ocat[here])
        for r in range(nh):
            gbt[inner_at(1, r), :] = tn(z_up, slope[r]) * LOWRANK
        zeros = jnp.zeros((4 * RANK, model), F32)
        grads[0] = jnp.concatenate([g3, g4, g8, g9, zeros], axis=0).T
        grads[1] = gbt[...].T
        give_grads = pltpu.make_async_copy(grads, grads_out, store.at[3])
        give_grads.start()
        for c in range(len(chunks)):
            over_x(c).wait_send()
            for axis in (1, 2):
                spread_w(c, axis).wait_send()
                relay_w(c, axis).wait_send()
        for slot in (critical, later):
            for k in range(1, nd):
                to_dp(k, slot).wait_send()
            for b in (1, 2):
                to_head(b, slot).wait_send()
            pass_on(slot).wait_send()
        for s in range(count):
            for r in range(1, nh):
                send_block(r, s).wait_send()
        for w in range(3):
            sibling_own(w).wait_send()
            sibling_far(w).wait_send()
        for s in range(AHEAD):
            keep_go(s).wait()
            for r in range(1, nh):
                send_go(r, s).wait()
        for give in (give_result, give_gat, give_go, give_grads):
            give.wait()


def forward(
    nd, nh, hidden, lengths, adapters_m, adapters_i, weight, bias, wo, wu, wd, gout, shifts,
    gains, up_bias,
):
    count, keys, model = hidden.shape
    width = weight.shape[1]
    heads = width // DH
    tall = 3 * width + 3 * RANK
    part = keys // nh
    tokens = count * part
    rows = adapters_m.shape[2]
    padded, padded_more = (-(-k * rows // 16) * 16 for k in (1, 2))
    shape = jax.ShapeDtypeStruct
    dma = pltpu.SemaphoreType.DMA
    return pl.pallas_call(
        functools.partial(forward_kernel, nd, nh),
        grid=(count,),
        in_specs=[
            pl.BlockSpec(memory_space=pltpu.SMEM),
            vmem(), vmem(),
            pl.BlockSpec((1, keys, model), lambda s: (s, 0, 0)),
            anywhere(), vmem(), vmem(), anywhere(), anywhere(), anywhere(),
            vmem(), vmem(), vmem(), vmem(),
        ],
        out_specs=[
            pl.BlockSpec((1, tall, keys), lambda s: (s, 0, 0)),
            pl.BlockSpec((1, heads, keys, keys), lambda s: (s, 0, 0, 0)),
            pl.BlockSpec((1, heads, keys), lambda s: (s, 0, 0)),
            vmem(), vmem(),
            anywhere(), anywhere(), anywhere(), anywhere(), anywhere(),
        ],
        out_shape=[
            shape((count, tall, keys), BF16),
            shape((count, heads, keys, keys), BF16),
            shape((count, heads, keys), F32),
            shape((tall, model), BF16),
            shape((LANES, width), BF16),
            shape((count, part, model), BF16),
            shape((tokens, model), BF16),
            shape((model, (count - AHEAD) * part), BF16),
            shape((2, model, LANES), F32),
            shape((AHEAD, width, keys), BF16),
        ],
        scratch_shapes=[
            pltpu.VMEM((padded, LANES), BF16),
            pltpu.VMEM((padded_more, LANES), BF16),
            pltpu.VMEM((nh, nd, padded, LANES), BF16),
            pltpu.VMEM((nh, nd, padded_more, LANES), BF16),
            pltpu.VMEM((count, width, keys), BF16),
            pltpu.VMEM((model, 8), F32),
            pltpu.VMEM((model, LANES), F32),
            pltpu.VMEM((model, LANES), F32),
            pltpu.VMEM((LANES, model), BF16),
            pltpu.VMEM((model, tokens), BF16),
            pltpu.VMEM((model, model), BF16),
            pltpu.VMEM((nh, model, model), BF16),
            pltpu.VMEM((nh, model, model), BF16),
            pltpu.VMEM((count, part, model), BF16),
            pltpu.VMEM((tokens, model), BF16),
            pltpu.VMEM((nh, tokens, model), BF16),
            pltpu.VMEM((nh, tokens, model), BF16),
            pltpu.VMEM((tokens, model), F32),
            pltpu.VMEM((tokens, model), F32),
            pltpu.VMEM((tokens, 1), F32),
            pltpu.VMEM((tokens, model), BF16),
            pltpu.VMEM((tokens, model), F32),
            pltpu.VMEM((tokens, model), BF16),
            pltpu.VMEM((tokens, model), F32),
            pltpu.VMEM((tokens, model), BF16),
            pltpu.VMEM((LANES, model), F32),
            pltpu.VMEM((count, part, model), BF16),
            pltpu.VMEM((model, tokens), BF16),
            pltpu.VMEM((2, model, LANES), F32),
            dma((2, nd)), dma((2, nd)), dma((2, 4)), dma((2, 4)),
            dma((nh, count)), dma((nh, count)), dma((count,)),
            dma((5, 5)), dma((5, 5)), dma((2, 3)), dma((2, 3)),
            dma((4,)), dma((4,)),
            dma((nh, AHEAD)), dma((nh, AHEAD)), dma((AHEAD,)),
        ],
        compiler_params=pltpu.CompilerParams(
            collective_id=1, has_side_effects=True, vmem_limit_bytes=VMEM_LIMIT
        ),
        name="forward",
    )(
        lengths, adapters_m, adapters_i, hidden, hidden, weight, bias, wo, wu, wd, gout, shifts,
        gains, up_bias,
    )


def attend_back_kernel(
    nd, nh, x_ref, proj_ref, p_ref, inv_ref, go, got_ready, first_hbm, early, wt, down_t,
    roots_m_hbm, roots_i_hbm, roots_r,
    grad_in, gradients, step_m, step_i, squares,
    roots_m, roots_i, first, load, got_all, gproj, grad_t, late, whole_buf, near, far, last, blocks, mixed, sq, sq_head, sq_dp,
    send_g, recv_g, keep_g, send_n, recv_n, send_f, recv_f,
    send_a, recv_a, send_b, recv_b, *rest,
):
    step = pl.program_id(0)
    d, h = lax.axis_index("dp"), lax.axis_index("head")
    relative = [jnp.bitwise_xor(h, r) for r in range(nh)]
    count, part, model = first.shape
    width = got_all.shape[1]
    own_rows = pl.ds(pl.multiple_of(h * width, width), width)
    one = Reduction(nd, nh, rest[0:4], rest[8:14])
    two = Reduction(nd, nh, rest[4:8], rest[14:20])

    def at(b):
        return (d, jnp.bitwise_xor(h, b))

    def fetch(w):
        source, target = (
            (roots_i_hbm, roots_i), (roots_m_hbm, roots_m), (first_hbm, first)
        )[w]
        return pltpu.make_async_copy(source, target, load.at[w])

    def block_of(r, s):
        return go.at[
            pl.ds(pl.multiple_of(relative[r] * width, width), width),
            pl.ds((s - AHEAD) * part, part),
        ]

    def place_of(r, s):
        return got_all.at[s, :, pl.ds(pl.multiple_of(relative[r] * part, part), part)]

    def bring(r, s):
        return remote(
            block_of(r, s), place_of(0, s), send_g.at[r, s], recv_g.at[r, s], at(r)
        )

    def brought(r, s):
        return remote(
            block_of(r, s), place_of(r, s), send_g.at[r, s], recv_g.at[r, s], at(r)
        )

    def keep(s):
        if s < AHEAD:
            return pltpu.make_async_copy(got_ready.at[s], got_all.at[s], keep_g.at[s])
        return pltpu.make_async_copy(block_of(0, s), place_of(0, s), keep_g.at[s])

    def to_near(i, s):
        return remote(
            whole_buf.at[s, relative[1 + 2 * i]], near.at[s, i], send_n.at[i, s],
            recv_n.at[i, s], at(1),
        )

    def to_far(s):
        return remote(far.at[s], last.at[s], send_f.at[s], recv_f.at[s], at(2))

    def pass_far(s):
        to_near(1, s).wait_recv()
        far[s] = (whole_buf[s, relative[2]].astype(F32) + near[s, 1].astype(F32)).astype(BF16)
        to_far(s).start()

    def complete(s):
        to_near(0, s).wait_recv()
        to_far(s).wait_recv()
        grad_in[s] = (
            first[s].astype(F32)
            + whole_buf[s, h].astype(F32)
            + near[s, 0].astype(F32)
            + last[s].astype(F32)
        ).astype(BF16)

    @pl.when(step == 0)
    def _():
        greet_signal(nd, nh)
        for s in range(count):
            keep(s).start()
        for w in range(3):
            fetch(w).start()
        grad_t[...] = jnp.zeros_like(grad_t)

    for s in range(count):

        @pl.when(step == s)
        def _(s=s):
            keep(s).wait()
            if s >= AHEAD:
                for r in range(1, nh):
                    brought(r, s).wait_recv()

    got = got_all.at[step]
    scale = jnp.asarray(DH ** (-0.5), BF16)
    for head in range(width // DH):
        part_h = slice(head * DH, (head + 1) * DH)
        rows_k = slice(width + head * DH, width + (head + 1) * DH)
        rows_v = slice(2 * width + head * DH, 2 * width + (head + 1) * DH)
        inverse = inv_ref[0, head : head + 1]
        qt = proj_ref[0, part_h] * scale
        kt = proj_ref[0, rows_k] * scale
        vt = proj_ref[0, rows_v]
        gs = (got[part_h].astype(F32) * inverse).astype(BF16)
        et = p_ref[0, head]
        ef = et.astype(F32)
        dpt = tn(vt, gs)
        delta = jnp.sum(ef * dpt, axis=0, keepdims=True) * inverse
        gst = (ef * (dpt - delta)).astype(BF16)
        gproj[part_h] = nn(kt, gst).astype(BF16)
        gproj[rows_k] = nt(qt, gst).astype(BF16)
        gproj[rows_v] = nt(gs, et).astype(BF16)

    @pl.when(step == 0)
    def _():
        greet_wait(nd, nh)
        for s in range(AHEAD, count):
            for r in (2, 3, 1):
                bring(r, s).start()
        two.start(early[...])

    @pl.when(step >= 1)
    def _():
        pass_far(jnp.maximum(step - 1, 0))

    inner = []
    for j in range(3):
        block = gproj[j * width : (j + 1) * width]
        ut = proj_ref[0, 3 * width + j * RANK : 3 * width + (j + 1) * RANK]
        grad_t[(3 + j) * RANK : (4 + j) * RANK, 0:width] += nt(ut, block) * LOWRANK
        inner.append(nn(down_t[(3 + j) * RANK : (4 + j) * RANK], block) * LOWRANK)
    inner = jnp.concatenate(inner, axis=0).astype(BF16)
    grad_t[0 : 3 * RANK] += nn(inner, x_ref[0])

    @pl.when(step == count - 1)
    def _():
        full = grad_t[...].T
        lane = lax.broadcasted_iota(jnp.int32, full.shape, 1)
        late[0] = jnp.where(lane < 3 * RANK, full, 0.0)
        rows = full[0:width]
        lane = lax.broadcasted_iota(jnp.int32, rows.shape, 1)
        late[0, own_rows, :] = jnp.where(lane < 3 * RANK, late[0, own_rows, :], rows)
        one.start(late[...])

    whole_buf[step] = tn(gproj[...], wt[0 : 3 * width]).astype(BF16).reshape(nh, part, model)
    to_near(1, step).start()
    to_near(0, step).start()

    @pl.when(step == 1)
    def _():
        two.over_dp()

    @pl.when(step == 2)
    def _():
        two.over_head()

    def preconditioned(j, u, where, i):
        where[i] = u
        sq[j : j + 1] = jnp.broadcast_to(
            jnp.sum(jnp.sum(u * u, axis=0, keepdims=True), axis=1, keepdims=True), (1, LANES)
        )

    def mix(t):
        mixed[t] = tn(blocks[t], gradients[t].T, HIGH).astype(BF16)

    def steps_model(t):
        for j in range(roots_m.shape[0]):
            tile, m = slot_of(j)
            if tile == t:
                g = mixed[t, m * RANK : (m + 1) * RANK]
                preconditioned(j, nt(g, roots_m[j].astype(BF16)), step_m, j)

    @pl.when(step == count - 1)
    def _():
        blocks[...] = jnp.zeros_like(blocks)
        sq[...] = jnp.zeros_like(sq)
        for j in range(roots_m.shape[0]):
            t, m = slot_of(j)
            blocks[t, m * RANK : (m + 1) * RANK, m * RANK : (m + 1) * RANK] = roots_r[j]
        split = roots_i.shape[2] // model
        for k in range(split):
            for q in range(2):
                m = 2 * k + q
                blocks[2, m * RANK : (m + 1) * RANK, m * RANK : (m + 1) * RANK] = roots_r[
                    roots_m.shape[0] + q
                ]
        one.over_dp()
        pass_far(count - 1)
        two.finish(gradients.at[1:3])
        for w in range(3):
            fetch(w).wait()
        one.over_head()
        mix(1)
        mix(2)
        for q in range(2):
            u = jnp.zeros((RANK, roots_i.shape[1]), F32)
            for k in range(split):
                m = 2 * k + q
                u = u + nt(
                    mixed[2, m * RANK : (m + 1) * RANK],
                    roots_i[q, :, k * model : (k + 1) * model].astype(BF16),
                )
            preconditioned(roots_m.shape[0] + q, u, step_i, q)
        steps_model(1)
        one.finish(gradients.at[0:1])
        mix(0)
        steps_model(0)

        def sq_over_head(k):
            return remote(
                sq, sq_head.at[k], send_a.at[k], recv_a.at[k], (d, lax.rem(h + k, nh))
            )

        def sq_over_dp(k):
            return remote(
                sq_dp.at[0], sq_dp.at[k], send_b.at[k], recv_b.at[k], (lax.rem(d + k, nd), h)
            )

        for k in range(1, nh):
            sq_over_head(k).start()
        total = sq[...]
        for k in range(1, nh):
            sq_over_head(k).wait_recv()
            total = total + sq_head[k]
        sq_dp[0] = total
        for k in range(1, nd):
            sq_over_dp(k).start()
        for s in range(count):
            complete(s)
        for k in range(1, nd):
            sq_over_dp(k).wait_recv()
            total = total + sq_dp[k]
        squares[...] = total
        for k in range(1, nh):
            sq_over_head(k).wait_send()
        for k in range(1, nd):
            sq_over_dp(k).wait_send()
        for s in range(count):
            to_far(s).wait_send()
            for i in range(2):
                to_near(i, s).wait_send()
            if s >= AHEAD:
                for r in range(1, nh):
                    bring(r, s).wait_send()


def attend_back(
    nd, nh, hidden, proj, p, inverse, go, got, first, early, wt, down_t, roots_m, roots_i, roots_r
):
    count, keys, model = hidden.shape
    part, width = first.shape[1], model // nh
    heads = width // DH
    tall = 3 * width + 3 * RANK
    shape = jax.ShapeDtypeStruct
    dma = pltpu.SemaphoreType.DMA
    bufs_one, sems_one = Reduction.scratch(nd, nh, 1, model)
    bufs_two, sems_two = Reduction.scratch(nd, nh, 2, model)
    return pl.pallas_call(
        functools.partial(attend_back_kernel, nd, nh),
        grid=(count,),
        in_specs=[
            pl.BlockSpec((1, keys, model), lambda s: (s, 0, 0)),
            pl.BlockSpec((1, tall, keys), lambda s: (s, 0, 0)),
            pl.BlockSpec((1, heads, keys, keys), lambda s: (s, 0, 0, 0)),
            pl.BlockSpec((1, heads, keys), lambda s: (s, 0, 0)),
            anywhere(), anywhere(), anywhere(), vmem(), vmem(), vmem(), anywhere(), anywhere(),
            vmem(),
        ],
        out_specs=[vmem()] * 5,
        out_shape=[
            shape((count, part, model), BF16),
            shape((3, model, LANES), F32),
            shape((roots_m.shape[0], RANK, roots_m.shape[1]), F32),
            shape((2, RANK, roots_i.shape[1]), F32),
            shape((16, LANES), F32),
        ],
        scratch_shapes=[
            pltpu.VMEM(roots_m.shape, F32),
            pltpu.VMEM(roots_i.shape, F32),
            pltpu.VMEM((count, part, model), BF16),
            dma((3,)),
            pltpu.VMEM((count, width, keys), BF16),
            pltpu.VMEM((3 * width, keys), BF16),
            pltpu.VMEM((LANES, model), F32),
            pltpu.VMEM((1, model, LANES), F32),
            pltpu.VMEM((count, nh, part, model), BF16),
            pltpu.VMEM((count, 2, part, model), BF16),
            pltpu.VMEM((count, part, model), BF16),
            pltpu.VMEM((count, part, model), BF16),
            pltpu.VMEM((3, LANES, LANES), F32),
            pltpu.VMEM((3, LANES, model), BF16),
            pltpu.VMEM((16, LANES), F32),
            pltpu.VMEM((nh, 16, LANES), F32),
            pltpu.VMEM((nd, 16, LANES), F32),
            dma((nh, count)), dma((nh, count)), dma((count,)),
            dma((2, count)), dma((2, count)), dma((count,)), dma((count,)),
            dma((nh,)), dma((nh,)), dma((nd,)), dma((nd,)),
            *bufs_one, *bufs_two, *sems_one, *sems_two,
        ],
        compiler_params=pltpu.CompilerParams(
            collective_id=2, has_side_effects=True, vmem_limit_bytes=VMEM_LIMIT
        ),
        name="attend_back",
    )(hidden, proj, p, inverse, go, got, first, early, wt, down_t, roots_m, roots_i, roots_r)


def finish_kernel(
    nh, owners, grad_in, g_ref, stats_m, stats_i, stats_r, am, ai, step_m, step_i, squares,
    grad_out, grad_m, grad_i, adapt_m, adapt_i, new_m, new_i, new_r, gt,
):
    grad_out[...] = grad_in[...]
    owner = lax.axis_index("dp") * nh + lax.axis_index("head")
    count, rows, model = stats_m.shape
    rows_i = stats_i.shape[1]
    for t in range(3):
        gt[t] = g_ref[t].T.astype(BF16)
    own = [g_ref[t, pl.ds(owner * rows, rows), :] for t in range(2)]
    turned = [v.T for v in own]

    def update(j, old, u, rate):
        size = model if j < count else rows_i * owners
        mean = squares[j : j + 1, 0:1] * (1.0 / (size * RANK))
        return old - rate * lax.rsqrt(mean + 1e-6) * u

    for j in range(count):
        t, m = slot_of(j)
        lanes = slice(m * RANK, (m + 1) * RANK)
        full = gt[t, lanes]
        grad_m[j] = turned[t][lanes]
        new_m[j] = DECAY * stats_m[j] + (1.0 - DECAY) * nn(own[t][:, lanes].astype(BF16), full)
        new_r[j] = DECAY * stats_r[j] + (1.0 - DECAY) * nt(full, full)
        adapt_m[j] = update(j, am[j], step_m[j], RATE_FIRST if j < 5 else RATE_SECOND)
    blocks = stats_i.shape[2] // model
    per = model // rows_i
    block = owner // per
    tall = g_ref[2, pl.ds((owner - block * per) * rows_i, rows_i), :]
    tall_t = tall.T
    for q in range(2):
        mine = jnp.zeros((rows_i, RANK), F32)
        mine_t = jnp.zeros((RANK, rows_i), F32)
        gram = jnp.zeros((RANK, RANK), F32)
        for k in range(blocks):
            lanes = slice((2 * k + q) * RANK, (2 * k + q + 1) * RANK)
            mine = jnp.where(block == k, tall[:, lanes], mine)
            mine_t = jnp.where(block == k, tall_t[lanes], mine_t)
        grad_i[q] = mine_t
        mine = mine.astype(BF16)
        for k in range(blocks):
            lanes = slice((2 * k + q) * RANK, (2 * k + q + 1) * RANK)
            cols = slice(k * model, (k + 1) * model)
            full = gt[2, lanes]
            gram = gram + nt(full, full)
            new_i[q, :, cols] = DECAY * stats_i[q, :, cols] + (1.0 - DECAY) * nn(mine, full)
        new_r[count + q] = DECAY * stats_r[count + q] + (1.0 - DECAY) * gram
        adapt_i[q] = update(count + q, ai[q], step_i[q], RATE_FIRST if q < 1 else RATE_SECOND)


def finish(nd, nh, grad_in, g, stats_m, stats_i, stats_r, am, ai, step_m, step_i, squares):
    shape = jax.ShapeDtypeStruct
    model = stats_m.shape[2]
    return pl.pallas_call(
        functools.partial(finish_kernel, nh, nd * nh),
        in_specs=[vmem()] * 10,
        out_specs=[vmem()] * 8,
        out_shape=[
            shape(grad_in.shape, BF16),
            shape(am.shape, F32),
            shape(ai.shape, F32),
            shape(am.shape, F32),
            shape(ai.shape, F32),
            shape(stats_m.shape, F32),
            shape(stats_i.shape, F32),
            shape(stats_r.shape, F32),
        ],
        scratch_shapes=[pltpu.VMEM((3, LANES, model), BF16)],
        compiler_params=pltpu.CompilerParams(vmem_limit_bytes=VMEM_LIMIT),
        name="finish",
    )(grad_in, g, stats_m, stats_i, stats_r, am, ai, step_m, step_i, squares)


def local(
    nd,
    nh,
    hidden_input,
    grad_out,
    pair_lengths,
    query_key_value_weight,
    qkv_bias,
    output_projection_weight,
    shifts,
    gains,
    up_projection_weight,
    up_bias,
    down_projection_weight,
    adapters_model,
    adapters_inner,
    stats_model,
    stats_inner,
    stats_rank,
    roots_model,
    roots_inner,
    roots_rank,
):
    model = hidden_input.shape[2]
    turned_m = jnp.swapaxes(adapters_model, 1, 2)
    turned_i = jnp.swapaxes(adapters_inner, 1, 2)
    proj, p, inverse, wt, down_t, result, gat, go, early, got = forward(
        nd, nh, hidden_input, pair_lengths, turned_m, turned_i,
        jnp.swapaxes(query_key_value_weight, 1, 2), qkv_bias,
        output_projection_weight, up_projection_weight, down_projection_weight,
        grad_out, shifts, gains, up_bias.reshape(1, -1),
    )
    grad_in, gradients, step_m, step_i, squares = attend_back(
        nd, nh, hidden_input, proj, p, inverse, go, got, gat.reshape(grad_out.shape), early, wt, down_t,
        roots_model, roots_inner, roots_rank,
    )
    grad_in, grad_m, grad_i, adapt_m, adapt_i, new_m, new_i, new_r = finish(
        nd, nh, grad_in, gradients, stats_model, stats_inner, stats_rank, turned_m, turned_i,
        step_m, step_i, squares,
    )
    grad_m, grad_i, adapt_m, adapt_i = (
        jnp.swapaxes(v, 1, 2) for v in (grad_m, grad_i, adapt_m, adapt_i)
    )
    return (result, grad_in, grad_m, grad_i, adapt_m, adapt_i, new_m, new_i, new_r)


def solution(mesh):
    rows = P(None, ("dp", "head"), None)
    in_specs = (
        P("dp", None, None),
        P("dp", "head", None),
        P("dp"),
        P(None, None, "head"),
        P(),
        P("head", None),
        P(),
        P(),
        P(None, "head"),
        P(),
        P("head", None),
        rows, rows, rows, rows,
        P(),
        rows, rows,
        P(),
    )
    out_specs = (
        P("dp", "head", None),
        P("dp", "head", None),
        rows, rows, rows, rows, rows, rows,
        P(),
    )
    body = functools.partial(local, mesh.shape["dp"], mesh.shape["head"])
    return jax.shard_map(body, mesh=mesh, in_specs=in_specs, out_specs=out_specs, check_vma=False)
```
